32 devices in a mesh: row: 4 (over x, core), col: 8 (over z, y).
Axes of the slice: x: 2, y: 2, z: 4, core: 2. Of those that a mesh axis runs over, the one named last changes fastest.
Arguments:
- tokens: bfloat16 [3584, 4096], P('col', 'row'), may hold values from -50 to 50
- ln_gain: float32 [4096], P('row'), may hold values from 0.1 to 1.9
- ln_shift: float32 [4096], P('row'), may hold values from -4 to 4
- w_qkv: bfloat16 [4096, 12288], P('row', 'col'), may hold values from -2 to 2
- w_out: bfloat16 [4096, 4096], P('col', 'row'), may hold values from -0.09375 to 0.09375
- layer_scale: float32 [4096], P('row'), may hold values from 0.5 to 2
- segments: int32 [3584], replicated, may hold values from 0 to 8, as said below
- present: int32 [3584], replicated, may hold values from 0 to 1, as said below
- coords: int32 [2, 3584], replicated, may hold values from 0 to 22, as said below
- owner_slot: int32 [3584], replicated, may hold values from 0 to 3583, as said below
Outputs:
- layer_out: bfloat16 [3584, 4096], P('col', 'row')
The draws below stay inside these ranges and needn't reach their ends.
Inputs may be any that keep to these rules, and one draw needn't show every extreme that they name: `segments`: the picture of each token, pictures numbered in stream order; each picture's tokens form one run, pictures follow each other from position 0, and the padding tokens after them carry 8. `present`: 1 exactly where segments is below 8. A picture has h rows of w patches, 8 <= h <= 18 and 12 <= w <= 22, and some picture has 18 rows of 22; its first 5 tokens (class and registers) have 0 in both rows of coords, then its patches follow in row-major order with patch row and column counted from 1; padding tokens have 0 in both. `owner_slot`: A permutation of the 3584 tokens onto slots. Each block of 896 slots (slot // 896) holds 2 whole pictures, each on consecutive slots in stream order, followed by padding tokens.
All inputs are finite; a program needn't handle non-finite values.
Results may differ from the reference program's by a relative error of at most 0.017.
Values may be sent and summed in bfloat16 or wider, within the bound.
No kernel may reach another device: no remote copies, remote signals or barrier semaphores. Data moves between devices by JAX's collectives and lax.ppermute only.
A program may use at most 64 MiB of HBM per device.

```python
import math
import jax
import jax.numpy as jnp
from jax import lax

D = 4096
HEADS = 32
HD = 128
IMG_ROW = 2
PREFIX = 5
HMIN = 8
HMAX = 18
WMIN = 12
WMAX = 22
TOK_ROW = 896
IMAGES = 8
TOKENS = 3584
N_ROW = 4


def layout(key):
    base_key = jax.random.fold_in(key, 7)
    height_key, width_key, order_key = jax.random.split(base_key, 3)
    heights = jax.random.randint(height_key, (IMAGES,), HMIN, HMAX + 1).astype(jnp.int32).at[0].set(HMAX)
    widths = jax.random.randint(width_key, (IMAGES,), WMIN, WMAX + 1).astype(jnp.int32).at[0].set(WMAX)
    lengths = PREFIX + heights * widths
    placing = jax.random.permutation(order_key, IMAGES).astype(jnp.int32)
    holder = placing // IMG_ROW
    earlier = (holder[None, :] == holder[:, None]) & (placing[None, :] < placing[:, None])
    offset = jnp.sum(jnp.where(earlier, lengths[None, :], 0), axis=1)
    group_ids = jnp.arange(N_ROW, dtype=jnp.int32)
    filled = jnp.sum(jnp.where(holder[None, :] == group_ids[:, None], lengths[None, :], 0), axis=1)
    stream_start = jnp.cumsum(lengths) - lengths
    real_total = jnp.sum(lengths)
    position = jnp.arange(TOKENS, dtype=jnp.int32)
    picture = jnp.sum((position[:, None] >= stream_start[None, :]).astype(jnp.int32), axis=1) - 1
    is_real = position < real_total
    within = position - stream_start[picture]
    real_slot = holder[picture] * TOK_ROW + offset[picture] + within
    leftover = TOK_ROW - filled
    leftover_start = jnp.cumsum(leftover) - leftover
    pad_index = position - real_total
    pad_group = jnp.sum((pad_index[:, None] >= leftover_start[None, :]).astype(jnp.int32), axis=1) - 1
    pad_group = jnp.clip(pad_group, 0, N_ROW - 1)
    pad_slot = pad_group * TOK_ROW + filled[pad_group] + pad_index - leftover_start[pad_group]
    target = jnp.where(is_real, real_slot, pad_slot).astype(jnp.int32)
    patch_index = within - PREFIX
    on_grid = is_real & (patch_index >= 0)
    safe_patch = jnp.maximum(patch_index, 0)
    row_pos = jnp.where(on_grid, safe_patch // widths[picture] + 1, 0).astype(jnp.int32)
    col_pos = jnp.where(on_grid, safe_patch % widths[picture] + 1, 0).astype(jnp.int32)
    segment = jnp.where(is_real, picture, IMAGES).astype(jnp.int32)
    return (segment, is_real.astype(jnp.int32), jnp.stack([row_pos, col_pos]), target)


def draw_segments(key, part):
    return layout(key)[0]


def draw_present(key, part):
    return layout(key)[1]


def draw_coords(key, part):
    return layout(key)[2]


def draw_owner_slot(key, part):
    return layout(key)[3]


def draw_tokens(key, part):
    base_key = jax.random.fold_in(key, 11)
    first_key, second_key, third_key = jax.random.split(base_key, 3)
    row_scale = 10.0 ** (jax.random.uniform(second_key, (TOKENS, 1), dtype=jnp.float32) - 0.5)
    column = jnp.arange(D, dtype=jnp.float32) / D
    col_scale = 10.0 ** (0.5 * column[None, :] + 0.5 * jax.random.uniform(third_key, (1, D), dtype=jnp.float32) - 0.5)
    noise = jnp.clip(jax.random.normal(first_key, (TOKENS, D), dtype=jnp.float32), -5.0, 5.0)
    result = noise * row_scale * col_scale
    return result.astype(jnp.bfloat16)


def draw_w_qkv(key, part):
    base_key = jax.random.fold_in(key, 13)
    first_key = jax.random.fold_in(base_key, 0)
    block = jnp.clip(jax.random.normal(first_key, (D, HEADS, 3, HD), dtype=jnp.float32), -5.0, 5.0)
    return (block.reshape(D, HEADS * 3 * HD) * D ** (-0.5)).astype(jnp.bfloat16)


def level_of(own_key, shape, cuts, least, high):
    factor_of, own = 1.0, jax.random.fold_in(own_key, 6)
    for dim, blocks in cuts:
        draws = jnp.exp(jax.random.uniform(jax.random.fold_in(own, dim), (blocks,), jnp.float32, least / len(cuts), high / len(cuts)))
        factor_of = factor_of * jnp.repeat(draws, shape[dim] // blocks).reshape([-1 if axis == dim else 1 for axis in range(len(shape))])
    return factor_of


def normal_values(stream_key, shape, scale, reach, shards=(), kind=jnp.bfloat16):
    gain = level_of(stream_key, shape, shards, -0.22, 0.18) if shards else 1.0
    entries = jax.random.normal(stream_key, shape, jnp.float32) * scale * gain
    return jnp.minimum(jnp.maximum(entries, -reach), reach).astype(kind)


def setup_inputs(seed: int = 0) -> dict:
    keys = jax.random.split(jax.random.key(seed), 11)
    return {
        "tokens": draw_tokens(jax.random.fold_in(keys[10], 71), 0),
        "ln_gain": jnp.clip(1.0 + 0.18 * jax.random.normal(keys[1], (D,), jnp.float32), 0.1, 1.9),
        "ln_shift": normal_values(keys[2], (D,), 0.3, 4.0, ((0, 4),), jnp.float32),
        "w_qkv": draw_w_qkv(jax.random.fold_in(keys[10], 71), 0),
        "w_out": normal_values(keys[4], (D, D), D ** -0.5, 0.09375, ((0, 8), (1, 4))),
        "layer_scale": jnp.clip(jnp.exp(math.log(2.0) - 1.3862944 * jax.random.uniform(keys[5], (D,), jnp.float32) ** level_of(keys[5], (D,), ((0, 4),), -0.2, 0.2)), 0.5, 2.0),
        "segments": draw_segments(jax.random.fold_in(keys[10], 71), 0),
        "present": draw_present(jax.random.fold_in(keys[10], 71), 0),
        "coords": draw_coords(jax.random.fold_in(keys[10], 71), 0),
        "owner_slot": draw_owner_slot(jax.random.fold_in(keys[10], 71), 0),
    }


def rotate(values, row_pos, col_pos):
    quarter = values.shape[-1] // 4
    frequency = 100.0 ** (-jnp.arange(quarter, dtype=jnp.float32) / quarter)
    angles = jnp.concatenate([row_pos[:, None] * frequency[None, :], col_pos[:, None] * frequency[None, :]], axis=1)
    cosine = jnp.cos(angles)[:, None, :]
    sine_wave = jnp.sin(angles)[:, None, :]
    former = jnp.concatenate([values[..., :quarter], values[..., 2 * quarter:3 * quarter]], axis=-1)
    latter = jnp.concatenate([values[..., quarter:2 * quarter], values[..., 3 * quarter:]], axis=-1)
    new_former = former * cosine - latter * sine_wave
    new_latter = latter * cosine + former * sine_wave
    return jnp.concatenate([new_former[..., :quarter], new_latter[..., :quarter], new_former[..., quarter:], new_latter[..., quarter:]], axis=-1)

def normalize(values, totals, squares, ln_gain, ln_shift):
    average = totals / D
    spread = squares / D - average * average
    scale_inv = lax.rsqrt(spread + 1e-06)
    return ((values - average[:, None]) * scale_inv[:, None] * ln_gain + ln_shift).astype(jnp.bfloat16)

def attend(query_rows, key_rows, values, seg_rows, live_rows):
    scores = jnp.einsum('qhe,khe->hqk', query_rows.astype(jnp.float32), key_rows.astype(jnp.float32)) * HD ** (-0.5)
    allowed = (seg_rows[:, None] == seg_rows[None, :]) & (live_rows[None, :] == 1)
    scores = jnp.where(allowed[None], scores, -1e+30)
    highest = lax.optimization_barrier(jnp.max(scores, axis=-1, keepdims=True))
    weights = jnp.exp(scores - highest)
    probability = (weights / lax.optimization_barrier(jnp.sum(weights, axis=-1, keepdims=True))).astype(jnp.bfloat16)
    result = jnp.einsum('hqk,khe->qhe', probability.astype(jnp.float32), values.astype(jnp.float32))
    return (result * live_rows[:, None, None].astype(jnp.float32)).astype(jnp.bfloat16)

def group_step(pieces):
    return attend(pieces[0], pieces[1], pieces[2], pieces[3], pieces[4])

def reference(tokens, ln_gain, ln_shift, w_qkv, w_out, layer_scale, segments, present, coords, owner_slot):
    own_rows = tokens.astype(jnp.float32)
    normed = normalize(own_rows, lax.optimization_barrier(jnp.sum(own_rows, axis=1)), lax.optimization_barrier(jnp.sum(own_rows * own_rows, axis=1)), ln_gain, ln_shift)
    slot_count = owner_slot.shape[0]
    at_slot = jnp.zeros((slot_count,), jnp.int32).at[owner_slot].set(jnp.arange(slot_count, dtype=jnp.int32))
    placed = normed[at_slot]
    stripe_width = D // N_ROW
    mixed = jnp.zeros((slot_count, w_qkv.shape[1]), jnp.float32)
    for stripe in range(N_ROW):
        start_col = stripe * stripe_width
        product = jnp.dot(placed[:, start_col:start_col + stripe_width], w_qkv[start_col:start_col + stripe_width], preferred_element_type=jnp.float32)
        rounded = lax.optimization_barrier(product.astype(jnp.bfloat16))
        mixed = mixed + rounded.astype(jnp.float32)
    mixed = mixed.reshape(slot_count, HEADS, 3, HD)
    row_pos = coords[0][at_slot].astype(jnp.float32)
    col_pos = coords[1][at_slot].astype(jnp.float32)
    query_rows = rotate(mixed[:, :, 0], row_pos, col_pos).astype(jnp.bfloat16)
    key_rows = rotate(mixed[:, :, 1], row_pos, col_pos).astype(jnp.bfloat16)
    values = mixed[:, :, 2].astype(jnp.bfloat16)
    seg_slot = segments[at_slot]
    live_slot = present[at_slot]
    groups = slot_count // TOK_ROW
    pieces = (query_rows.reshape(groups, TOK_ROW, HEADS, HD), key_rows.reshape(groups, TOK_ROW, HEADS, HD), values.reshape(groups, TOK_ROW, HEADS, HD), seg_slot.reshape(groups, TOK_ROW), live_slot.reshape(groups, TOK_ROW))
    attended = lax.map(group_step, pieces).reshape(slot_count, HEADS * HD)
    projected = jnp.dot(attended[owner_slot], w_out, preferred_element_type=jnp.float32)
    return (own_rows + layer_scale * projected).astype(jnp.bfloat16)
```

```python
import functools

import jax
import jax.numpy as jnp
from jax import lax
from jax.experimental import pallas as pl
from jax.experimental.pallas import tpu as pltpu
from jax.sharding import PartitionSpec as P

D = 4096
HD = 128
BF = jnp.bfloat16
F32 = jnp.float32
LONGEST = 5 + 18 * 22
POSITIONS = 32
MIB = 1024 * 1024


def rotate(values, row_pos, col_pos):
    quarter = values.shape[-1] // 4
    frequency = 100.0 ** (-jnp.arange(quarter, dtype=jnp.float32) / quarter)
    angles = jnp.concatenate(
        [row_pos[:, None] * frequency[None, :], col_pos[:, None] * frequency[None, :]], axis=1
    )
    cosine = jnp.cos(angles)[:, None, :]
    sine_wave = jnp.sin(angles)[:, None, :]
    former = jnp.concatenate(
        [values[..., :quarter], values[..., 2 * quarter : 3 * quarter]], axis=-1
    )
    latter = jnp.concatenate(
        [values[..., quarter : 2 * quarter], values[..., 3 * quarter :]], axis=-1
    )
    new_former = former * cosine - latter * sine_wave
    new_latter = latter * cosine + former * sine_wave
    return jnp.concatenate(
        [
            new_former[..., :quarter],
            new_latter[..., :quarter],
            new_former[..., quarter:],
            new_latter[..., quarter:],
        ],
        axis=-1,
    )


def normalize(values, totals, squares, ln_gain, ln_shift):
    average = totals / D
    spread = squares / D - average * average
    scale_inv = lax.rsqrt(spread + 1e-06)
    return ((values - average[:, None]) * scale_inv[:, None] * ln_gain + ln_shift).astype(
        jnp.bfloat16
    )


def local_general(
    tokens, ln_gain, ln_shift, w_qkv, w_out, layer_scale, segments, present, coords, owner_slot
):
    own_rows = tokens.astype(jnp.float32)
    totals, squares = lax.psum(
        (jnp.sum(own_rows, axis=1), jnp.sum(own_rows * own_rows, axis=1)), "row"
    )
    normed = normalize(own_rows, totals, squares, ln_gain, ln_shift)
    gathered = lax.all_gather(normed, "col", axis=0, tiled=True)
    slot_count = owner_slot.shape[0]
    at_slot = (
        jnp.zeros((slot_count,), jnp.int32)
        .at[owner_slot]
        .set(jnp.arange(slot_count, dtype=jnp.int32))
    )
    placed = gathered[at_slot]
    group_rows = slot_count // lax.axis_size("row")
    mixed = lax.psum_scatter(
        jnp.dot(placed, w_qkv, preferred_element_type=jnp.float32).astype(jnp.bfloat16),
        "row",
        scatter_dimension=0,
        tiled=True,
    ).astype(jnp.float32)
    heads_here = w_qkv.shape[1] // (3 * HD)
    mixed = mixed.reshape(group_rows, heads_here, 3, HD)
    my_slots = lax.dynamic_slice_in_dim(at_slot, lax.axis_index("row") * group_rows, group_rows, 0)
    row_pos = coords[0][my_slots].astype(jnp.float32)
    col_pos = coords[1][my_slots].astype(jnp.float32)
    seg_rows = segments[my_slots]
    live_rows = present[my_slots]
    query_rows = rotate(mixed[:, :, 0], row_pos, col_pos).astype(jnp.bfloat16)
    key_rows = rotate(mixed[:, :, 1], row_pos, col_pos).astype(jnp.bfloat16)
    values = mixed[:, :, 2].astype(jnp.bfloat16)
    scores = jnp.einsum(
        "qhe,khe->hqk", query_rows, key_rows, preferred_element_type=jnp.float32
    ) * HD ** (-0.5)
    allowed = (seg_rows[:, None] == seg_rows[None, :]) & (live_rows[None, :] == 1)
    scores = jnp.where(allowed[None], scores, -1e30)
    highest = jnp.max(scores, axis=-1, keepdims=True)
    weights = jnp.exp(scores - highest)
    probability = (weights / jnp.sum(weights, axis=-1, keepdims=True)).astype(jnp.bfloat16)
    result = jnp.einsum("hqk,khe->qhe", probability, values, preferred_element_type=jnp.float32)
    attended = (result * live_rows[:, None, None].astype(jnp.float32)).astype(jnp.bfloat16)
    attended = attended.reshape(group_rows, heads_here * HD)
    all_slots = lax.all_gather(attended, "row", axis=0, tiled=True)
    projected = lax.psum_scatter(
        jnp.dot(all_slots[owner_slot], w_out, preferred_element_type=jnp.float32).astype(
            jnp.bfloat16
        ),
        "col",
        scatter_dimension=0,
        tiled=True,
    ).astype(jnp.float32)
    return (own_rows + layer_scale * projected).astype(jnp.bfloat16)


def whole(memory_space=pltpu.VMEM):
    return pl.BlockSpec(memory_space=memory_space)


def qkv_kernel(own, peer, stats, affine_own, affine_peer, w_own, w_peer, keep, send, normed):
    columns = jnp.transpose(stats[...])
    average, scale_inv = columns[:, 0:1], columns[:, 1:2]
    width = own.shape[1]
    for part, (rows, affine) in enumerate(((own, affine_own), (peer, affine_peer))):
        for start in range(0, width, 256):
            piece = slice(start, start + 256)
            out = (rows[:, piece].astype(F32) - average) * scale_inv
            out = out * affine[0:1, piece] + affine[1:2, piece]
            normed[:, part * width + start : part * width + start + 256] = out.astype(BF)
    half = keep.shape[1]
    for target, first in ((send, half), (keep, 0)):
        total = jnp.dot(
            normed[:, :width], w_own[:, first : first + half], preferred_element_type=F32
        )
        total += jnp.dot(
            normed[:, width:], w_peer[:, first : first + half], preferred_element_type=F32
        )
        target[...] = total.astype(BF)


def qkv_block(own, peer, stats, affine_own, affine_peer, w_own, w_peer):
    rows, width = own.shape
    half = w_own.shape[1] // 2
    out = jax.ShapeDtypeStruct((rows, half), BF)
    return pl.pallas_call(
        qkv_kernel,
        out_shape=(out, out),
        in_specs=[whole()] * 7,
        out_specs=(whole(), whole()),
        scratch_shapes=[pltpu.VMEM((rows, 2 * width), BF)],
        compiler_params=pltpu.CompilerParams(vmem_limit_bytes=32 * MIB),
        cost_estimate=pl.CostEstimate(
            flops=2 * rows * 2 * width * 2 * half,
            bytes_accessed=4 * rows * width + 8 * width * half + 4 * rows * half,
            transcendentals=0,
        ),
        name="qkv_block",
    )(own, peer, stats, affine_own, affine_peer, w_own, w_peer)


def attend_kernel(tile, window, blocks, places, lows, seg_col, seg_row, table, *refs):
    pairs, (out, query, key, value) = refs[: 2 * blocks], refs[2 * blocks :]
    rows = pairs[0].shape[0]
    lane = lax.broadcasted_iota(jnp.int32, (rows, HD), 1)
    first_half = (lane % 64) < 32

    for m in range(blocks):
        at = pl.ds(pl.multiple_of(places[m] * rows, 16), rows)
        cosine = table[at, :HD]
        sine = table[at, HD:]

        def turned(part):
            cols = slice(part * HD, (part + 1) * HD)
            both = pairs[m][:, cols].astype(F32) + pairs[blocks + m][:, cols].astype(F32)
            if part == 2:
                return both.astype(BF)
            swapped = jnp.where(
                first_half, pltpu.roll(both, HD - 32, 1), pltpu.roll(both, 32, 1)
            )
            return (both * cosine + swapped * sine).astype(BF)

        query[at, :] = turned(0)
        key[at, :] = turned(1)
        value[at, :] = turned(2)

    scale = HD ** (-0.5) * 1.4426950408889634

    def step(i, carry):
        at = pl.ds(pl.multiple_of(i * tile, tile), tile)
        near = pl.ds(pl.multiple_of(lows[i], 128), window)
        scores = (
            lax.dot_general(
                query[at, :],
                key[near, :],
                (((1,), (1,)), ((), ())),
                preferred_element_type=F32,
            )
            * scale
        )
        marks = seg_col[at, :]
        scores = jnp.where(marks == seg_row[0:1, near], scores, -1e30)
        highest = jnp.max(scores, axis=1, keepdims=True)
        weights = jnp.exp2(scores - highest)
        total = jnp.sum(weights, axis=1, keepdims=True)
        result = jnp.dot(weights.astype(BF), value[near, :], preferred_element_type=F32)
        live = jnp.where(marks >= 0, 1.0 / total, 0.0)
        out[at, :] = (result * live).astype(BF)
        return carry

    lax.fori_loop(0, out.shape[0] // tile, step, 0)


def attend(places, lows, seg_col, seg_row, table, kept, received, tile, window):
    blocks = len(kept)
    count = seg_col.shape[0]
    smem = whole(pltpu.SMEM)
    return pl.pallas_call(
        functools.partial(attend_kernel, tile, window, blocks),
        out_shape=jax.ShapeDtypeStruct((count, HD), BF),
        in_specs=[smem, smem] + [whole()] * (3 + 2 * blocks),
        out_specs=whole(),
        scratch_shapes=[pltpu.VMEM((count, HD), BF)] * 3,
        compiler_params=pltpu.CompilerParams(vmem_limit_bytes=48 * MIB),
        cost_estimate=pl.CostEstimate(
            flops=4 * count * window * HD,
            bytes_accessed=count * HD * 26,
            transcendentals=count * window,
        ),
        name="attend",
    )(places, lows, seg_col, seg_row, table, *kept, *received)


def project_kernel(blocks, where, tokens, layer_scale, *refs):
    weights = refs[:blocks]
    parts = refs[blocks : 5 * blocks]
    out, total = refs[5 * blocks :]
    even = where[0] == 0
    for m in range(blocks):
        for pair in range(2):
            one = parts[(2 * pair) * blocks + m][...]
            two = parts[(2 * pair + 1) * blocks + m][...]
            rows = jnp.concatenate(
                [jnp.where(even, one, two), jnp.where(even, two, one)], axis=1
            )
            start = pl.multiple_of(where[1 + pair], 2 * HD)
            term = jnp.dot(
                rows, weights[m][pl.ds(start, 2 * HD), :], preferred_element_type=F32
            )
            if m == 0 and pair == 0:
                total[...] = term
            else:
                total[...] += term
    out[...] = (tokens[...].astype(F32) + layer_scale[...] * total[...]).astype(BF)


def project(where, tokens, layer_scale, weights, parts):
    blocks = len(weights)
    return pl.pallas_call(
        functools.partial(project_kernel, blocks),
        out_shape=jax.ShapeDtypeStruct(tokens.shape, BF),
        in_specs=[whole(pltpu.SMEM)] + [whole()] * (2 + 5 * blocks),
        out_specs=whole(),
        scratch_shapes=[pltpu.VMEM(tokens.shape, F32)],
        compiler_params=pltpu.CompilerParams(vmem_limit_bytes=48 * MIB),
        name="project",
    )(where, tokens, layer_scale, *weights, *parts)


def local_heads(
    tokens, ln_gain, ln_shift, w_qkv, w_out, layer_scale, segments, present, coords, owner_slot
):
    rows = lax.axis_size("row")
    cols = lax.axis_size("col")
    count = segments.shape[0]
    block = tokens.shape[0]
    row = lax.axis_index("row")
    col = lax.axis_index("col")
    core, x_index = row % 2, row // 2
    head = 2 * core + x_index

    lines = cols // 2
    ring = list(range(0, lines, 2)) + list(range(lines - 1 - lines % 2, 0, -2))
    after = {z: ring[(i + 1) % lines] for i, z in enumerate(ring)}
    y_swap = [(c, c ^ 1) for c in range(cols)]
    z_next = [(2 * z + y, 2 * after[z] + y) for z in range(lines) for y in range(2)]
    core_swap = [(r, r ^ 1) for r in range(rows)]
    x_swap = [(r, r ^ 2) for r in range(rows)]

    def by_y(value):
        return lax.ppermute(value, "col", y_swap)

    def by_z(value):
        return lax.ppermute(value, "col", z_next)

    def by_core(value):
        return lax.ppermute(value, "row", core_swap)

    def by_x(value):
        return lax.ppermute(value, "row", x_swap)

    def hold(*values):
        return lax.optimization_barrier(values)

    source = {}
    for c in range(cols):
        z, y = c // 2, c % 2
        back = {b: a for a, b in after.items()}
        for i in range(lines):
            source[c, i] = 2 * z + y
            source[c, lines + i] = 2 * z + 1 - y
            z = back[z]
    places = jnp.asarray([[source[c, m] for m in range(cols)] for c in range(cols)], jnp.int32)[col]
    targets = [{source[c, m]: c for c in range(cols)} for m in range(cols)]
    send_to = jnp.asarray([[targets[m][c] for m in range(cols)] for c in range(cols)], jnp.int32)[
        col
    ]

    own_rows = tokens.astype(F32)
    sums = lax.psum(
        jnp.stack([jnp.sum(own_rows, axis=1), jnp.sum(own_rows * own_rows, axis=1)]), "row"
    )
    average = sums[0] / D
    spread = sums[1] / D - average * average
    own_stats = jnp.concatenate(
        [average[None], lax.rsqrt(spread + 1e-06)[None], jnp.zeros((6, block), F32)]
    )

    width = 3 * HD

    def head_columns(which):
        return lax.dynamic_slice_in_dim(w_qkv, which * width, width, 1)

    w_own = jnp.concatenate([head_columns(head), head_columns(head ^ 1)], axis=1)
    w_peer = by_core(jnp.concatenate([head_columns(head ^ 2), head_columns(head ^ 3)], axis=1))
    affine_own = jnp.stack([ln_gain, ln_shift])
    affine_peer = by_core(affine_own)

    def qkv(own, peer, stats):
        return qkv_block(own, peer, stats, affine_own, affine_peer, w_own, w_peer)

    z_tok, z_stat = [tokens], [own_stats]
    y_tok, y_stat = [], []
    for i in range(lines):
        y_new, y_s = by_y(z_tok[i]), by_y(z_stat[i])
        if i < lines - 1:
            z_new, z_s = by_z(z_tok[i]), by_z(z_stat[i])
            z_new, y_new, z_s, y_s = hold(z_new, y_new, z_s, y_s)
            z_tok.append(z_new)
            z_stat.append(z_s)
        y_tok.append(y_new)
        y_stat.append(y_s)
    blocks_tok, blocks_stat = z_tok + y_tok, z_stat + y_stat
    kept, received = [], []
    for own, stats in zip(blocks_tok, blocks_stat):
        keep, send = qkv(own, by_core(own), stats)
        kept.append(keep)
        received.append(by_x(send))

    w_first, _ = hold(w_out, z_tok[-1])
    z_w, y_w = [w_first], []
    for i in range(lines):
        y_new = by_y(z_w[i])
        if i < lines - 1:
            z_new = by_z(z_w[i])
            z_new, y_new = hold(z_new, y_new)
            z_w.append(z_new)
        y_w.append(y_new)
    weights = z_w + y_w

    quarter = HD // 4
    frequency = 100.0 ** (-jnp.arange(quarter, dtype=F32) / quarter)
    angles = jnp.arange(POSITIONS, dtype=F32)[:, None] * frequency[None, :]
    cosine, sine = jnp.cos(angles), jnp.sin(angles)
    none = jnp.zeros((POSITIONS, 2 * quarter), F32)
    cos_pair = jnp.concatenate([cosine, cosine], axis=1)
    sin_pair = jnp.concatenate([-sine, sine], axis=1)
    turns = jnp.concatenate(
        [
            jnp.concatenate([cos_pair, none, sin_pair, none], axis=1),
            jnp.concatenate([none, cos_pair, none, sin_pair], axis=1),
        ],
        axis=0,
    )
    spots = jnp.arange(POSITIONS, dtype=jnp.int32)
    chosen = jnp.concatenate(
        [coords[0][:, None] == spots[None, :], coords[1][:, None] == spots[None, :]], axis=1
    )
    table = jnp.dot(
        chosen.astype(F32),
        turns,
        precision=lax.Precision.HIGHEST,
        preferred_element_type=F32,
    )

    tile = 256
    reach = -(-(LONGEST - 1) // 128) * 128
    window = min(count, tile + 2 * reach)
    tiles = count // tile
    marks = jnp.where(present == 1, segments, -1)
    lows = jnp.clip(jnp.arange(tiles, dtype=jnp.int32) * tile - reach, 0, count - window)
    attended = attend(
        places,
        lows,
        marks[:, None],
        marks[None, :],
        table,
        kept,
        received,
        tile,
        window,
    )

    parts = []
    for m in range(cols):
        piece = lax.dynamic_slice_in_dim(attended, send_to[m] * block, block, 0)
        pairs = [(c, targets[m][c]) for c in range(cols)]
        parts.append(piece if m == 0 else lax.ppermute(piece, "col", pairs))
    x_parts = [by_x(piece) for piece in parts]
    c_parts = [by_core(piece) for piece in parts]
    d_parts = [by_core(piece) for piece in x_parts]
    where = jnp.stack([x_index, core * 2 * HD, (1 - core) * 2 * HD]).astype(jnp.int32)
    return project(
        where,
        tokens,
        layer_scale[None, :],
        weights,
        parts + x_parts + c_parts + d_parts,
    )


def solution(mesh):
    in_specs = (
        P("col", "row"),
        P("row"),
        P("row"),
        P("row", "col"),
        P("col", "row"),
        P("row"),
        P(),
        P(),
        P(),
        P(),
    )
    out_specs = P("col", "row")
    rows, cols = mesh.shape["row"], mesh.shape["col"]

    def local(*args):
        heads_here = args[3].shape[1] // (3 * HD)
        if rows == 4 and heads_here == 4 and cols % 2 == 0 and args[6].shape[0] % 256 == 0:
            return local_heads(*args)
        return local_general(*args)

    return jax.shard_map(local, mesh=mesh, in_specs=in_specs, out_specs=out_specs, check_vma=False)
```

```python
import functools

import jax
import jax.numpy as jnp
from jax import lax
from jax.experimental import pallas as pl
from jax.experimental.pallas import tpu as pltpu
from jax.sharding import PartitionSpec as P

D = 4096
HD = 128
BF = jnp.bfloat16
F32 = jnp.float32
LONGEST = 5 + 18 * 22
POSITIONS = 32
MIB = 1024 * 1024


def rotate(values, row_pos, col_pos):
    quarter = values.shape[-1] // 4
    frequency = 100.0 ** (-jnp.arange(quarter, dtype=jnp.float32) / quarter)
    angles = jnp.concatenate(
        [row_pos[:, None] * frequency[None, :], col_pos[:, None] * frequency[None, :]], axis=1
    )
    cosine = jnp.cos(angles)[:, None, :]
    sine_wave = jnp.sin(angles)[:, None, :]
    former = jnp.concatenate(
        [values[..., :quarter], values[..., 2 * quarter : 3 * quarter]], axis=-1
    )
    latter = jnp.concatenate(
        [values[..., quarter : 2 * quarter], values[..., 3 * quarter :]], axis=-1
    )
    new_former = former * cosine - latter * sine_wave
    new_latter = latter * cosine + former * sine_wave
    return jnp.concatenate(
        [
            new_former[..., :quarter],
            new_latter[..., :quarter],
            new_former[..., quarter:],
            new_latter[..., quarter:],
        ],
        axis=-1,
    )


def normalize(values, totals, squares, ln_gain, ln_shift):
    average = totals / D
    spread = squares / D - average * average
    scale_inv = lax.rsqrt(spread + 1e-06)
    return ((values - average[:, None]) * scale_inv[:, None] * ln_gain + ln_shift).astype(
        jnp.bfloat16
    )


def local_general(
    tokens, ln_gain, ln_shift, w_qkv, w_out, layer_scale, segments, present, coords, owner_slot
):
    own_rows = tokens.astype(jnp.float32)
    totals, squares = lax.psum(
        (jnp.sum(own_rows, axis=1), jnp.sum(own_rows * own_rows, axis=1)), "row"
    )
    normed = normalize(own_rows, totals, squares, ln_gain, ln_shift)
    gathered = lax.all_gather(normed, "col", axis=0, tiled=True)
    slot_count = owner_slot.shape[0]
    at_slot = (
        jnp.zeros((slot_count,), jnp.int32)
        .at[owner_slot]
        .set(jnp.arange(slot_count, dtype=jnp.int32))
    )
    placed = gathered[at_slot]
    group_rows = slot_count // lax.axis_size("row")
    mixed = lax.psum_scatter(
        jnp.dot(placed, w_qkv, preferred_element_type=jnp.float32).astype(jnp.bfloat16),
        "row",
        scatter_dimension=0,
        tiled=True,
    ).astype(jnp.float32)
    heads_here = w_qkv.shape[1] // (3 * HD)
    mixed = mixed.reshape(group_rows, heads_here, 3, HD)
    my_slots = lax.dynamic_slice_in_dim(at_slot, lax.axis_index("row") * group_rows, group_rows, 0)
    row_pos = coords[0][my_slots].astype(jnp.float32)
    col_pos = coords[1][my_slots].astype(jnp.float32)
    seg_rows = segments[my_slots]
    live_rows = present[my_slots]
    query_rows = rotate(mixed[:, :, 0], row_pos, col_pos).astype(jnp.bfloat16)
    key_rows = rotate(mixed[:, :, 1], row_pos, col_pos).astype(jnp.bfloat16)
    values = mixed[:, :, 2].astype(jnp.bfloat16)
    scores = jnp.einsum(
        "qhe,khe->hqk", query_rows, key_rows, preferred_element_type=jnp.float32
    ) * HD ** (-0.5)
    allowed = (seg_rows[:, None] == seg_rows[None, :]) & (live_rows[None, :] == 1)
    scores = jnp.where(allowed[None], scores, -1e30)
    highest = jnp.max(scores, axis=-1, keepdims=True)
    weights = jnp.exp(scores - highest)
    probability = (weights / jnp.sum(weights, axis=-1, keepdims=True)).astype(jnp.bfloat16)
    result = jnp.einsum("hqk,khe->qhe", probability, values, preferred_element_type=jnp.float32)
    attended = (result * live_rows[:, None, None].astype(jnp.float32)).astype(jnp.bfloat16)
    attended = attended.reshape(group_rows, heads_here * HD)
    all_slots = lax.all_gather(attended, "row", axis=0, tiled=True)
    projected = lax.psum_scatter(
        jnp.dot(all_slots[owner_slot], w_out, preferred_element_type=jnp.float32).astype(
            jnp.bfloat16
        ),
        "col",
        scatter_dimension=0,
        tiled=True,
    ).astype(jnp.float32)
    return (own_rows + layer_scale * projected).astype(jnp.bfloat16)


def whole(memory_space=pltpu.VMEM):
    return pl.BlockSpec(memory_space=memory_space)


def qkv_kernel(own, peer, stats, affine_own, affine_peer, w_own, w_peer, keep, send, normed):
    columns = jnp.transpose(stats[...])
    average, scale_inv = columns[:, 0:1], columns[:, 1:2]
    width = own.shape[1]
    for part, (rows, affine) in enumerate(((own, affine_own), (peer, affine_peer))):
        for start in range(0, width, 256):
            piece = slice(start, start + 256)
            out = (rows[:, piece].astype(F32) - average) * scale_inv
            out = out * affine[0:1, piece] + affine[1:2, piece]
            normed[:, part * width + start : part * width + start + 256] = out.astype(BF)
    half = keep.shape[1]
    for target, first in ((send, half), (keep, 0)):
        total = jnp.dot(
            normed[:, :width], w_own[:, first : first + half], preferred_element_type=F32
        )
        total += jnp.dot(
            normed[:, width:], w_peer[:, first : first + half], preferred_element_type=F32
        )
        target[...] = total.astype(BF)


def qkv_block(own, peer, stats, affine_own, affine_peer, w_own, w_peer):
    rows, width = own.shape
    half = w_own.shape[1] // 2
    out = jax.ShapeDtypeStruct((rows, half), BF)
    return pl.pallas_call(
        qkv_kernel,
        out_shape=(out, out),
        in_specs=[whole()] * 7,
        out_specs=(whole(), whole()),
        scratch_shapes=[pltpu.VMEM((rows, 2 * width), BF)],
        compiler_params=pltpu.CompilerParams(vmem_limit_bytes=32 * MIB),
        cost_estimate=pl.CostEstimate(
            flops=2 * rows * 2 * width * 2 * half,
            bytes_accessed=4 * rows * width + 8 * width * half + 4 * rows * half,
            transcendentals=0,
        ),
        name="qkv_block",
    )(own, peer, stats, affine_own, affine_peer, w_own, w_peer)


def turn_kernel(place, kept, received, table, out, angles, sem):
    rows = kept.shape[0]
    at = pl.ds(pl.multiple_of(place[0] * rows, 16), rows)
    load = pltpu.make_async_copy(table.at[at, :], angles, sem)
    load.start()
    lane = lax.broadcasted_iota(jnp.int32, (rows, HD), 1)
    first_half = (lane % 64) < 32
    out[:, 2 * HD :] = (
        kept[:, 2 * HD :].astype(F32) + received[:, 2 * HD :].astype(F32)
    ).astype(BF)
    load.wait()
    for part in range(2):
        cols = slice(part * HD, (part + 1) * HD)
        both = kept[:, cols].astype(F32) + received[:, cols].astype(F32)
        swapped = jnp.where(first_half, pltpu.roll(both, HD - 32, 1), pltpu.roll(both, 32, 1))
        out[:, cols] = (both * angles[:, :HD] + swapped * angles[:, HD:]).astype(BF)


def turn(place, kept, received, table):
    rows = kept.shape[0]
    return pl.pallas_call(
        turn_kernel,
        out_shape=jax.ShapeDtypeStruct(kept.shape, BF),
        in_specs=[whole(pltpu.SMEM), whole(), whole(), whole(pl.ANY)],
        out_specs=whole(),
        scratch_shapes=[pltpu.VMEM((rows, 2 * HD), F32), pltpu.SemaphoreType.DMA],
        compiler_params=pltpu.CompilerParams(vmem_limit_bytes=16 * MIB),
        cost_estimate=pl.CostEstimate(
            flops=8 * rows * HD, bytes_accessed=26 * rows * HD, transcendentals=0
        ),
        name="turn",
    )(place, kept, received, table)


def attend_kernel(tile, windows, blocks, places, lows, sizes, seg_col, seg_row, *refs):
    pieces, (out, turned, sems) = refs[:blocks], refs[blocks:]
    rows = pieces[0].shape[0]

    def load(m):
        at = pl.ds(pl.multiple_of(places[m] * rows, 16), rows)
        return pltpu.make_async_copy(pieces[m], turned.at[at, :], sems.at[m])

    for m in range(blocks):
        load(m).start()
    for m in range(blocks):
        load(m).wait()
    scale = HD ** (-0.5) * 1.4426950408889634

    def step(i, carry):
        at = pl.ds(pl.multiple_of(i * tile, tile), tile)

        def look(window):
            near = pl.ds(pl.multiple_of(lows[i], 128), window)
            scores = (
                lax.dot_general(
                    turned[at, :HD],
                    turned[near, HD : 2 * HD],
                    (((1,), (1,)), ((), ())),
                    preferred_element_type=F32,
                )
                * scale
            )
            marks = seg_col[at, :]
            scores = jnp.where(marks == seg_row[0:1, near], scores, -1e30)
            highest = jnp.max(scores, axis=1, keepdims=True)
            weights = jnp.exp2(scores - highest)
            total = jnp.sum(weights, axis=1, keepdims=True)
            result = jnp.dot(
                weights.astype(BF), turned[near, 2 * HD :], preferred_element_type=F32
            )
            live = jnp.where(marks >= 0, 1.0 / total, 0.0)
            out[at, :] = (result * live).astype(BF)

        for kind, window in enumerate(windows):
            pl.when(sizes[i] == kind)(functools.partial(look, window))
        return carry

    lax.fori_loop(0, out.shape[0] // tile, step, 0)


def attend(places, lows, sizes, seg_col, seg_row, pieces, tile, windows):
    blocks = len(pieces)
    count = seg_col.shape[0]
    smem = whole(pltpu.SMEM)
    return pl.pallas_call(
        functools.partial(attend_kernel, tile, windows, blocks),
        out_shape=jax.ShapeDtypeStruct((count, HD), BF),
        in_specs=[smem, smem, smem, whole(), whole()] + [whole(pl.ANY)] * blocks,
        out_specs=whole(),
        scratch_shapes=[
            pltpu.VMEM((count, 3 * HD), BF),
            pltpu.SemaphoreType.DMA((blocks,)),
        ],
        compiler_params=pltpu.CompilerParams(vmem_limit_bytes=32 * MIB),
        cost_estimate=pl.CostEstimate(
            flops=4 * count * windows[-1] * HD,
            bytes_accessed=count * HD * 26,
            transcendentals=count * windows[-1],
        ),
        name="attend",
    )(places, lows, sizes, seg_col, seg_row, *pieces)


def project_kernel(blocks, groups, slots, tokens, layer_scale, *refs):
    weights, parts = refs[:blocks], refs[blocks : blocks + 4 * groups]
    out, all_weights, rows, weight_sems, sems = refs[blocks + 4 * groups :]
    depth = weights[0].shape[0]
    each = blocks // groups

    def load(m):
        return pltpu.make_async_copy(
            weights[m], all_weights.at[m * depth : (m + 1) * depth, :], weight_sems.at[m]
        )

    def place(m, j):
        start = pl.multiple_of(m * depth + slots[j] * HD, HD)
        first = (m % each) * HD
        return pltpu.make_async_copy(
            parts[4 * (m // each) + j].at[:, first : first + HD],
            rows.at[:, pl.ds(start, HD)],
            sems.at[4 * m + j],
        )

    for m in range(blocks):
        load(m).start()
        for j in range(4):
            place(m, j).start()
    for m in range(blocks):
        load(m).wait()
        for j in range(4):
            place(m, j).wait()
    for start in range(0, out.shape[1], 256):
        cols = slice(start, start + 256)
        total = jnp.dot(rows[...], all_weights[:, cols], preferred_element_type=F32)
        out[:, cols] = (tokens[:, cols].astype(F32) + layer_scale[:, cols] * total).astype(BF)


def project(slots, tokens, layer_scale, weights, parts):
    blocks, groups = len(weights), len(parts) // 4
    depth = weights[0].shape[0]
    count, width = tokens.shape
    return pl.pallas_call(
        functools.partial(project_kernel, blocks, groups),
        out_shape=jax.ShapeDtypeStruct(tokens.shape, BF),
        in_specs=[whole(pltpu.SMEM), whole(), whole()]
        + [whole(pl.ANY)] * (blocks + 4 * groups),
        out_specs=whole(),
        scratch_shapes=[
            pltpu.VMEM((blocks * depth, width), BF),
            pltpu.VMEM((count, blocks * depth), BF),
            pltpu.SemaphoreType.DMA((blocks,)),
            pltpu.SemaphoreType.DMA((4 * blocks,)),
        ],
        compiler_params=pltpu.CompilerParams(vmem_limit_bytes=32 * MIB),
        cost_estimate=pl.CostEstimate(
            flops=2 * count * blocks * depth * width,
            bytes_accessed=2 * (blocks * depth * (width + count) + 2 * count * width),
            transcendentals=0,
        ),
        name="project",
    )(slots, tokens, layer_scale, *weights, *parts)


def local_heads(
    tokens, ln_gain, ln_shift, w_qkv, w_out, layer_scale, segments, present, coords, owner_slot
):
    rows = lax.axis_size("row")
    cols = lax.axis_size("col")
    count = segments.shape[0]
    block = tokens.shape[0]
    row = lax.axis_index("row")
    col = lax.axis_index("col")
    core, x_index = row % 2, row // 2
    head = 2 * core + x_index

    lines = cols // 2
    ring = list(range(0, lines, 2)) + list(range(lines - 1 - lines % 2, 0, -2))
    after = {z: ring[(i + 1) % lines] for i, z in enumerate(ring)}
    y_swap = [(c, c ^ 1) for c in range(cols)]
    z_next = [(2 * z + y, 2 * after[z] + y) for z in range(lines) for y in range(2)]
    core_swap = [(r, r ^ 1) for r in range(rows)]
    x_swap = [(r, r ^ 2) for r in range(rows)]

    def by_y(value):
        return lax.ppermute(value, "col", y_swap)

    def by_z(value):
        return lax.ppermute(value, "col", z_next)

    def by_core(value):
        return lax.ppermute(value, "row", core_swap)

    def by_x(value):
        return lax.ppermute(value, "row", x_swap)

    def hold(*values):
        return lax.optimization_barrier(values)

    source = {}
    back = {b: a for a, b in after.items()}
    for c in range(cols):
        z, y = c // 2, c % 2
        for i in range(lines):
            source[c, i] = 2 * z + y
            source[c, lines + i] = 2 * z + 1 - y
            z = back[z]
    places = jnp.asarray([[source[c, m] for m in range(cols)] for c in range(cols)], jnp.int32)[col]
    targets = [{source[c, m]: c for c in range(cols)} for m in range(cols)]
    send_to = jnp.asarray([[targets[m][c] for m in range(cols)] for c in range(cols)], jnp.int32)[
        col
    ]

    z_tok, y_tok = [tokens], []
    z_new, y_new = by_z(tokens), by_y(tokens)

    own_rows = tokens.astype(F32)
    sums = lax.psum(
        jnp.stack([jnp.sum(own_rows, axis=1), jnp.sum(own_rows * own_rows, axis=1)]), "row"
    )
    average = sums[0] / D
    spread = sums[1] / D - average * average
    own_stats = jnp.concatenate(
        [average[None], lax.rsqrt(spread + 1e-06)[None], jnp.zeros((6, block), F32)]
    )
    stats = jnp.stack([own_stats, by_y(own_stats)])
    next_stats = by_z(stats)

    width = 3 * HD

    def head_columns(which):
        return lax.dynamic_slice_in_dim(w_qkv, which * width, width, 1)

    w_peer = by_core(jnp.concatenate([head_columns(head ^ 2), head_columns(head ^ 3)], axis=1))
    w_own = jnp.concatenate([head_columns(head), head_columns(head ^ 1)], axis=1)
    affine_own = jnp.stack([ln_gain, ln_shift])
    affine_peer = by_core(affine_own)

    def qkv(own, peer, its_stats):
        return qkv_block(own, peer, its_stats, affine_own, affine_peer, w_own, w_peer)

    quarter = HD // 4
    frequency = 100.0 ** (-jnp.arange(quarter, dtype=F32) / quarter)
    angles = jnp.arange(POSITIONS, dtype=F32)[:, None] * frequency[None, :]
    cosine, sine = jnp.cos(angles), jnp.sin(angles)
    none = jnp.zeros((POSITIONS, 2 * quarter), F32)
    cos_pair = jnp.concatenate([cosine, cosine], axis=1)
    sin_pair = jnp.concatenate([-sine, sine], axis=1)
    turns = jnp.concatenate(
        [
            jnp.concatenate([cos_pair, none, sin_pair, none], axis=1),
            jnp.concatenate([none, cos_pair, none, sin_pair], axis=1),
        ],
        axis=0,
    )
    spots = jnp.arange(POSITIONS, dtype=jnp.int32)
    chosen = jnp.concatenate(
        [coords[0][:, None] == spots[None, :], coords[1][:, None] == spots[None, :]], axis=1
    )
    table = jnp.dot(
        chosen.astype(F32),
        turns,
        precision=lax.Precision.HIGHEST,
        preferred_element_type=F32,
    )

    tile = 256
    reach = -(-(LONGEST - 1) // 128) * 128
    windows = tuple(sorted({min(count, w) for w in (512, 640, 896, tile + 2 * reach)}))
    tiles = count // tile
    marks = jnp.where(present == 1, segments, -1)
    heads_of = segments.reshape(tiles, tile)
    real = jnp.sum(present)
    begin = jnp.sum((segments[None, :] < heads_of[:, :1]).astype(jnp.int32), axis=1)
    end = jnp.sum((segments[None, :] <= heads_of[:, -1:]).astype(jnp.int32), axis=1)
    begin = jnp.minimum(begin, real) // 128 * 128
    need = jnp.minimum(end, real) - begin
    sizes = sum((need > w).astype(jnp.int32) for w in windows[:-1])
    spans = sum(jnp.where(sizes == k, w, 0) for k, w in enumerate(windows))
    lows = jnp.minimum(begin, count - spans).astype(jnp.int32)
    seg_col, seg_row = marks[:, None], marks[None, :]

    own_pair = qkv(tokens, by_core(tokens), stats[0])
    z_new, y_new, next_stats, table, seg_col, seg_row, lows, sizes, own_keep, own_send = hold(
        z_new, y_new, next_stats, table, seg_col, seg_row, lows, sizes, *own_pair
    )
    kept, sent, received = {0: own_keep}, {0: own_send}, {}
    ring_stats = [stats]
    w_ring = [w_out]
    for i in range(1, lines + 1):
        y_tok.append(y_new)
        fresh = [lines + i - 1]
        if i < lines:
            z_tok.append(z_new)
            ring_stats.append(next_stats)
            fresh.append(i)
        moving = []
        if i < lines:
            y_new = by_y(z_tok[i])
            moving.append(y_new)
        if i < lines - 1:
            z_new, next_stats = by_z(z_tok[i]), by_z(ring_stats[i])
            moving += [z_new, next_stats]
        else:
            w_ring.append(by_z(w_ring[-1]))
            if i == lines - 1:
                moving.append(w_ring[-1])
        for m in list(sent):
            received[m] = by_x(sent.pop(m))
        for m in fresh:
            mine = z_tok[m] if m < lines else y_tok[m - lines]
            kept[m], sent[m] = qkv(mine, by_core(mine), ring_stats[m % lines][m // lines])
        if i == lines:
            break
        work = [kept[m] for m in fresh] + [sent[m] for m in fresh] + list(received.values())
        moving = list(hold(*moving, *work))
        y_new = moving.pop(0)
        if i < lines - 1:
            z_new, next_stats = moving.pop(0), moving.pop(0)
        else:
            w_ring[-1] = moving.pop(0)
        for m in fresh:
            kept[m] = moving.pop(0)
        for m in fresh:
            sent[m] = moving.pop(0)
        for m in received:
            received[m] = moving.pop(0)
    for m in list(sent):
        received[m] = by_x(sent.pop(m))
    pieces = [turn(places[m : m + 1], kept[m], received[m], table) for m in range(cols)]

    while len(w_ring) < lines:
        w_ring.append(by_z(w_ring[-1]))
    weights = w_ring + [by_y(w) for w in w_ring]

    attended = attend(places, lows, sizes, seg_col, seg_row, pieces, tile, windows)

    arrived = []
    for m in range(cols):
        piece = lax.dynamic_slice_in_dim(attended, send_to[m] * block, block, 0)
        pairs = [(c, targets[m][c]) for c in range(cols)]
        arrived.append(piece if m == 0 else lax.ppermute(piece, "col", pairs))
    half = lines // 2
    order = [i + lines * y for part in range(2) for y in range(2) for i in range(part * half, (part + 1) * half)]
    parts = []
    for part in range(2):
        group = jnp.concatenate([arrived[m] for m in order[part * lines : (part + 1) * lines]], axis=1)
        other = by_x(group)
        parts += [group, other, by_core(group), by_core(other)]
    slots = jnp.stack([head, head ^ 1, head ^ 2, head ^ 3]).astype(jnp.int32)
    return project(slots, tokens, layer_scale[None, :], [weights[m] for m in order], parts)


def solution(mesh):
    in_specs = (
        P("col", "row"),
        P("row"),
        P("row"),
        P("row", "col"),
        P("col", "row"),
        P("row"),
        P(),
        P(),
        P(),
        P(),
    )
    out_specs = P("col", "row")
    rows, cols = mesh.shape["row"], mesh.shape["col"]

    def local(*args):
        heads_here = args[3].shape[1] // (3 * HD)
        if rows == 4 and heads_here == 4 and cols % 4 == 0 and args[6].shape[0] % 256 == 0:
            return local_heads(*args)
        return local_general(*args)

    return jax.shard_map(local, mesh=mesh, in_specs=in_specs, out_specs=out_specs, check_vma=False)
```

```python
import functools

import jax
import jax.numpy as jnp
from jax import lax
from jax.experimental import pallas as pl
from jax.experimental.pallas import tpu as pltpu
from jax.sharding import PartitionSpec as P

D = 4096
HD = 128
BF = jnp.bfloat16
F32 = jnp.float32
LONGEST = 5 + 18 * 22
POSITIONS = 32
MIB = 1024 * 1024


def rotate(values, row_pos, col_pos):
    quarter = values.shape[-1] // 4
    frequency = 100.0 ** (-jnp.arange(quarter, dtype=jnp.float32) / quarter)
    angles = jnp.concatenate(
        [row_pos[:, None] * frequency[None, :], col_pos[:, None] * frequency[None, :]], axis=1
    )
    cosine = jnp.cos(angles)[:, None, :]
    sine_wave = jnp.sin(angles)[:, None, :]
    former = jnp.concatenate(
        [values[..., :quarter], values[..., 2 * quarter : 3 * quarter]], axis=-1
    )
    latter = jnp.concatenate(
        [values[..., quarter : 2 * quarter], values[..., 3 * quarter :]], axis=-1
    )
    new_former = former * cosine - latter * sine_wave
    new_latter = latter * cosine + former * sine_wave
    return jnp.concatenate(
        [
            new_former[..., :quarter],
            new_latter[..., :quarter],
            new_former[..., quarter:],
            new_latter[..., quarter:],
        ],
        axis=-1,
    )


def normalize(values, totals, squares, ln_gain, ln_shift):
    average = totals / D
    spread = squares / D - average * average
    scale_inv = lax.rsqrt(spread + 1e-06)
    return ((values - average[:, None]) * scale_inv[:, None] * ln_gain + ln_shift).astype(
        jnp.bfloat16
    )


def local_general(
    tokens, ln_gain, ln_shift, w_qkv, w_out, layer_scale, segments, present, coords, owner_slot
):
    own_rows = tokens.astype(jnp.float32)
    totals, squares = lax.psum(
        (jnp.sum(own_rows, axis=1), jnp.sum(own_rows * own_rows, axis=1)), "row"
    )
    normed = normalize(own_rows, totals, squares, ln_gain, ln_shift)
    gathered = lax.all_gather(normed, "col", axis=0, tiled=True)
    slot_count = owner_slot.shape[0]
    at_slot = (
        jnp.zeros((slot_count,), jnp.int32)
        .at[owner_slot]
        .set(jnp.arange(slot_count, dtype=jnp.int32))
    )
    placed = gathered[at_slot]
    group_rows = slot_count // lax.axis_size("row")
    mixed = lax.psum_scatter(
        jnp.dot(placed, w_qkv, preferred_element_type=jnp.float32).astype(jnp.bfloat16),
        "row",
        scatter_dimension=0,
        tiled=True,
    ).astype(jnp.float32)
    heads_here = w_qkv.shape[1] // (3 * HD)
    mixed = mixed.reshape(group_rows, heads_here, 3, HD)
    my_slots = lax.dynamic_slice_in_dim(at_slot, lax.axis_index("row") * group_rows, group_rows, 0)
    row_pos = coords[0][my_slots].astype(jnp.float32)
    col_pos = coords[1][my_slots].astype(jnp.float32)
    seg_rows = segments[my_slots]
    live_rows = present[my_slots]
    query_rows = rotate(mixed[:, :, 0], row_pos, col_pos).astype(jnp.bfloat16)
    key_rows = rotate(mixed[:, :, 1], row_pos, col_pos).astype(jnp.bfloat16)
    values = mixed[:, :, 2].astype(jnp.bfloat16)
    scores = jnp.einsum(
        "qhe,khe->hqk", query_rows, key_rows, preferred_element_type=jnp.float32
    ) * HD ** (-0.5)
    allowed = (seg_rows[:, None] == seg_rows[None, :]) & (live_rows[None, :] == 1)
    scores = jnp.where(allowed[None], scores, -1e30)
    highest = jnp.max(scores, axis=-1, keepdims=True)
    weights = jnp.exp(scores - highest)
    probability = (weights / jnp.sum(weights, axis=-1, keepdims=True)).astype(jnp.bfloat16)
    result = jnp.einsum("hqk,khe->qhe", probability, values, preferred_element_type=jnp.float32)
    attended = (result * live_rows[:, None, None].astype(jnp.float32)).astype(jnp.bfloat16)
    attended = attended.reshape(group_rows, heads_here * HD)
    all_slots = lax.all_gather(attended, "row", axis=0, tiled=True)
    projected = lax.psum_scatter(
        jnp.dot(all_slots[owner_slot], w_out, preferred_element_type=jnp.float32).astype(
            jnp.bfloat16
        ),
        "col",
        scatter_dimension=0,
        tiled=True,
    ).astype(jnp.float32)
    return (own_rows + layer_scale * projected).astype(jnp.bfloat16)


def whole(memory_space=pltpu.VMEM):
    return pl.BlockSpec(memory_space=memory_space)


def qkv_kernel(own, peer, stats, affine_own, affine_peer, w_own, w_peer, keep, send, normed):
    columns = jnp.transpose(stats[...])
    average, scale_inv = columns[:, 0:1], columns[:, 1:2]
    width = own.shape[1]
    for part, (rows, affine) in enumerate(((own, affine_own), (peer, affine_peer))):
        for start in range(0, width, 256):
            piece = slice(start, start + 256)
            out = (rows[:, piece].astype(F32) - average) * scale_inv
            out = out * affine[0:1, piece] + affine[1:2, piece]
            normed[:, part * width + start : part * width + start + 256] = out.astype(BF)
    half = keep.shape[1]
    for target, first in ((send, half), (keep, 0)):
        total = jnp.dot(
            normed[:, :width], w_own[:, first : first + half], preferred_element_type=F32
        )
        total += jnp.dot(
            normed[:, width:], w_peer[:, first : first + half], preferred_element_type=F32
        )
        target[...] = total.astype(BF)


def qkv_block(own, peer, stats, affine_own, affine_peer, w_own, w_peer):
    rows, width = own.shape
    half = w_own.shape[1] // 2
    out = jax.ShapeDtypeStruct((rows, half), BF)
    return pl.pallas_call(
        qkv_kernel,
        out_shape=(out, out),
        in_specs=[whole()] * 7,
        out_specs=(whole(), whole()),
        scratch_shapes=[pltpu.VMEM((rows, 2 * width), BF)],
        compiler_params=pltpu.CompilerParams(vmem_limit_bytes=32 * MIB),
        cost_estimate=pl.CostEstimate(
            flops=2 * rows * 2 * width * 2 * half,
            bytes_accessed=4 * rows * width + 8 * width * half + 4 * rows * half,
            transcendentals=0,
        ),
        name="qkv_block",
    )(own, peer, stats, affine_own, affine_peer, w_own, w_peer)


def turn_kernel(start, kept, received, table, out, angles, sem):
    rows = kept.shape[0]
    at = pl.ds(pl.multiple_of(start[0], 16), rows)
    load = pltpu.make_async_copy(table.at[at, :], angles, sem)
    load.start()
    lane = lax.broadcasted_iota(jnp.int32, (rows, HD), 1)
    first_half = (lane % 64) < 32
    out[:, 2 * HD :] = (
        kept[:, 2 * HD :].astype(F32) + received[:, 2 * HD :].astype(F32)
    ).astype(BF)
    load.wait()
    for part in range(2):
        cols = slice(part * HD, (part + 1) * HD)
        both = kept[:, cols].astype(F32) + received[:, cols].astype(F32)
        swapped = jnp.where(first_half, pltpu.roll(both, HD - 32, 1), pltpu.roll(both, 32, 1))
        out[:, cols] = (both * angles[:, :HD] + swapped * angles[:, HD:]).astype(BF)


def turn(start, kept, received, table):
    rows = kept.shape[0]
    return pl.pallas_call(
        turn_kernel,
        out_shape=jax.ShapeDtypeStruct(kept.shape, BF),
        in_specs=[whole(pltpu.SMEM), whole(), whole(), whole(pl.ANY)],
        out_specs=whole(),
        scratch_shapes=[pltpu.VMEM((rows, 2 * HD), F32), pltpu.SemaphoreType.DMA],
        compiler_params=pltpu.CompilerParams(vmem_limit_bytes=16 * MIB),
        cost_estimate=pl.CostEstimate(
            flops=8 * rows * HD, bytes_accessed=26 * rows * HD, transcendentals=0
        ),
        name="turn",
    )(start, kept, received, table)


def attend_kernel(
    count, tile, windows, starts, firsts, lows, sizes, seg_col, seg_row, *refs
):
    pieces, outs, (turned, sems) = refs[:count], refs[count:-2], refs[-2:]

    def load(k):
        rows = pieces[k].shape[0]
        at = pl.ds(pl.multiple_of(starts[k], 16), rows)
        return pltpu.make_async_copy(pieces[k], turned.at[at, :], sems.at[k])

    for k in range(count):
        load(k).start()
    for k in range(count):
        load(k).wait()
    scale = HD ** (-0.5) * 1.4426950408889634

    for n, out in enumerate(outs):

        def step(j, carry):
            i = firsts[n] + j
            at = pl.ds(pl.multiple_of(i * tile, 16), tile)
            to = pl.ds(pl.multiple_of(j * tile, 16), tile)

            def look(window):
                near = pl.ds(pl.multiple_of(lows[i], 128), window)
                scores = (
                    lax.dot_general(
                        turned[at, :HD],
                        turned[near, HD : 2 * HD],
                        (((1,), (1,)), ((), ())),
                        preferred_element_type=F32,
                    )
                    * scale
                )
                marks = seg_col[at, :]
                scores = jnp.where(marks == seg_row[0:1, near], scores, -1e30)
                highest = jnp.max(scores, axis=1, keepdims=True)
                weights = jnp.exp2(scores - highest)
                total = jnp.sum(weights, axis=1, keepdims=True)
                result = jnp.dot(
                    weights.astype(BF), turned[near, 2 * HD :], preferred_element_type=F32
                )
                live = jnp.where(marks >= 0, 1.0 / total, 0.0)
                out[to, :] = (result * live).astype(BF)

            for kind, window in enumerate(windows):
                pl.when(sizes[i] == kind)(functools.partial(look, window))
            return carry

        lax.fori_loop(0, out.shape[0] // tile, step, 0)


def attend(starts, firsts, lows, sizes, seg_col, seg_row, pieces, block, tile, windows):
    count = len(pieces)
    outs = firsts.shape[0]
    total = seg_col.shape[0]
    return pl.pallas_call(
        functools.partial(attend_kernel, count, tile, windows),
        out_shape=[jax.ShapeDtypeStruct((block, HD), BF)] * outs,
        in_specs=[whole(pltpu.SMEM)] * 4 + [whole()] * 2 + [whole(pl.ANY)] * count,
        out_specs=[whole()] * outs,
        scratch_shapes=[
            pltpu.VMEM((total, 3 * HD), BF),
            pltpu.SemaphoreType.DMA((count,)),
        ],
        compiler_params=pltpu.CompilerParams(vmem_limit_bytes=32 * MIB),
        cost_estimate=pl.CostEstimate(
            flops=4 * outs * block * windows[-1] * HD,
            bytes_accessed=total * HD * 26,
            transcendentals=outs * block * windows[-1],
        ),
        name="attend",
    )(starts, firsts, lows, sizes, seg_col, seg_row, *pieces)


def project_kernel(blocks, slots, *refs):
    weights, parts = refs[:blocks], refs[blocks : blocks + 4]
    out, all_weights, rows, weight_sems, sems = refs[blocks + 4 :]
    depth = weights[0].shape[0]

    def load(m):
        return pltpu.make_async_copy(
            weights[m], all_weights.at[m * depth : (m + 1) * depth, :], weight_sems.at[m]
        )

    def place(m, j):
        start = pl.multiple_of(m * depth + slots[j] * HD, HD)
        return pltpu.make_async_copy(
            parts[j].at[:, m * HD : (m + 1) * HD], rows.at[:, pl.ds(start, HD)], sems.at[4 * m + j]
        )

    for m in range(blocks):
        load(m).start()
        for j in range(4):
            place(m, j).start()
    for m in range(blocks):
        load(m).wait()
        for j in range(4):
            place(m, j).wait()
    for start in range(0, out.shape[1], 256):
        cols = slice(start, start + 256)
        total = jnp.dot(rows[...], all_weights[:, cols], preferred_element_type=F32)
        out[:, cols] = total.astype(out.dtype)


def project(slots, weights, parts, kind):
    blocks = len(weights)
    depth, width = weights[0].shape
    count = parts[0].shape[0]
    return pl.pallas_call(
        functools.partial(project_kernel, blocks),
        out_shape=jax.ShapeDtypeStruct((count, width), kind),
        in_specs=[whole(pltpu.SMEM)] + [whole(pl.ANY)] * (blocks + 4),
        out_specs=whole(),
        scratch_shapes=[
            pltpu.VMEM((blocks * depth, width), BF),
            pltpu.VMEM((count, blocks * depth), BF),
            pltpu.SemaphoreType.DMA((blocks,)),
            pltpu.SemaphoreType.DMA((4 * blocks,)),
        ],
        compiler_params=pltpu.CompilerParams(vmem_limit_bytes=32 * MIB),
        cost_estimate=pl.CostEstimate(
            flops=2 * count * blocks * depth * width,
            bytes_accessed=2 * (blocks * depth * (width + count) + 2 * count * width),
            transcendentals=0,
        ),
        name="project",
    )(slots, *weights, *parts)


def local_heads(
    tokens, ln_gain, ln_shift, w_qkv, w_out, layer_scale, segments, present, coords, owner_slot
):
    rows = lax.axis_size("row")
    cols = lax.axis_size("col")
    count = segments.shape[0]
    block = tokens.shape[0]
    row = lax.axis_index("row")
    col = lax.axis_index("col")
    core, x_index = row % 2, row // 2
    head = 2 * core + x_index

    lines = cols // 2
    ring = list(range(0, lines, 2)) + list(range(lines - 1 - lines % 2, 0, -2))
    after = {z: ring[(i + 1) % lines] for i, z in enumerate(ring)}
    back = {b: a for a, b in after.items()}
    y_swap = [(c, c ^ 1) for c in range(cols)]
    z_next = [(2 * z + y, 2 * after[z] + y) for z in range(lines) for y in range(2)]
    core_swap = [(r, r ^ 1) for r in range(rows)]
    x_swap = [(r, r ^ 2) for r in range(rows)]

    def by_y(value):
        return lax.ppermute(value, "col", y_swap)

    def by_z(value):
        return lax.ppermute(value, "col", z_next)

    def by_core(value):
        return lax.ppermute(value, "row", core_swap)

    def by_x(value):
        return lax.ppermute(value, "row", x_swap)

    def hold(*values):
        return lax.optimization_barrier(values)

    def along(step, z, times):
        for _ in range(times):
            z = step[z]
        return z

    def per_col(value_of):
        return jnp.asarray([value_of(c // 2, c % 2) for c in range(cols)], jnp.int32)[col]

    z_from = per_col(lambda z, y: [(2 * along(back, z, i) + y) * block for i in range(lines)])
    y_from = per_col(lambda z, y: [(2 * along(back, z, i) + 1 - y) * block for i in range(lines)])

    z_tok, y_tok = [tokens], []
    z_new, y_new = by_z(tokens), by_y(tokens)

    own_rows = tokens.astype(F32)
    sums = lax.psum(
        jnp.stack([jnp.sum(own_rows, axis=1), jnp.sum(own_rows * own_rows, axis=1)]), "row"
    )
    average = sums[0] / D
    spread = sums[1] / D - average * average
    own_stats = jnp.concatenate(
        [average[None], lax.rsqrt(spread + 1e-06)[None], jnp.zeros((6, block), F32)]
    )
    ring_stats = [jnp.stack([own_stats, by_y(own_stats)])]
    for i in range(1, lines):
        ring_stats.append(by_z(ring_stats[-1]))

    width = 3 * HD

    def head_columns(which):
        return lax.dynamic_slice_in_dim(w_qkv, which * width, width, 1)

    w_peer = by_core(jnp.concatenate([head_columns(head ^ 2), head_columns(head ^ 3)], axis=1))
    w_own = jnp.concatenate([head_columns(head), head_columns(head ^ 1)], axis=1)
    affine_own = jnp.stack([ln_gain, ln_shift])
    affine_peer = by_core(affine_own)

    quarter = HD // 4
    frequency = 100.0 ** (-jnp.arange(quarter, dtype=F32) / quarter)
    angles = jnp.arange(POSITIONS, dtype=F32)[:, None] * frequency[None, :]
    cosine, sine = jnp.cos(angles), jnp.sin(angles)
    none = jnp.zeros((POSITIONS, 2 * quarter), F32)
    cos_pair = jnp.concatenate([cosine, cosine], axis=1)
    sin_pair = jnp.concatenate([-sine, sine], axis=1)
    turns = jnp.concatenate(
        [
            jnp.concatenate([cos_pair, none, sin_pair, none], axis=1),
            jnp.concatenate([none, cos_pair, none, sin_pair], axis=1),
        ],
        axis=0,
    )
    spots = jnp.arange(POSITIONS, dtype=jnp.int32)
    chosen = jnp.concatenate(
        [coords[0][:, None] == spots[None, :], coords[1][:, None] == spots[None, :]], axis=1
    )
    table = jnp.dot(
        chosen.astype(F32),
        turns,
        precision=lax.Precision.HIGHEST,
        preferred_element_type=F32,
    )

    tile = block // 2
    most = -(-(127 + 2 * (LONGEST - 1) + tile) // 128) * 128
    windows = tuple(sorted({min(count, w) for w in (512, 640, 896, most)}))
    tiles = count // tile
    marks = jnp.where(present == 1, segments, -1)
    heads_of = segments.reshape(tiles, tile)
    real = jnp.sum(present)
    begin = jnp.sum((segments[None, :] < heads_of[:, :1]).astype(jnp.int32), axis=1)
    end = jnp.sum((segments[None, :] <= heads_of[:, -1:]).astype(jnp.int32), axis=1)
    begin = jnp.minimum(begin, real) // 128 * 128
    need = jnp.minimum(end, real) - begin
    sizes = sum((need > w).astype(jnp.int32) for w in windows[:-1])
    spans = sum(jnp.where(sizes == k, w, 0) for k, w in enumerate(windows))
    lows = jnp.minimum(begin, count - spans).astype(jnp.int32)
    seg_col, seg_row = marks[:, None], marks[None, :]

    z_new, y_new, table, seg_col, seg_row, lows, sizes = hold(
        z_new, y_new, table, seg_col, seg_row, lows, sizes
    )

    fresh = [(z_from[0], tokens, ring_stats[0][0])]
    products, exchanged, turned = [], [], []
    w_ring = [w_out]

    def advance():
        nonlocal products, exchanged, fresh
        for at, kept, received in exchanged:
            turned.append((at, turn(at[None], kept, received, table)))
        exchanged = [(at, keep, by_x(send)) for at, keep, send in products]
        products = []
        for at, own, stats in fresh:
            keep, send = qkv_block(
                own, by_core(own), stats, affine_own, affine_peer, w_own, w_peer
            )
            products.append((at, keep, send))
        fresh = []

    def settle(*moving):
        nonlocal products, exchanged, turned
        flat, tree = jax.tree.flatten((moving, products, exchanged, turned))
        moving, products, exchanged, turned = jax.tree.unflatten(tree, hold(*flat))
        return moving

    for i in range(1, lines + 1):
        fresh.append((y_from[i - 1], y_new, ring_stats[i - 1][1]))
        if i == lines:
            break
        z_tok.append(z_new)
        fresh.append((z_from[i], z_new, ring_stats[i][0]))
        if i < lines - 1:
            y_new, z_new = by_y(z_tok[i]), by_z(z_tok[i])
            advance()
            y_new, z_new = settle(y_new, z_new)
        else:
            middle = block // 2
            y_new, y_last = by_y(z_tok[i][:middle]), by_y(z_tok[i][middle:])
            w_ring.append(by_z(w_ring[-1]))
            advance()
            y_new, w_ring[-1] = settle(y_new, w_ring[-1])
            fresh.append((y_from[i], y_new, ring_stats[i][1][:, :middle]))
            fresh.append((y_from[i] + middle, y_last, ring_stats[i][1][:, middle:]))
            break
    w_ring.append(by_z(w_ring[-1]))
    for _ in range(3):
        advance()
    w_ring[-1], = settle(w_ring[-1])
    while len(w_ring) < lines:
        w_ring.append(by_z(w_ring[-1]))
    starts = jnp.stack([at for at, _ in turned]).astype(jnp.int32)
    pieces = [piece for _, piece in turned]

    slots = jnp.stack([head, head ^ 1, head ^ 2, head ^ 3]).astype(jnp.int32)
    ringed = []
    for i in range(lines):
        ringed.append([(2 * z + y, 2 * along(after, z, i) + y) for z in range(lines) for y in range(2)])
    sums = []
    for other in (True, False):
        firsts = per_col(
            lambda z, y: [
                (2 * along(after, z, i) + (1 - y if other else y)) * block // tile
                for i in range(lines)
            ]
        )
        outs = attend(starts, firsts, lows, sizes, seg_col, seg_row, pieces, block, tile, windows)
        arrived = [outs[0]] + [
            lax.ppermute(outs[i], "col", ringed[i]) for i in range(1, lines)
        ]
        group = jnp.concatenate(arrived, axis=1)
        crossed = by_x(group)
        parts = [group, crossed, by_core(group), by_core(crossed)]
        sums.append(project(slots, w_ring, parts, BF if other else F32))
    projected = sums[1] + by_y(sums[0]).astype(F32)
    return (own_rows + layer_scale * projected).astype(BF)


def solution(mesh):
    in_specs = (
        P("col", "row"),
        P("row"),
        P("row"),
        P("row", "col"),
        P("col", "row"),
        P("row"),
        P(),
        P(),
        P(),
        P(),
    )
    out_specs = P("col", "row")
    rows, cols = mesh.shape["row"], mesh.shape["col"]

    def local(*args):
        heads_here = args[3].shape[1] // (3 * HD)
        if rows == 4 and heads_here == 4 and cols % 4 == 0 and args[0].shape[0] % 32 == 0:
            return local_heads(*args)
        return local_general(*args)

    return jax.shard_map(local, mesh=mesh, in_specs=in_specs, out_specs=out_specs, check_vma=False)
```

```python
import functools

import jax
import jax.numpy as jnp
from jax import lax
from jax.experimental import pallas as pl
from jax.experimental.pallas import tpu as pltpu
from jax.sharding import PartitionSpec as P

D = 4096
HD = 128
BF = jnp.bfloat16
F32 = jnp.float32
LONGEST = 5 + 18 * 22
POSITIONS = 32
MIB = 1024 * 1024


def rotate(values, row_pos, col_pos):
    quarter = values.shape[-1] // 4
    frequency = 100.0 ** (-jnp.arange(quarter, dtype=jnp.float32) / quarter)
    angles = jnp.concatenate(
        [row_pos[:, None] * frequency[None, :], col_pos[:, None] * frequency[None, :]], axis=1
    )
    cosine = jnp.cos(angles)[:, None, :]
    sine_wave = jnp.sin(angles)[:, None, :]
    former = jnp.concatenate(
        [values[..., :quarter], values[..., 2 * quarter : 3 * quarter]], axis=-1
    )
    latter = jnp.concatenate(
        [values[..., quarter : 2 * quarter], values[..., 3 * quarter :]], axis=-1
    )
    new_former = former * cosine - latter * sine_wave
    new_latter = latter * cosine + former * sine_wave
    return jnp.concatenate(
        [
            new_former[..., :quarter],
            new_latter[..., :quarter],
            new_former[..., quarter:],
            new_latter[..., quarter:],
        ],
        axis=-1,
    )


def normalize(values, totals, squares, ln_gain, ln_shift):
    average = totals / D
    spread = squares / D - average * average
    scale_inv = lax.rsqrt(spread + 1e-06)
    return ((values - average[:, None]) * scale_inv[:, None] * ln_gain + ln_shift).astype(
        jnp.bfloat16
    )


def local_general(
    tokens, ln_gain, ln_shift, w_qkv, w_out, layer_scale, segments, present, coords, owner_slot
):
    own_rows = tokens.astype(jnp.float32)
    totals, squares = lax.psum(
        (jnp.sum(own_rows, axis=1), jnp.sum(own_rows * own_rows, axis=1)), "row"
    )
    normed = normalize(own_rows, totals, squares, ln_gain, ln_shift)
    gathered = lax.all_gather(normed, "col", axis=0, tiled=True)
    slot_count = owner_slot.shape[0]
    at_slot = (
        jnp.zeros((slot_count,), jnp.int32)
        .at[owner_slot]
        .set(jnp.arange(slot_count, dtype=jnp.int32))
    )
    placed = gathered[at_slot]
    group_rows = slot_count // lax.axis_size("row")
    mixed = lax.psum_scatter(
        jnp.dot(placed, w_qkv, preferred_element_type=jnp.float32).astype(jnp.bfloat16),
        "row",
        scatter_dimension=0,
        tiled=True,
    ).astype(jnp.float32)
    heads_here = w_qkv.shape[1] // (3 * HD)
    mixed = mixed.reshape(group_rows, heads_here, 3, HD)
    my_slots = lax.dynamic_slice_in_dim(at_slot, lax.axis_index("row") * group_rows, group_rows, 0)
    row_pos = coords[0][my_slots].astype(jnp.float32)
    col_pos = coords[1][my_slots].astype(jnp.float32)
    seg_rows = segments[my_slots]
    live_rows = present[my_slots]
    query_rows = rotate(mixed[:, :, 0], row_pos, col_pos).astype(jnp.bfloat16)
    key_rows = rotate(mixed[:, :, 1], row_pos, col_pos).astype(jnp.bfloat16)
    values = mixed[:, :, 2].astype(jnp.bfloat16)
    scores = jnp.einsum(
        "qhe,khe->hqk", query_rows, key_rows, preferred_element_type=jnp.float32
    ) * HD ** (-0.5)
    allowed = (seg_rows[:, None] == seg_rows[None, :]) & (live_rows[None, :] == 1)
    scores = jnp.where(allowed[None], scores, -1e30)
    highest = jnp.max(scores, axis=-1, keepdims=True)
    weights = jnp.exp(scores - highest)
    probability = (weights / jnp.sum(weights, axis=-1, keepdims=True)).astype(jnp.bfloat16)
    result = jnp.einsum("hqk,khe->qhe", probability, values, preferred_element_type=jnp.float32)
    attended = (result * live_rows[:, None, None].astype(jnp.float32)).astype(jnp.bfloat16)
    attended = attended.reshape(group_rows, heads_here * HD)
    all_slots = lax.all_gather(attended, "row", axis=0, tiled=True)
    projected = lax.psum_scatter(
        jnp.dot(all_slots[owner_slot], w_out, preferred_element_type=jnp.float32).astype(
            jnp.bfloat16
        ),
        "col",
        scatter_dimension=0,
        tiled=True,
    ).astype(jnp.float32)
    return (own_rows + layer_scale * projected).astype(jnp.bfloat16)


def whole(memory_space=pltpu.VMEM):
    return pl.BlockSpec(memory_space=memory_space)


def qkv_kernel(count, *refs):
    blocks, rest = refs[: 3 * count], refs[3 * count :]
    affine_own, affine_peer, w_own, w_peer, keep, send, normed = rest
    first = 0
    for own, peer, stats in (blocks[3 * k : 3 * k + 3] for k in range(count)):
        rows, width = own.shape
        columns = jnp.transpose(stats[...])
        average, scale_inv = columns[:, 0:1], columns[:, 1:2]
        for part, (values, affine) in enumerate(((own, affine_own), (peer, affine_peer))):
            for start in range(0, width, 256):
                piece = slice(start, start + 256)
                out = (values[:, piece].astype(F32) - average) * scale_inv
                out = out * affine[0:1, piece] + affine[1:2, piece]
                normed[:rows, part * width + start : part * width + start + 256] = out.astype(BF)
        half = keep.shape[1]
        for target, at in ((send, half), (keep, 0)):
            total = jnp.dot(
                normed[:rows, :width], w_own[:, at : at + half], preferred_element_type=F32
            )
            total += jnp.dot(
                normed[:rows, width:], w_peer[:, at : at + half], preferred_element_type=F32
            )
            target[first : first + rows, :] = total.astype(BF)
        first += rows


def qkv(blocks, affine_own, affine_peer, w_own, w_peer):
    rows = [own.shape[0] for own, _, _ in blocks]
    width, columns = w_own.shape
    out = jax.ShapeDtypeStruct((sum(rows), columns // 2), BF)
    return pl.pallas_call(
        functools.partial(qkv_kernel, len(blocks)),
        out_shape=(out, out),
        in_specs=[whole()] * (3 * len(blocks) + 4),
        out_specs=(whole(), whole()),
        scratch_shapes=[pltpu.VMEM((max(rows), 2 * width), BF)],
        compiler_params=pltpu.CompilerParams(vmem_limit_bytes=32 * MIB),
        cost_estimate=pl.CostEstimate(
            flops=4 * sum(rows) * width * columns,
            bytes_accessed=4 * sum(rows) * width + 4 * width * columns + 2 * sum(rows) * columns,
            transcendentals=0,
        ),
        name="qkv",
    )(*[array for block in blocks for array in block], affine_own, affine_peer, w_own, w_peer)


def turn_kernel(group, block, starts, kept, received, table, *refs):
    out, turned, angles, load_sems, store_sems = refs[-5:]
    count = kept.shape[0] // block

    def place(k):
        return pl.ds(pl.multiple_of(starts[group + k], 16), block)

    def local(k):
        return pl.ds(k * block, block)

    def load(k):
        return pltpu.make_async_copy(table.at[place(k), :], angles.at[local(k), :], load_sems.at[k])

    def store(k):
        return pltpu.make_async_copy(turned.at[local(k), :], out.at[place(k), :], store_sems.at[k])

    for k in range(count):
        load(k).start()
    lane = lax.broadcasted_iota(jnp.int32, (block, HD), 1)
    first_half = (lane % 64) < 32
    for k in range(count):
        rows = slice(k * block, (k + 1) * block)
        turned[rows, 2 * HD :] = (
            kept[rows, 2 * HD :].astype(F32) + received[rows, 2 * HD :].astype(F32)
        ).astype(BF)
        load(k).wait()
        for part in range(2):
            cols = slice(part * HD, (part + 1) * HD)
            both = kept[rows, cols].astype(F32) + received[rows, cols].astype(F32)
            swapped = jnp.where(first_half, pltpu.roll(both, HD - 32, 1), pltpu.roll(both, 32, 1))
            turned[rows, cols] = (both * angles[rows, :HD] + swapped * angles[rows, HD:]).astype(BF)
        store(k).start()
    for k in range(count):
        store(k).wait()


def turn(group, block, starts, kept, received, table, so_far):
    rows, columns = kept.shape
    operands = [starts, kept, received, table] + ([] if so_far is None else [so_far])
    return pl.pallas_call(
        functools.partial(turn_kernel, group, block),
        out_shape=jax.ShapeDtypeStruct((table.shape[0], columns), BF),
        in_specs=[whole(pltpu.SMEM), whole(), whole()] + [whole(pl.ANY)] * (len(operands) - 3),
        out_specs=whole(pl.ANY),
        input_output_aliases={} if so_far is None else {4: 0},
        scratch_shapes=[
            pltpu.VMEM((rows, columns), BF),
            pltpu.VMEM((rows, 2 * HD), F32),
            pltpu.SemaphoreType.DMA((rows // block,)),
            pltpu.SemaphoreType.DMA((rows // block,)),
        ],
        compiler_params=pltpu.CompilerParams(vmem_limit_bytes=16 * MIB),
        cost_estimate=pl.CostEstimate(
            flops=8 * rows * HD, bytes_accessed=26 * rows * HD, transcendentals=0
        ),
        name="turn",
    )(*operands)


def attend_kernel(tile, windows, group, firsts, lows, sizes, seg_col, seg_row, rows, *refs):
    outs, (turned, sem) = refs[:-2], refs[-2:]
    load = pltpu.make_async_copy(rows, turned, sem)
    load.start()
    load.wait()
    scale = HD ** (-0.5) * 1.4426950408889634

    for n, out in enumerate(outs):

        def step(j, carry):
            i = firsts[group + n] + j
            at = pl.ds(pl.multiple_of(i * tile, 16), tile)
            to = pl.ds(pl.multiple_of(j * tile, 16), tile)

            def look(window):
                near = pl.ds(pl.multiple_of(lows[i], 128), window)
                scores = (
                    lax.dot_general(
                        turned[at, :HD],
                        turned[near, HD : 2 * HD],
                        (((1,), (1,)), ((), ())),
                        preferred_element_type=F32,
                    )
                    * scale
                )
                marks = seg_col[at, :]
                scores = jnp.where(marks == seg_row[0:1, near], scores, -1e30)
                highest = jnp.max(scores, axis=1, keepdims=True)
                weights = jnp.exp2(scores - highest)
                total = jnp.sum(weights, axis=1, keepdims=True)
                result = jnp.dot(
                    weights.astype(BF), turned[near, 2 * HD :], preferred_element_type=F32
                )
                live = jnp.where(marks >= 0, 1.0 / total, 0.0)
                out[to, :] = (result * live).astype(BF)

            for kind, window in enumerate(windows):
                pl.when(sizes[i] == kind)(functools.partial(look, window))
            return carry

        lax.fori_loop(0, out.shape[0] // tile, step, 0)


def attend(group, outs, firsts, lows, sizes, seg_col, seg_row, rows, block, tile, windows):
    total = seg_col.shape[0]
    return pl.pallas_call(
        functools.partial(attend_kernel, tile, windows, group),
        out_shape=[jax.ShapeDtypeStruct((block, HD), BF)] * outs,
        in_specs=[whole(pltpu.SMEM)] * 3 + [whole()] * 2 + [whole(pl.ANY)],
        out_specs=[whole()] * outs,
        scratch_shapes=[pltpu.VMEM((total, 3 * HD), BF), pltpu.SemaphoreType.DMA],
        compiler_params=pltpu.CompilerParams(vmem_limit_bytes=32 * MIB),
        cost_estimate=pl.CostEstimate(
            flops=4 * outs * block * windows[-1] * HD,
            bytes_accessed=total * HD * 26,
            transcendentals=outs * block * windows[-1],
        ),
        name="attend",
    )(firsts, lows, sizes, seg_col, seg_row, rows)


def project_kernel(blocks, slots, *refs):
    weights, parts = refs[:blocks], refs[blocks : blocks + 4]
    out, all_weights, rows, weight_sems, sems = refs[blocks + 4 :]
    depth = weights[0].shape[0]

    def load(m):
        return pltpu.make_async_copy(
            weights[m], all_weights.at[m * depth : (m + 1) * depth, :], weight_sems.at[m]
        )

    def place(m, j):
        start = pl.multiple_of(m * depth + slots[j] * HD, HD)
        return pltpu.make_async_copy(
            parts[j].at[:, m * HD : (m + 1) * HD], rows.at[:, pl.ds(start, HD)], sems.at[4 * m + j]
        )

    for m in range(blocks):
        load(m).start()
        for j in range(4):
            place(m, j).start()
    for m in range(blocks):
        load(m).wait()
        for j in range(4):
            place(m, j).wait()
    for start in range(0, out.shape[1], 256):
        cols = slice(start, start + 256)
        total = jnp.dot(rows[...], all_weights[:, cols], preferred_element_type=F32)
        out[:, cols] = total.astype(out.dtype)


def project(slots, weights, parts, kind):
    blocks = len(weights)
    depth, width = weights[0].shape
    count = parts[0].shape[0]
    return pl.pallas_call(
        functools.partial(project_kernel, blocks),
        out_shape=jax.ShapeDtypeStruct((count, width), kind),
        in_specs=[whole(pltpu.SMEM)] + [whole(pl.ANY)] * (blocks + 4),
        out_specs=whole(),
        scratch_shapes=[
            pltpu.VMEM((blocks * depth, width), BF),
            pltpu.VMEM((count, blocks * depth), BF),
            pltpu.SemaphoreType.DMA((blocks,)),
            pltpu.SemaphoreType.DMA((4 * blocks,)),
        ],
        compiler_params=pltpu.CompilerParams(vmem_limit_bytes=32 * MIB),
        cost_estimate=pl.CostEstimate(
            flops=2 * count * blocks * depth * width,
            bytes_accessed=2 * (blocks * depth * (width + count) + 2 * count * width),
            transcendentals=0,
        ),
        name="project",
    )(slots, *weights, *parts)


def local_heads(
    tokens, ln_gain, ln_shift, w_qkv, w_out, layer_scale, segments, present, coords, owner_slot
):
    rows = lax.axis_size("row")
    cols = lax.axis_size("col")
    count = segments.shape[0]
    block = tokens.shape[0]
    row = lax.axis_index("row")
    col = lax.axis_index("col")
    core, x_index = row % 2, row // 2
    head = 2 * core + x_index

    lines = cols // 2
    ring = list(range(0, lines, 2)) + list(range(lines - 1 - lines % 2, 0, -2))
    after = {z: ring[(i + 1) % lines] for i, z in enumerate(ring)}
    back = {b: a for a, b in after.items()}
    y_swap = [(c, c ^ 1) for c in range(cols)]
    z_next = [(2 * z + y, 2 * after[z] + y) for z in range(lines) for y in range(2)]
    core_swap = [(r, r ^ 1) for r in range(rows)]
    x_swap = [(r, r ^ 2) for r in range(rows)]

    def by_y(value):
        return lax.ppermute(value, "col", y_swap)

    def by_z(value):
        return lax.ppermute(value, "col", z_next)

    def by_core(value):
        return lax.ppermute(value, "row", core_swap)

    def by_x(value):
        return lax.ppermute(value, "row", x_swap)

    def hold(*values):
        return lax.optimization_barrier(values)

    def along(step, z, times):
        for _ in range(times):
            z = step[z]
        return z

    def per_col(value_of):
        return jnp.asarray([value_of(c // 2, c % 2) for c in range(cols)], jnp.int32)[col]

    def origins(z, y):
        at = [(0, 0)] + [(k, u) for i in range(1, lines + 1) for k, u in ((i - 1, 1), (i, 0))][:-1]
        return [(2 * along(back, z, i) + (y ^ u)) * block for i, u in at]

    starts = per_col(origins)

    z_tok, y_tok = [tokens], []
    z_new, y_new = by_z(tokens), by_y(tokens)

    own_rows = tokens.astype(F32)
    sums = lax.psum(
        jnp.stack([jnp.sum(own_rows, axis=1), jnp.sum(own_rows * own_rows, axis=1)]), "row"
    )
    average = sums[0] / D
    spread = sums[1] / D - average * average
    own_stats = jnp.concatenate(
        [average[None], lax.rsqrt(spread + 1e-06)[None], jnp.zeros((6, block), F32)]
    )
    ring_stats = [jnp.stack([own_stats, by_y(own_stats)])]
    for i in range(1, lines):
        ring_stats.append(by_z(ring_stats[-1]))

    width = 3 * HD

    def head_columns(which):
        return lax.dynamic_slice_in_dim(w_qkv, which * width, width, 1)

    w_peer = by_core(jnp.concatenate([head_columns(head ^ 2), head_columns(head ^ 3)], axis=1))
    w_own = jnp.concatenate([head_columns(head), head_columns(head ^ 1)], axis=1)
    affine_own = jnp.stack([ln_gain, ln_shift])
    affine_peer = by_core(affine_own)

    quarter = HD // 4
    frequency = 100.0 ** (-jnp.arange(quarter, dtype=F32) / quarter)
    angles = jnp.arange(POSITIONS, dtype=F32)[:, None] * frequency[None, :]
    cosine, sine = jnp.cos(angles), jnp.sin(angles)
    none = jnp.zeros((POSITIONS, 2 * quarter), F32)
    cos_pair = jnp.concatenate([cosine, cosine], axis=1)
    sin_pair = jnp.concatenate([-sine, sine], axis=1)
    turns = jnp.concatenate(
        [
            jnp.concatenate([cos_pair, none, sin_pair, none], axis=1),
            jnp.concatenate([none, cos_pair, none, sin_pair], axis=1),
        ],
        axis=0,
    )
    spots = jnp.arange(POSITIONS, dtype=jnp.int32)
    chosen = jnp.concatenate(
        [coords[0][:, None] == spots[None, :], coords[1][:, None] == spots[None, :]], axis=1
    )
    table = jnp.dot(
        chosen.astype(F32),
        turns,
        precision=lax.Precision.HIGHEST,
        preferred_element_type=F32,
    )

    tile = block // 2
    most = -(-(127 + 2 * (LONGEST - 1) + tile) // 128) * 128
    windows = tuple(sorted({min(count, w) for w in (512, 640, 896, most)}))
    tiles = count // tile
    marks = jnp.where(present == 1, segments, -1)
    heads_of = segments.reshape(tiles, tile)
    real = jnp.sum(present)
    begin = jnp.sum((segments[None, :] < heads_of[:, :1]).astype(jnp.int32), axis=1)
    end = jnp.sum((segments[None, :] <= heads_of[:, -1:]).astype(jnp.int32), axis=1)
    begin = jnp.minimum(begin, real) // 128 * 128
    need = jnp.minimum(end, real) - begin
    sizes = sum((need > w).astype(jnp.int32) for w in windows[:-1])
    spans = sum(jnp.where(sizes == k, w, 0) for k, w in enumerate(windows))
    lows = jnp.minimum(begin, count - spans).astype(jnp.int32)
    seg_col, seg_row = marks[:, None], marks[None, :]

    z_new, y_new, table, seg_col, seg_row, lows, sizes = hold(
        z_new, y_new, table, seg_col, seg_row, lows, sizes
    )

    fresh = [(tokens, ring_stats[0][0])]
    products, exchanged, rows_turned = [], [], None
    w_ring = [w_out]
    done = 0

    def advance():
        nonlocal products, exchanged, rows_turned, fresh, done
        for kept, received in exchanged:
            rows_turned = turn(done, block, starts, kept, received, table, rows_turned)
            done += kept.shape[0] // block
        exchanged = [(keep, by_x(send)) for keep, send in products]
        products = []
        if fresh:
            blocks = [(own, by_core(own), stats) for own, stats in fresh]
            products = [qkv(blocks, affine_own, affine_peer, w_own, w_peer)]
        fresh = []

    def settle(*moving):
        nonlocal products, exchanged, rows_turned
        flat, tree = jax.tree.flatten((moving, products, exchanged, rows_turned))
        moving, products, exchanged, rows_turned = jax.tree.unflatten(tree, hold(*flat))
        return moving

    for i in range(1, lines):
        z_tok.append(z_new)
        fresh += [(y_new, ring_stats[i - 1][1]), (z_new, ring_stats[i][0])]
        y_new = by_y(z_tok[i])
        if i < lines - 1:
            z_new = by_z(z_tok[i])
            advance()
            y_new, z_new = settle(y_new, z_new)
        else:
            w_ring.append(by_z(w_ring[-1]))
            advance()
            y_new, w_ring[-1] = settle(y_new, w_ring[-1])
    fresh = [(y_new, ring_stats[-1][1])]
    w_ring.append(by_z(w_ring[-1]))
    for _ in range(3):
        advance()
    w_ring[-1], = settle(w_ring[-1])

    ringed = [
        [(2 * z + y, 2 * along(after, z, i) + y) for z in range(lines) for y in range(2)]
        for i in range(lines)
    ]
    firsts = per_col(
        lambda z, y: [
            (2 * along(after, z, i) + u) * block // tile for u in (1 - y, y) for i in range(lines)
        ]
    )
    slots = jnp.stack([head, head ^ 1, head ^ 2, head ^ 3]).astype(jnp.int32)

    def attended(group):
        return attend(
            group, lines, firsts, lows, sizes, seg_col, seg_row, rows_turned, block, tile, windows
        )

    def ring_out(outs):
        return [outs[0]] + [lax.ppermute(outs[i], "col", ringed[i]) for i in range(1, lines)]

    def all_heads(arrived):
        group = jnp.concatenate(arrived, axis=1)
        crossed = by_x(group)
        return [group, crossed, by_core(group), by_core(crossed)]

    arrived = ring_out(attended(0))
    own_outs = attended(lines)
    *both, last = hold(*arrived, *own_outs, w_ring[-1])
    arrived, own_outs = both[:lines], both[lines:]
    for _ in range(lines - len(w_ring)):
        last = by_z(last)
        w_ring.append(last)
    other = project(slots, w_ring, all_heads(arrived), BF)
    own = project(slots, w_ring, all_heads(ring_out(own_outs)), F32)
    projected = own + by_y(other).astype(F32)
    return (own_rows + layer_scale * projected).astype(BF)


def solution(mesh):
    in_specs = (
        P("col", "row"),
        P("row"),
        P("row"),
        P("row", "col"),
        P("col", "row"),
        P("row"),
        P(),
        P(),
        P(),
        P(),
    )
    out_specs = P("col", "row")
    rows, cols = mesh.shape["row"], mesh.shape["col"]

    def local(*args):
        heads_here = args[3].shape[1] // (3 * HD)
        if rows == 4 and heads_here == 4 and cols % 4 == 0 and args[0].shape[0] % 32 == 0:
            return local_heads(*args)
        return local_general(*args)

    return jax.shard_map(local, mesh=mesh, in_specs=in_specs, out_specs=out_specs, check_vma=False)
```

```python
import functools

import jax
import jax.numpy as jnp
from jax import lax
from jax.experimental import pallas as pl
from jax.experimental.pallas import tpu as pltpu
from jax.sharding import PartitionSpec as P

D = 4096
HD = 128
BF = jnp.bfloat16
F32 = jnp.float32
LONGEST = 5 + 18 * 22
POSITIONS = 32
MIB = 1024 * 1024
STAT_ROWS = 16


def rotate(values, row_pos, col_pos):
    quarter = values.shape[-1] // 4
    frequency = 100.0 ** (-jnp.arange(quarter, dtype=jnp.float32) / quarter)
    angles = jnp.concatenate(
        [row_pos[:, None] * frequency[None, :], col_pos[:, None] * frequency[None, :]], axis=1
    )
    cosine = jnp.cos(angles)[:, None, :]
    sine_wave = jnp.sin(angles)[:, None, :]
    former = jnp.concatenate(
        [values[..., :quarter], values[..., 2 * quarter : 3 * quarter]], axis=-1
    )
    latter = jnp.concatenate(
        [values[..., quarter : 2 * quarter], values[..., 3 * quarter :]], axis=-1
    )
    new_former = former * cosine - latter * sine_wave
    new_latter = latter * cosine + former * sine_wave
    return jnp.concatenate(
        [
            new_former[..., :quarter],
            new_latter[..., :quarter],
            new_former[..., quarter:],
            new_latter[..., quarter:],
        ],
        axis=-1,
    )


def normalize(values, totals, squares, ln_gain, ln_shift):
    average = totals / D
    spread = squares / D - average * average
    scale_inv = lax.rsqrt(spread + 1e-06)
    return ((values - average[:, None]) * scale_inv[:, None] * ln_gain + ln_shift).astype(
        jnp.bfloat16
    )


def local_general(
    tokens, ln_gain, ln_shift, w_qkv, w_out, layer_scale, segments, present, coords, owner_slot
):
    own_rows = tokens.astype(jnp.float32)
    totals, squares = lax.psum(
        (jnp.sum(own_rows, axis=1), jnp.sum(own_rows * own_rows, axis=1)), "row"
    )
    normed = normalize(own_rows, totals, squares, ln_gain, ln_shift)
    gathered = lax.all_gather(normed, "col", axis=0, tiled=True)
    slot_count = owner_slot.shape[0]
    at_slot = (
        jnp.zeros((slot_count,), jnp.int32)
        .at[owner_slot]
        .set(jnp.arange(slot_count, dtype=jnp.int32))
    )
    placed = gathered[at_slot]
    group_rows = slot_count // lax.axis_size("row")
    mixed = lax.psum_scatter(
        jnp.dot(placed, w_qkv, preferred_element_type=jnp.float32).astype(jnp.bfloat16),
        "row",
        scatter_dimension=0,
        tiled=True,
    ).astype(jnp.float32)
    heads_here = w_qkv.shape[1] // (3 * HD)
    mixed = mixed.reshape(group_rows, heads_here, 3, HD)
    my_slots = lax.dynamic_slice_in_dim(at_slot, lax.axis_index("row") * group_rows, group_rows, 0)
    row_pos = coords[0][my_slots].astype(jnp.float32)
    col_pos = coords[1][my_slots].astype(jnp.float32)
    seg_rows = segments[my_slots]
    live_rows = present[my_slots]
    query_rows = rotate(mixed[:, :, 0], row_pos, col_pos).astype(jnp.bfloat16)
    key_rows = rotate(mixed[:, :, 1], row_pos, col_pos).astype(jnp.bfloat16)
    values = mixed[:, :, 2].astype(jnp.bfloat16)
    scores = jnp.einsum(
        "qhe,khe->hqk", query_rows, key_rows, preferred_element_type=jnp.float32
    ) * HD ** (-0.5)
    allowed = (seg_rows[:, None] == seg_rows[None, :]) & (live_rows[None, :] == 1)
    scores = jnp.where(allowed[None], scores, -1e30)
    highest = jnp.max(scores, axis=-1, keepdims=True)
    weights = jnp.exp(scores - highest)
    probability = (weights / jnp.sum(weights, axis=-1, keepdims=True)).astype(jnp.bfloat16)
    result = jnp.einsum("hqk,khe->qhe", probability, values, preferred_element_type=jnp.float32)
    attended = (result * live_rows[:, None, None].astype(jnp.float32)).astype(jnp.bfloat16)
    attended = attended.reshape(group_rows, heads_here * HD)
    all_slots = lax.all_gather(attended, "row", axis=0, tiled=True)
    projected = lax.psum_scatter(
        jnp.dot(all_slots[owner_slot], w_out, preferred_element_type=jnp.float32).astype(
            jnp.bfloat16
        ),
        "col",
        scatter_dimension=0,
        tiled=True,
    ).astype(jnp.float32)
    return (own_rows + layer_scale * projected).astype(jnp.bfloat16)


def whole(memory_space=pltpu.VMEM):
    return pl.BlockSpec(memory_space=memory_space)


def pack_kernel(sums, out):
    average = sums[0:1, :] / D
    spread = sums[1:2, :] / D - average * average
    rows = []
    for value in (average, lax.rsqrt(spread + 1e-06)):
        for _ in range(3):
            part = value.astype(BF).astype(F32)
            rows.append(part)
            value = value - part
    rows.append(jnp.zeros((STAT_ROWS - len(rows), out.shape[1]), F32))
    out[...] = jnp.concatenate(rows, axis=0).astype(BF)


def pack(sums, width):
    return pl.pallas_call(
        pack_kernel,
        out_shape=jax.ShapeDtypeStruct((STAT_ROWS, width), BF),
        in_specs=[whole()],
        out_specs=whole(),
        compiler_params=pltpu.CompilerParams(vmem_limit_bytes=16 * MIB),
        name="pack",
    )(jnp.pad(sums, ((0, 0), (0, width - sums.shape[1]))))


def join_kernel(plan, count, *refs):
    arrays, outs = refs[:count], refs[count:]
    for k, rows, out, at in plan:
        outs[out][at : at + rows, :] = arrays[k][:rows, :]


def join(arrays, *wanted):
    plan, outs = [], []
    for out, pieces in enumerate(wanted):
        at = 0
        for k, rows in pieces:
            plan.append((k, rows, out, at))
            at += rows
        outs.append(jax.ShapeDtypeStruct((at, arrays[0].shape[1]), BF))
    return pl.pallas_call(
        functools.partial(join_kernel, plan, len(arrays)),
        out_shape=outs,
        in_specs=[whole()] * len(arrays),
        out_specs=[whole()] * len(outs),
        compiler_params=pltpu.CompilerParams(vmem_limit_bytes=24 * MIB),
        name="join",
    )(*arrays)


def qkv_kernel(count, skipped, block, heads, affine_own, affine_peer, w_own, w_peer, *refs):
    blocks, peers, (keep, send, normed) = refs[: 2 * count], refs[2 * count], refs[-3:]
    depth, width = w_own.shape[0], keep.shape[1]
    lanes = -(-block // 128) * 128
    for n in range(count):
        own, stats = blocks[2 * n], blocks[2 * n + 1]
        rows = stats[stats.shape[0] - STAT_ROWS :, :lanes].astype(F32)
        columns = jnp.transpose(rows)[:block]
        average = columns[:, 0:1] + columns[:, 1:2] + columns[:, 2:3]
        scale_inv = columns[:, 3:4] + columns[:, 4:5] + columns[:, 5:6]
        for part in range(2):
            values, affine = ((own, affine_own), (peers, affine_peer))[part]
            top = part * (n + skipped) * block
            for left in range(0, depth, 256):
                piece = slice(left, left + 256)
                out = (values[top : top + block, piece].astype(F32) - average) * scale_inv
                out = out * affine[0:1, piece] + affine[1:2, piece]
                normed[:, part * depth + left : part * depth + left + 256] = out.astype(BF)
        for k, target in ((1, send), (0, keep)):
            chosen = pl.ds(pl.multiple_of(heads[k] * width, HD), width)
            total = jnp.dot(normed[:, :depth], w_own[:, chosen], preferred_element_type=F32)
            total += jnp.dot(
                normed[:, depth:],
                w_peer[:, k * width : (k + 1) * width],
                preferred_element_type=F32,
            )
            target[n * block : (n + 1) * block, :] = total.astype(BF)


def qkv(blocks, peers, skipped, block, heads, affine_own, affine_peer, w_own, w_peer):
    rows = block * len(blocks)
    depth, columns = w_peer.shape
    out = jax.ShapeDtypeStruct((rows, columns // 2), BF)
    arrays = [array for pair in blocks for array in pair]
    return pl.pallas_call(
        functools.partial(qkv_kernel, len(blocks), skipped, block),
        out_shape=(out, out),
        in_specs=[whole(pltpu.SMEM)] + [whole()] * (len(arrays) + 5),
        out_specs=(whole(), whole()),
        scratch_shapes=[pltpu.VMEM((block, 2 * depth), BF)],
        compiler_params=pltpu.CompilerParams(vmem_limit_bytes=32 * MIB),
        cost_estimate=pl.CostEstimate(
            flops=4 * rows * depth * columns,
            bytes_accessed=4 * rows * depth + 4 * depth * columns + 2 * rows * columns,
            transcendentals=0,
        ),
        name="qkv",
    )(heads, affine_own, affine_peer, w_own, w_peer, *arrays, peers)


def turn_kernel(group, block, starts, kept, received, table, *refs):
    out, turned, angles, load_sems, store_sems = refs[-5:]
    count = kept.shape[0] // block

    def place(k):
        return pl.ds(pl.multiple_of(starts[group + k], 16), block)

    def local(k):
        return pl.ds(k * block, block)

    def load(k):
        return pltpu.make_async_copy(table.at[place(k), :], angles.at[local(k), :], load_sems.at[k])

    def store(k):
        return pltpu.make_async_copy(turned.at[local(k), :], out.at[place(k), :], store_sems.at[k])

    for k in range(count):
        load(k).start()
    lane = lax.broadcasted_iota(jnp.int32, (block, HD), 1)
    first_half = (lane % 64) < 32
    for k in range(count):
        rows = slice(k * block, (k + 1) * block)

        def mixed(part):
            cols = slice(part * HD, (part + 1) * HD)
            terms = (ref[rows, cols].astype(F32) for ref in (kept, received))
            return sum(terms)

        turned[rows, 2 * HD :] = mixed(2).astype(BF)
        load(k).wait()
        for part in range(2):
            cols = slice(part * HD, (part + 1) * HD)
            both = mixed(part)
            swapped = jnp.where(first_half, pltpu.roll(both, HD - 32, 1), pltpu.roll(both, 32, 1))
            turned[rows, cols] = (both * angles[rows, :HD] + swapped * angles[rows, HD:]).astype(BF)
        store(k).start()
    for k in range(count):
        store(k).wait()


def turn(group, block, starts, kept, received, table, so_far):
    rows, columns = kept.shape
    operands = [starts, kept, received, table] + ([] if so_far is None else [so_far])
    return pl.pallas_call(
        functools.partial(turn_kernel, group, block),
        out_shape=jax.ShapeDtypeStruct((table.shape[0], columns), BF),
        in_specs=[whole(pltpu.SMEM)] + [whole()] * 2 + [whole(pl.ANY)] * (len(operands) - 3),
        out_specs=whole(pl.ANY),
        input_output_aliases={} if so_far is None else {4: 0},
        scratch_shapes=[
            pltpu.VMEM((rows, columns), BF),
            pltpu.VMEM((rows, 2 * HD), F32),
            pltpu.SemaphoreType.DMA((rows // block,)),
            pltpu.SemaphoreType.DMA((rows // block,)),
        ],
        compiler_params=pltpu.CompilerParams(vmem_limit_bytes=16 * MIB),
        cost_estimate=pl.CostEstimate(
            flops=8 * rows * HD, bytes_accessed=26 * rows * HD, transcendentals=0
        ),
        name="turn",
    )(*operands)


def attend_kernel(tile, windows, group, firsts, lows, sizes, seg_tiles, seg_row, rows, *refs):
    outs, (turned, sem) = refs[:-2], refs[-2:]
    load = pltpu.make_async_copy(rows, turned, sem)
    load.start()
    load.wait()
    scale = HD ** (-0.5) * 1.4426950408889634

    for n, out in enumerate(outs):

        def step(j, carry):
            i = firsts[group + n] + j
            at = pl.ds(pl.multiple_of(i * tile, 16), tile)
            to = pl.ds(pl.multiple_of(j * tile, 16), tile)

            def look(window):
                near = pl.ds(pl.multiple_of(lows[i], 128), window)
                scores = (
                    lax.dot_general(
                        turned[at, :HD],
                        turned[near, HD : 2 * HD],
                        (((1,), (1,)), ((), ())),
                        preferred_element_type=F32,
                    )
                    * scale
                )
                lanes = jnp.broadcast_to(seg_tiles[pl.ds(i, 1), :], (8, tile))
                marks = jnp.transpose(lanes)[:, 0:1]
                scores = jnp.where(marks == seg_row[0:1, near], scores, -1e30)
                highest = jnp.max(scores, axis=1, keepdims=True)
                weights = jnp.exp2(scores - highest)
                total = jnp.sum(weights, axis=1, keepdims=True)
                result = jnp.dot(
                    weights.astype(BF), turned[near, 2 * HD :], preferred_element_type=F32
                )
                live = jnp.where(marks >= 0, 1.0 / total, 0.0)
                out[to, :] = (result * live).astype(BF)

            for kind, window in enumerate(windows):
                pl.when(sizes[i] == kind)(functools.partial(look, window))
            return carry

        lax.fori_loop(0, out.shape[0] // tile, step, 0)


def attend(group, outs, firsts, lows, sizes, seg_tiles, seg_row, rows, block, tile, windows):
    total = rows.shape[0]
    return pl.pallas_call(
        functools.partial(attend_kernel, tile, windows, group),
        out_shape=[jax.ShapeDtypeStruct((block, HD), BF)] * outs,
        in_specs=[whole(pltpu.SMEM)] * 3 + [whole()] * 2 + [whole(pl.ANY)],
        out_specs=[whole()] * outs,
        scratch_shapes=[pltpu.VMEM((total, 3 * HD), BF), pltpu.SemaphoreType.DMA],
        compiler_params=pltpu.CompilerParams(vmem_limit_bytes=32 * MIB),
        cost_estimate=pl.CostEstimate(
            flops=4 * outs * block * windows[-1] * HD,
            bytes_accessed=total * HD * 26,
            transcendentals=outs * block * windows[-1],
        ),
        name="attend",
    )(firsts, lows, sizes, seg_tiles, seg_row, rows)


def project_kernel(pieces, blocks, first, before, slots, *refs):
    weights, parts, rest = refs[:pieces], refs[pieces : pieces + 4], refs[pieces + 4 :]
    earlier, (out, all_weights, rows, weight_sems, sems) = rest[:-5], rest[-5:]
    depth = all_weights.shape[0] // blocks
    copies = []
    top = 0
    for m in range(pieces):
        size = weights[m].shape[0]
        copies.append(
            pltpu.make_async_copy(
                weights[m], all_weights.at[top : top + size, :], weight_sems.at[m]
            )
        )
        top += size
    for m in range(blocks):
        for j in range(4):
            start = pl.multiple_of(m * depth + slots[j] * HD, HD)
            left = (first + m) * HD
            copies.append(
                pltpu.make_async_copy(
                    parts[j].at[:, left : left + HD], rows.at[:, pl.ds(start, HD)], sems.at[4 * m + j]
                )
            )
    for copy in copies:
        copy.start()
    for copy in copies:
        copy.wait()
    for start in range(0, out.shape[1], 256):
        end = min(start + 256, out.shape[1])
        total = jnp.dot(rows[...], all_weights[:, start:end], preferred_element_type=F32)
        if earlier:
            total += earlier[0][:, before + start : before + end]
        out[:, start:end] = total.astype(out.dtype)


def project(slots, first, weights, parts, earlier, kind, left=0):
    pieces = len(weights)
    width = weights[0].shape[1]
    depth = sum(piece.shape[0] for piece in weights)
    blocks = depth // (4 * HD)
    count = parts[0].shape[0]
    more = [] if earlier is None else [earlier]
    return pl.pallas_call(
        functools.partial(project_kernel, pieces, blocks, first, left),
        out_shape=jax.ShapeDtypeStruct((count, width), kind),
        in_specs=[whole(pltpu.SMEM)]
        + [whole(pl.ANY)] * (pieces + 4)
        + [whole()] * len(more),
        out_specs=whole(),
        scratch_shapes=[
            pltpu.VMEM((depth, width), BF),
            pltpu.VMEM((count, depth), BF),
            pltpu.SemaphoreType.DMA((pieces,)),
            pltpu.SemaphoreType.DMA((4 * blocks,)),
        ],
        compiler_params=pltpu.CompilerParams(vmem_limit_bytes=32 * MIB),
        cost_estimate=pl.CostEstimate(
            flops=2 * count * depth * width,
            bytes_accessed=2 * (depth * (width + count) + 2 * count * width),
            transcendentals=0,
        ),
        name="project",
    )(slots, *weights, *parts, *more)


def local_heads(
    tokens, ln_gain, ln_shift, w_qkv, w_out, layer_scale, segments, present, coords, owner_slot
):
    rows = lax.axis_size("row")
    cols = lax.axis_size("col")
    count = segments.shape[0]
    block = tokens.shape[0]
    row = lax.axis_index("row")
    col = lax.axis_index("col")
    core, x_index = row % 2, row // 2
    head = 2 * core + x_index

    lines = cols // 2
    ring = list(range(0, lines, 2)) + list(range(lines - 1 - lines % 2, 0, -2))
    after = {z: ring[(i + 1) % lines] for i, z in enumerate(ring)}
    back = {b: a for a, b in after.items()}
    y_swap = [(c, c ^ 1) for c in range(cols)]
    z_next = [(2 * z + y, 2 * after[z] + y) for z in range(lines) for y in range(2)]
    core_swap = [(r, r ^ 1) for r in range(rows)]
    x_swap = [(r, r ^ 2) for r in range(rows)]

    def by_y(value):
        return lax.ppermute(value, "col", y_swap)

    def by_z(value):
        return lax.ppermute(value, "col", z_next)

    def by_core(value):
        return lax.ppermute(value, "row", core_swap)

    def by_x(value):
        return lax.ppermute(value, "row", x_swap)

    def hold(*values):
        return lax.optimization_barrier(values)

    def along(step, z, times):
        for _ in range(times):
            z = step[z]
        return z

    def per_col(value_of):
        return jnp.asarray([value_of(c // 2, c % 2) for c in range(cols)], jnp.int32)[col]

    def origins(z, y):
        at = [(0, 0)] + [(k, u) for i in range(1, lines + 1) for k, u in ((i - 1, 1), (i, 0))][:-1]
        return [(2 * along(back, z, i) + (y ^ u)) * block for i, u in at]

    starts = per_col(origins)

    z_new, y_new = by_z(tokens), by_y(tokens)
    own_rows = tokens.astype(F32)
    sums = lax.psum(
        jnp.stack([jnp.sum(own_rows, axis=1), jnp.sum(own_rows * own_rows, axis=1)]), "row"
    )
    own_stats = pack(sums, tokens.shape[1])
    z_stats, y_stats = by_z(own_stats), by_y(own_stats)

    heads = jnp.stack([head, head ^ 1, head ^ 2, head ^ 3]).astype(jnp.int32)
    width = 3 * HD

    def head_columns(which):
        return lax.dynamic_slice_in_dim(w_qkv, which * width, width, 1)

    w_sent = jnp.concatenate([head_columns(head ^ 2), head_columns(head ^ 3)], axis=1)
    affine_own = jnp.stack([ln_gain, ln_shift])
    affine_peer = by_core(affine_own)
    z_new, y_new, z_stats, y_stats, w_sent, affine_peer, segments, present, coords = hold(
        z_new, y_new, z_stats, y_stats, w_sent, affine_peer, segments, present, coords
    )
    w_peer = by_core(w_sent)
    y_first = y_new
    (z_new,) = join([z_new, z_stats], [(0, block), (1, STAT_ROWS)])
    (both,) = join([tokens, y_first, z_new], [(0, block), (1, block), (2, block)])

    w_ring = [w_out]
    rows_turned = None

    def product(own, stats, peers, skipped=0):
        return qkv(
            [(own, stats)] if not isinstance(own, list) else list(zip(own, stats)),
            peers, skipped, block, heads, affine_own, affine_peer, w_qkv, w_peer,
        )

    def turn_all(entries):
        nonlocal rows_turned
        for first, kept, received in entries:
            rows_turned = turn(first, block, starts, kept, received, table, rows_turned)

    y_new, ahead, peers = by_y(z_new), by_z(z_new), by_core(both)
    kept, send = product(tokens, own_stats, peers)
    received = by_x(send)
    late_kept, late_send = product([y_first, z_new], [y_stats, z_new], peers, 1)
    y_new, z_new, kept, received, late_kept, late_send, segments, present, coords = hold(
        y_new, ahead, kept, received, late_kept, late_send, segments, present, coords
    )
    exchanged, pending = [(0, kept, received)], [(1, late_kept, late_send)]

    quarter = HD // 4
    frequency = 100.0 ** (-jnp.arange(quarter, dtype=F32) / quarter)
    angles = jnp.arange(POSITIONS, dtype=F32)[:, None] * frequency[None, :]
    cosine, sine = jnp.cos(angles), jnp.sin(angles)
    none = jnp.zeros((POSITIONS, 2 * quarter), F32)
    cos_pair = jnp.concatenate([cosine, cosine], axis=1)
    sin_pair = jnp.concatenate([-sine, sine], axis=1)
    turns = jnp.concatenate(
        [
            jnp.concatenate([cos_pair, none, sin_pair, none], axis=1),
            jnp.concatenate([none, cos_pair, none, sin_pair], axis=1),
        ],
        axis=0,
    )
    spots = jnp.arange(POSITIONS, dtype=jnp.int32)
    chosen = jnp.concatenate(
        [coords[0][:, None] == spots[None, :], coords[1][:, None] == spots[None, :]], axis=1
    )
    table = jnp.dot(
        chosen.astype(F32),
        turns,
        precision=lax.Precision.HIGHEST,
        preferred_element_type=F32,
    )

    tile = block // 2
    most = -(-(127 + 2 * (LONGEST - 1) + tile) // 128) * 128
    windows = tuple(sorted({min(count, w) for w in (512, 640, 896, most)}))
    tiles = count // tile
    marks = jnp.where(present == 1, segments, -1).astype(F32)
    heads_of = segments.reshape(tiles, tile)
    real = jnp.sum(present)
    begin = jnp.sum((segments[None, :] < heads_of[:, :1]).astype(jnp.int32), axis=1)
    end = jnp.sum((segments[None, :] <= heads_of[:, -1:]).astype(jnp.int32), axis=1)
    begin = jnp.minimum(begin, real) // 128 * 128
    need = jnp.minimum(end, real) - begin
    sizes = sum((need > w).astype(jnp.int32) for w in windows[:-1])
    spans = sum(jnp.where(sizes == k, w, 0) for k, w in enumerate(windows))
    lows = jnp.minimum(begin, count - spans).astype(jnp.int32)
    seg_tiles, seg_row = marks.reshape(tiles, tile), marks[None, :]

    for i in range(2, lines):
        last = i == lines - 1
        y_hand, z_hand = y_new, z_new
        y_new = by_y(z_hand)
        ahead = by_z(w_ring[-1] if last else z_hand)
        entries = [(first, kept, by_x(send)) for first, kept, send in pending]
        kept, send = product(z_hand, z_hand, by_core(z_hand))
        late_kept, late_send = product(y_hand, y_hand, by_core(y_hand))
        pending = [(2 * i - 1, late_kept, late_send)]
        if last:
            entries.append((2 * i, kept, by_x(send)))
        else:
            pending.append((2 * i, kept, send))
        turn_all(exchanged)
        extra = (table, seg_tiles, seg_row, lows, sizes)
        arrays = [(kept, received) for _, kept, received in entries]
        later = [(kept, send) for _, kept, send in pending]
        flat, tree = jax.tree.flatten((ahead, y_new, arrays, rows_turned, extra, later))
        held = jax.tree.unflatten(tree, hold(*flat))
        ahead, y_new, arrays, rows_turned, extra, later = held
        table, seg_tiles, seg_row, lows, sizes = extra
        exchanged = [(entry[0], *pair) for entry, pair in zip(entries, arrays)]
        pending = [(entry[0], *pair) for entry, pair in zip(pending, later)]
        if last:
            w_ring.append(ahead)
        else:
            z_new = ahead

    w_ring.append(by_z(w_ring[-1]))
    kept, send = product(y_new, y_new, by_core(y_new))
    pending.append((2 * lines - 1, kept, send))
    turn_all(exchanged)
    turn_all([(first, kept, by_x(send)) for first, kept, send in pending])
    rows_turned, w_ring[-1] = hold(rows_turned, w_ring[-1])

    ringed = [
        [(2 * z + y, 2 * along(after, z, i) + y) for z in range(lines) for y in range(2)]
        for i in range(lines)
    ]
    firsts = per_col(
        lambda z, y: [
            (2 * along(after, z, i) + u) * block // tile for u in (1 - y, y) for i in range(lines)
        ]
    )

    def attended(group):
        return attend(
            group, lines, firsts, lows, sizes, seg_tiles, seg_row, rows_turned, block, tile, windows
        )

    def ring_out(outs):
        return [outs[0]] + [lax.ppermute(outs[i], "col", ringed[i]) for i in range(1, lines)]

    def cross(group):
        return group, by_x(group), by_core(group)

    left = w_out.shape[1] * 3 // 8
    w_left = by_z(w_ring[-1][:, :left])
    other_outs = ring_out(attended(0))
    own_outs = attended(lines)
    *both, w_left, w_last = hold(*other_outs, *own_outs, w_left, w_ring[-1])
    others = cross(jnp.concatenate(both[:lines], axis=1))
    own_outs = ring_out(both[lines:])
    *both, w_last = hold(*others, *own_outs, w_last)
    others, own_outs = both[:3], both[3:]
    w_right = by_z(w_last[:, left:])
    others = [*others, by_core(others[1])]
    owns = cross(jnp.concatenate(own_outs, axis=1))
    other = project(heads, 0, w_ring, others, None, F32)
    crossed = by_y(project(heads, lines - 1, [w_left], others, other, BF))
    *owns, crossed, w_right = hold(*owns, crossed, w_right)
    crossed_right = by_y(project(heads, lines - 1, [w_right], others, other, BF, left))
    owns = [*owns, by_core(owns[1])]
    own = project(heads, 0, w_ring, owns, None, F32)
    own_left = project(heads, lines - 1, [w_left], owns, own, F32)
    own_right = project(heads, lines - 1, [w_right], owns, own, F32, left)
    projected = jnp.concatenate(
        [own_left + crossed.astype(F32), own_right + crossed_right.astype(F32)], axis=1
    )
    return (own_rows + layer_scale * projected).astype(BF)


def solution(mesh):
    in_specs = (
        P("col", "row"),
        P("row"),
        P("row"),
        P("row", "col"),
        P("col", "row"),
        P("row"),
        P(),
        P(),
        P(),
        P(),
    )
    out_specs = P("col", "row")
    rows, cols = mesh.shape["row"], mesh.shape["col"]

    def local(*args):
        heads_here = args[3].shape[1] // (3 * HD)
        if rows == 4 and heads_here == 4 and cols % 4 == 0 and cols > 4 and args[0].shape[0] % 32 == 0:
            return local_heads(*args)
        return local_general(*args)

    return jax.shard_map(local, mesh=mesh, in_specs=in_specs, out_specs=out_specs, check_vma=False)
```

```python
import functools

import jax
import jax.numpy as jnp
from jax import lax
from jax.experimental import pallas as pl
from jax.experimental.pallas import tpu as pltpu
from jax.sharding import PartitionSpec as P

D = 4096
HD = 128
BF = jnp.bfloat16
F32 = jnp.float32
LONGEST = 5 + 18 * 22
POSITIONS = 32
MIB = 1024 * 1024
STAT_ROWS = 16


def rotate(values, row_pos, col_pos):
    quarter = values.shape[-1] // 4
    frequency = 100.0 ** (-jnp.arange(quarter, dtype=jnp.float32) / quarter)
    angles = jnp.concatenate(
        [row_pos[:, None] * frequency[None, :], col_pos[:, None] * frequency[None, :]], axis=1
    )
    cosine = jnp.cos(angles)[:, None, :]
    sine_wave = jnp.sin(angles)[:, None, :]
    former = jnp.concatenate(
        [values[..., :quarter], values[..., 2 * quarter : 3 * quarter]], axis=-1
    )
    latter = jnp.concatenate(
        [values[..., quarter : 2 * quarter], values[..., 3 * quarter :]], axis=-1
    )
    new_former = former * cosine - latter * sine_wave
    new_latter = latter * cosine + former * sine_wave
    return jnp.concatenate(
        [
            new_former[..., :quarter],
            new_latter[..., :quarter],
            new_former[..., quarter:],
            new_latter[..., quarter:],
        ],
        axis=-1,
    )


def normalize(values, totals, squares, ln_gain, ln_shift):
    average = totals / D
    spread = squares / D - average * average
    scale_inv = lax.rsqrt(spread + 1e-06)
    return ((values - average[:, None]) * scale_inv[:, None] * ln_gain + ln_shift).astype(
        jnp.bfloat16
    )


def local_general(
    tokens, ln_gain, ln_shift, w_qkv, w_out, layer_scale, segments, present, coords, owner_slot
):
    own_rows = tokens.astype(jnp.float32)
    totals, squares = lax.psum(
        (jnp.sum(own_rows, axis=1), jnp.sum(own_rows * own_rows, axis=1)), "row"
    )
    normed = normalize(own_rows, totals, squares, ln_gain, ln_shift)
    gathered = lax.all_gather(normed, "col", axis=0, tiled=True)
    slot_count = owner_slot.shape[0]
    at_slot = (
        jnp.zeros((slot_count,), jnp.int32)
        .at[owner_slot]
        .set(jnp.arange(slot_count, dtype=jnp.int32))
    )
    placed = gathered[at_slot]
    group_rows = slot_count // lax.axis_size("row")
    mixed = lax.psum_scatter(
        jnp.dot(placed, w_qkv, preferred_element_type=jnp.float32).astype(jnp.bfloat16),
        "row",
        scatter_dimension=0,
        tiled=True,
    ).astype(jnp.float32)
    heads_here = w_qkv.shape[1] // (3 * HD)
    mixed = mixed.reshape(group_rows, heads_here, 3, HD)
    my_slots = lax.dynamic_slice_in_dim(at_slot, lax.axis_index("row") * group_rows, group_rows, 0)
    row_pos = coords[0][my_slots].astype(jnp.float32)
    col_pos = coords[1][my_slots].astype(jnp.float32)
    seg_rows = segments[my_slots]
    live_rows = present[my_slots]
    query_rows = rotate(mixed[:, :, 0], row_pos, col_pos).astype(jnp.bfloat16)
    key_rows = rotate(mixed[:, :, 1], row_pos, col_pos).astype(jnp.bfloat16)
    values = mixed[:, :, 2].astype(jnp.bfloat16)
    scores = jnp.einsum(
        "qhe,khe->hqk", query_rows, key_rows, preferred_element_type=jnp.float32
    ) * HD ** (-0.5)
    allowed = (seg_rows[:, None] == seg_rows[None, :]) & (live_rows[None, :] == 1)
    scores = jnp.where(allowed[None], scores, -1e30)
    highest = jnp.max(scores, axis=-1, keepdims=True)
    weights = jnp.exp(scores - highest)
    probability = (weights / jnp.sum(weights, axis=-1, keepdims=True)).astype(jnp.bfloat16)
    result = jnp.einsum("hqk,khe->qhe", probability, values, preferred_element_type=jnp.float32)
    attended = (result * live_rows[:, None, None].astype(jnp.float32)).astype(jnp.bfloat16)
    attended = attended.reshape(group_rows, heads_here * HD)
    all_slots = lax.all_gather(attended, "row", axis=0, tiled=True)
    projected = lax.psum_scatter(
        jnp.dot(all_slots[owner_slot], w_out, preferred_element_type=jnp.float32).astype(
            jnp.bfloat16
        ),
        "col",
        scatter_dimension=0,
        tiled=True,
    ).astype(jnp.float32)
    return (own_rows + layer_scale * projected).astype(jnp.bfloat16)


def whole(memory_space=pltpu.VMEM):
    return pl.BlockSpec(memory_space=memory_space)


def pack_kernel(sums, out):
    average = sums[0:1, :] / D
    spread = sums[1:2, :] / D - average * average
    rows = []
    for value in (average, lax.rsqrt(spread + 1e-06)):
        for _ in range(3):
            part = value.astype(BF).astype(F32)
            rows.append(part)
            value = value - part
    rows.append(jnp.zeros((STAT_ROWS - len(rows), out.shape[1]), F32))
    out[...] = jnp.concatenate(rows, axis=0).astype(BF)


def pack(sums, width):
    return pl.pallas_call(
        pack_kernel,
        out_shape=jax.ShapeDtypeStruct((STAT_ROWS, width), BF),
        in_specs=[whole()],
        out_specs=whole(),
        compiler_params=pltpu.CompilerParams(vmem_limit_bytes=16 * MIB),
        name="pack",
    )(jnp.pad(sums, ((0, 0), (0, width - sums.shape[1]))))


def norm_kernel(tokens, stats, gain, shift, out):
    block = tokens.shape[0]
    lanes = -(-block // 128) * 128
    columns = jnp.transpose(stats[:, :lanes].astype(F32))[:block]
    average = columns[:, 0:1] + columns[:, 1:2] + columns[:, 2:3]
    scale_inv = columns[:, 3:4] + columns[:, 4:5] + columns[:, 5:6]
    for left in range(0, tokens.shape[1], 256):
        piece = slice(left, left + 256)
        normed = (tokens[:, piece].astype(F32) - average) * scale_inv
        out[:, piece] = (normed * gain[:, piece] + shift[:, piece]).astype(BF)


def norm(tokens, stats, gain, shift):
    rows, width = tokens.shape
    return pl.pallas_call(
        norm_kernel,
        out_shape=jax.ShapeDtypeStruct(tokens.shape, BF),
        in_specs=[whole()] * 4,
        out_specs=whole(),
        compiler_params=pltpu.CompilerParams(vmem_limit_bytes=16 * MIB),
        cost_estimate=pl.CostEstimate(
            flops=4 * rows * width, bytes_accessed=4 * rows * width, transcendentals=0
        ),
        name="norm",
    )(tokens, stats, gain[None, :], shift[None, :])


def qkv_kernel(count, heads, w_own, w_peer, *refs):
    owns, peers, (keep, send) = refs[:count], refs[count : 2 * count], refs[2 * count :]
    width = keep.shape[1]
    first = 0
    for own, peer in zip(owns, peers):
        rows = own.shape[0]
        for k, target in ((1, send), (0, keep)):
            chosen = pl.ds(pl.multiple_of(heads[k] * width, HD), width)
            total = jnp.dot(own[...], w_own[:, chosen], preferred_element_type=F32)
            total += jnp.dot(
                peer[...], w_peer[:, k * width : (k + 1) * width], preferred_element_type=F32
            )
            target[first : first + rows, :] = total.astype(BF)
        first += rows


def qkv(owns, peers, heads, w_own, w_peer):
    rows = sum(own.shape[0] for own in owns)
    depth, columns = w_peer.shape
    out = jax.ShapeDtypeStruct((rows, columns // 2), BF)
    return pl.pallas_call(
        functools.partial(qkv_kernel, len(owns)),
        out_shape=(out, out),
        in_specs=[whole(pltpu.SMEM)] + [whole()] * (2 + 2 * len(owns)),
        out_specs=(whole(), whole()),
        compiler_params=pltpu.CompilerParams(vmem_limit_bytes=32 * MIB),
        cost_estimate=pl.CostEstimate(
            flops=4 * rows * depth * columns,
            bytes_accessed=4 * rows * depth + 4 * depth * columns + 2 * rows * columns,
            transcendentals=0,
        ),
        name="qkv",
    )(heads, w_own, w_peer, *owns, *peers)


def turn_kernel(group, block, starts, kept, received, table, *refs):
    out, turned, angles, load_sems, store_sems = refs[-5:]
    count = kept.shape[0] // block

    def place(k):
        return pl.ds(pl.multiple_of(starts[group + k], 16), block)

    def local(k):
        return pl.ds(k * block, block)

    def load(k):
        return pltpu.make_async_copy(table.at[place(k), :], angles.at[local(k), :], load_sems.at[k])

    def store(k):
        return pltpu.make_async_copy(turned.at[local(k), :], out.at[place(k), :], store_sems.at[k])

    for k in range(count):
        load(k).start()
    lane = lax.broadcasted_iota(jnp.int32, (block, HD), 1)
    first_half = (lane % 64) < 32
    for k in range(count):
        rows = slice(k * block, (k + 1) * block)

        def mixed(part):
            cols = slice(part * HD, (part + 1) * HD)
            terms = (ref[rows, cols].astype(F32) for ref in (kept, received))
            return sum(terms)

        turned[rows, 2 * HD :] = mixed(2).astype(BF)
        load(k).wait()
        for part in range(2):
            cols = slice(part * HD, (part + 1) * HD)
            both = mixed(part)
            swapped = jnp.where(first_half, pltpu.roll(both, HD - 32, 1), pltpu.roll(both, 32, 1))
            turned[rows, cols] = (both * angles[rows, :HD] + swapped * angles[rows, HD:]).astype(BF)
        store(k).start()
    for k in range(count):
        store(k).wait()


def turn(group, block, starts, kept, received, table, so_far):
    rows, columns = kept.shape
    operands = [starts, kept, received, table] + ([] if so_far is None else [so_far])
    return pl.pallas_call(
        functools.partial(turn_kernel, group, block),
        out_shape=jax.ShapeDtypeStruct((table.shape[0], columns), BF),
        in_specs=[whole(pltpu.SMEM)] + [whole()] * 2 + [whole(pl.ANY)] * (len(operands) - 3),
        out_specs=whole(pl.ANY),
        input_output_aliases={} if so_far is None else {4: 0},
        scratch_shapes=[
            pltpu.VMEM((rows, columns), BF),
            pltpu.VMEM((rows, 2 * HD), F32),
            pltpu.SemaphoreType.DMA((rows // block,)),
            pltpu.SemaphoreType.DMA((rows // block,)),
        ],
        compiler_params=pltpu.CompilerParams(vmem_limit_bytes=16 * MIB),
        cost_estimate=pl.CostEstimate(
            flops=8 * rows * HD, bytes_accessed=26 * rows * HD, transcendentals=0
        ),
        name="turn",
    )(*operands)


def attend_kernel(tile, windows, group, firsts, lows, sizes, seg_tiles, seg_row, rows, *refs):
    outs, (turned, sem) = refs[:-2], refs[-2:]
    load = pltpu.make_async_copy(rows, turned, sem)
    load.start()
    load.wait()
    scale = HD ** (-0.5) * 1.4426950408889634

    for n, out in enumerate(outs):

        def step(j, carry):
            i = firsts[group + n] + j
            at = pl.ds(pl.multiple_of(i * tile, 16), tile)
            to = pl.ds(pl.multiple_of(j * tile, 16), tile)

            def look(window):
                near = pl.ds(pl.multiple_of(lows[i], 128), window)
                scores = (
                    lax.dot_general(
                        turned[at, :HD],
                        turned[near, HD : 2 * HD],
                        (((1,), (1,)), ((), ())),
                        preferred_element_type=F32,
                    )
                    * scale
                )
                lanes = jnp.broadcast_to(seg_tiles[pl.ds(i, 1), :], (8, tile))
                marks = jnp.transpose(lanes)[:, 0:1]
                scores = jnp.where(marks == seg_row[0:1, near], scores, -1e30)
                highest = jnp.max(scores, axis=1, keepdims=True)
                weights = jnp.exp2(scores - highest)
                total = jnp.sum(weights, axis=1, keepdims=True)
                result = jnp.dot(
                    weights.astype(BF), turned[near, 2 * HD :], preferred_element_type=F32
                )
                live = jnp.where(marks >= 0, 1.0 / total, 0.0)
                out[to, :] = (result * live).astype(BF)

            for kind, window in enumerate(windows):
                pl.when(sizes[i] == kind)(functools.partial(look, window))
            return carry

        lax.fori_loop(0, out.shape[0] // tile, step, 0)


def attend(group, outs, firsts, lows, sizes, seg_tiles, seg_row, rows, block, tile, windows):
    total = rows.shape[0]
    return pl.pallas_call(
        functools.partial(attend_kernel, tile, windows, group),
        out_shape=[jax.ShapeDtypeStruct((block, HD), BF)] * outs,
        in_specs=[whole(pltpu.SMEM)] * 3 + [whole()] * 2 + [whole(pl.ANY)],
        out_specs=[whole()] * outs,
        scratch_shapes=[pltpu.VMEM((total, 3 * HD), BF), pltpu.SemaphoreType.DMA],
        compiler_params=pltpu.CompilerParams(vmem_limit_bytes=32 * MIB),
        cost_estimate=pl.CostEstimate(
            flops=4 * outs * block * windows[-1] * HD,
            bytes_accessed=total * HD * 26,
            transcendentals=outs * block * windows[-1],
        ),
        name="attend",
    )(firsts, lows, sizes, seg_tiles, seg_row, rows)


def project_kernel(pieces, blocks, first, before, slots, *refs):
    weights, parts, rest = refs[:pieces], refs[pieces : pieces + 4], refs[pieces + 4 :]
    earlier, (out, all_weights, rows, weight_sems, sems) = rest[:-5], rest[-5:]
    depth = all_weights.shape[0] // blocks
    copies = []
    top = 0
    for m in range(pieces):
        size = weights[m].shape[0]
        copies.append(
            pltpu.make_async_copy(
                weights[m], all_weights.at[top : top + size, :], weight_sems.at[m]
            )
        )
        top += size
    for m in range(blocks):
        for j in range(4):
            start = pl.multiple_of(m * depth + slots[j] * HD, HD)
            left = (first + m) * HD
            copies.append(
                pltpu.make_async_copy(
                    parts[j].at[:, left : left + HD], rows.at[:, pl.ds(start, HD)], sems.at[4 * m + j]
                )
            )
    for copy in copies:
        copy.start()
    for copy in copies:
        copy.wait()
    for start in range(0, out.shape[1], 256):
        end = min(start + 256, out.shape[1])
        total = jnp.dot(rows[...], all_weights[:, start:end], preferred_element_type=F32)
        if earlier:
            total += earlier[0][:, before + start : before + end]
        out[:, start:end] = total.astype(out.dtype)


def project(slots, first, weights, parts, earlier, kind, left=0):
    pieces = len(weights)
    width = weights[0].shape[1]
    depth = sum(piece.shape[0] for piece in weights)
    blocks = depth // (4 * HD)
    count = parts[0].shape[0]
    more = [] if earlier is None else [earlier]
    return pl.pallas_call(
        functools.partial(project_kernel, pieces, blocks, first, left),
        out_shape=jax.ShapeDtypeStruct((count, width), kind),
        in_specs=[whole(pltpu.SMEM)]
        + [whole(pl.ANY)] * (pieces + 4)
        + [whole()] * len(more),
        out_specs=whole(),
        scratch_shapes=[
            pltpu.VMEM((depth, width), BF),
            pltpu.VMEM((count, depth), BF),
            pltpu.SemaphoreType.DMA((pieces,)),
            pltpu.SemaphoreType.DMA((4 * blocks,)),
        ],
        compiler_params=pltpu.CompilerParams(vmem_limit_bytes=32 * MIB),
        cost_estimate=pl.CostEstimate(
            flops=2 * count * depth * width,
            bytes_accessed=2 * (depth * (width + count) + 2 * count * width),
            transcendentals=0,
        ),
        name="project",
    )(slots, *weights, *parts, *more)


def local_heads(
    tokens, ln_gain, ln_shift, w_qkv, w_out, layer_scale, segments, present, coords, owner_slot
):
    rows = lax.axis_size("row")
    cols = lax.axis_size("col")
    count = segments.shape[0]
    block = tokens.shape[0]
    row = lax.axis_index("row")
    col = lax.axis_index("col")
    core, x_index = row % 2, row // 2
    head = 2 * core + x_index

    lines = cols // 2
    ring = list(range(0, lines, 2)) + list(range(lines - 1 - lines % 2, 0, -2))
    after = {z: ring[(i + 1) % lines] for i, z in enumerate(ring)}
    back = {b: a for a, b in after.items()}
    y_swap = [(c, c ^ 1) for c in range(cols)]
    z_next = [(2 * z + y, 2 * after[z] + y) for z in range(lines) for y in range(2)]
    core_swap = [(r, r ^ 1) for r in range(rows)]
    x_swap = [(r, r ^ 2) for r in range(rows)]

    def by_y(value):
        return lax.ppermute(value, "col", y_swap)

    def by_z(value):
        return lax.ppermute(value, "col", z_next)

    def by_core(value):
        return lax.ppermute(value, "row", core_swap)

    def by_x(value):
        return lax.ppermute(value, "row", x_swap)

    def hold(*values):
        return lax.optimization_barrier(values)

    def along(step, z, times):
        for _ in range(times):
            z = step[z]
        return z

    def per_col(value_of):
        return jnp.asarray([value_of(c // 2, c % 2) for c in range(cols)], jnp.int32)[col]

    def origins(z, y):
        at = [(0, 0), (1, 0), (0, 1)]
        at += [(k, u) for i in range(2, lines + 1) for k, u in ((i - 1, 1), (i, 0))][:-1]
        return [(2 * along(back, z, i) + (y ^ u)) * block for i, u in at]

    starts = per_col(origins)

    z_new, y_new = by_z(tokens), by_y(tokens)
    own_rows = tokens.astype(F32)
    sums = lax.psum(
        jnp.stack([jnp.sum(own_rows, axis=1), jnp.sum(own_rows * own_rows, axis=1)]), "row"
    )
    own_stats = pack(sums, tokens.shape[1])
    z_stats, y_stats = by_z(own_stats), by_y(own_stats)

    heads = jnp.stack([head, head ^ 1, head ^ 2, head ^ 3]).astype(jnp.int32)
    width = 3 * HD

    def head_columns(which):
        return lax.dynamic_slice_in_dim(w_qkv, which * width, width, 1)

    w_sent = jnp.concatenate([head_columns(head ^ 2), head_columns(head ^ 3)], axis=1)
    own_normed = norm(tokens, own_stats, ln_gain, ln_shift)
    z_new, y_new, z_stats, y_stats, w_sent, own_normed, segments, present, coords = hold(
        z_new, y_new, z_stats, y_stats, w_sent, own_normed, segments, present, coords
    )
    w_peer = by_core(w_sent)
    z_new = norm(z_new, z_stats, ln_gain, ln_shift)

    w_ring = [w_out]
    rows_turned = None

    def product(*blocks):
        return qkv(blocks, [by_core(own) for own in blocks], heads, w_qkv, w_peer)

    def turn_all(entries):
        nonlocal rows_turned
        for first, kept, received in entries:
            rows_turned = turn(first, block, starts, kept, received, table, rows_turned)

    quarter = HD // 4
    frequency = 100.0 ** (-jnp.arange(quarter, dtype=F32) / quarter)
    angles = jnp.arange(POSITIONS, dtype=F32)[:, None] * frequency[None, :]
    cosine, sine = jnp.cos(angles), jnp.sin(angles)
    none = jnp.zeros((POSITIONS, 2 * quarter), F32)
    cos_pair = jnp.concatenate([cosine, cosine], axis=1)
    sin_pair = jnp.concatenate([-sine, sine], axis=1)
    turns = jnp.concatenate(
        [
            jnp.concatenate([cos_pair, none, sin_pair, none], axis=1),
            jnp.concatenate([none, cos_pair, none, sin_pair], axis=1),
        ],
        axis=0,
    )
    spots = jnp.arange(POSITIONS, dtype=jnp.int32)
    chosen = jnp.concatenate(
        [coords[0][:, None] == spots[None, :], coords[1][:, None] == spots[None, :]], axis=1
    )
    table = jnp.dot(
        chosen.astype(F32),
        turns,
        precision=lax.Precision.HIGHEST,
        preferred_element_type=F32,
    )

    tile = block // 2
    most = -(-(127 + 2 * (LONGEST - 1) + tile) // 128) * 128
    windows = tuple(sorted({min(count, w) for w in (512, 640, 896, most)}))
    tiles = count // tile
    marks = jnp.where(present == 1, segments, -1).astype(F32)
    heads_of = segments.reshape(tiles, tile)
    real = jnp.sum(present)
    begin = jnp.sum((segments[None, :] < heads_of[:, :1]).astype(jnp.int32), axis=1)
    end = jnp.sum((segments[None, :] <= heads_of[:, -1:]).astype(jnp.int32), axis=1)
    begin = jnp.minimum(begin, real) // 128 * 128
    need = jnp.minimum(end, real) - begin
    sizes = sum((need > w).astype(jnp.int32) for w in windows[:-1])
    spans = sum(jnp.where(sizes == k, w, 0) for k, w in enumerate(windows))
    lows = jnp.minimum(begin, count - spans).astype(jnp.int32)
    seg_tiles, seg_row = marks.reshape(tiles, tile), marks[None, :]

    early = [norm(y_new, y_stats, ln_gain, ln_shift)]
    early.append(by_core(early[0]))
    y_new, ahead = by_y(z_new), by_z(z_new)
    kept, send = product(own_normed)
    received = by_x(send)
    late = product(z_new)
    extra = (table, seg_tiles, seg_row, lows, sizes)
    flat, tree = jax.tree.flatten((y_new, ahead, kept, received, early, late, extra))
    y_new, z_new, kept, received, early, late, extra = jax.tree.unflatten(tree, hold(*flat))
    table, seg_tiles, seg_row, lows, sizes = extra
    exchanged, pending = [(0, kept, received)], [(1, *late)]

    for i in range(2, lines):
        last = i == lines - 1
        y_hand, z_hand = y_new, z_new
        y_new = by_y(z_hand)
        ahead = by_z(w_ring[-1] if last else z_hand)
        entries = [(first, kept, by_x(send)) for first, kept, send in pending]
        if early:
            kept, send = qkv(early[:1], early[1:], heads, w_qkv, w_peer)
            entries.append((2, kept, by_x(send)))
            early = []
        kept, send = product(z_hand)
        pending = [(2 * i - 1, *product(y_hand))]
        if last:
            entries.append((2 * i, kept, by_x(send)))
        else:
            pending.append((2 * i, kept, send))
        turn_all(exchanged)
        arrays = [(kept, received) for _, kept, received in entries]
        later = [(kept, send) for _, kept, send in pending]
        flat, tree = jax.tree.flatten((ahead, y_new, arrays, rows_turned, later))
        held = jax.tree.unflatten(tree, hold(*flat))
        ahead, y_new, arrays, rows_turned, later = held
        exchanged = [(entry[0], *pair) for entry, pair in zip(entries, arrays)]
        pending = [(entry[0], *pair) for entry, pair in zip(pending, later)]
        if last:
            w_ring.append(ahead)
        else:
            z_new = ahead

    w_ring.append(by_z(w_ring[-1]))
    kept, send = product(y_new)
    pending.append((2 * lines - 1, kept, send))
    turn_all(exchanged)
    turn_all([(first, kept, by_x(send)) for first, kept, send in pending])
    ringed = [
        [(2 * z + y, 2 * along(after, z, i) + y) for z in range(lines) for y in range(2)]
        for i in range(lines)
    ]
    firsts = per_col(
        lambda z, y: [
            (2 * along(after, z, i) + u) * block // tile for u in (1 - y, y) for i in range(lines)
        ]
    )

    def attended(group):
        return attend(
            group, lines, firsts, lows, sizes, seg_tiles, seg_row, rows_turned, block, tile, windows
        )

    def ring_out(outs):
        return [outs[0]] + [lax.ppermute(outs[i], "col", ringed[i]) for i in range(1, lines)]

    def cross(group):
        return group, by_x(group), by_core(group)

    *other_outs, w_ring[-1] = hold(*attended(0), w_ring[-1])
    other_outs = ring_out(other_outs)
    own_outs = attended(lines)
    *both, w_last = hold(*other_outs, *own_outs, w_ring[-1])
    left = w_out.shape[1] * 4 // 8
    w_left = by_z(w_last[:, :left])
    others = cross(jnp.concatenate(both[:lines], axis=1))
    *both, w_left, w_last = hold(*others, *both[lines:], w_left, w_last)
    others, own_outs = both[:3], ring_out(both[3:])
    w_right = by_z(w_last[:, left:])
    others = [*others, by_core(others[1])]
    other = project(heads, 0, w_ring, others, None, F32)
    crossed = by_y(project(heads, lines - 1, [w_left], others, other, BF))
    owns = cross(jnp.concatenate(own_outs, axis=1))
    crossed, w_right = hold(crossed, w_right)
    crossed_right = by_y(project(heads, lines - 1, [w_right], others, other, BF, left))
    owns = [*owns, by_core(owns[1])]
    own = project(heads, 0, w_ring, owns, None, F32)
    own_left = project(heads, lines - 1, [w_left], owns, own, F32)
    own_right = project(heads, lines - 1, [w_right], owns, own, F32, left)
    projected = jnp.concatenate(
        [own_left + crossed.astype(F32), own_right + crossed_right.astype(F32)], axis=1
    )
    return (own_rows + layer_scale * projected).astype(BF)


def solution(mesh):
    in_specs = (
        P("col", "row"),
        P("row"),
        P("row"),
        P("row", "col"),
        P("col", "row"),
        P("row"),
        P(),
        P(),
        P(),
        P(),
    )
    out_specs = P("col", "row")
    rows, cols = mesh.shape["row"], mesh.shape["col"]

    def local(*args):
        heads_here = args[3].shape[1] // (3 * HD)
        if rows == 4 and heads_here == 4 and cols % 4 == 0 and cols > 4 and args[0].shape[0] % 32 == 0:
            return local_heads(*args)
        return local_general(*args)

    return jax.shard_map(local, mesh=mesh, in_specs=in_specs, out_specs=out_specs, check_vma=False)
```

```python
import functools

import jax
import jax.numpy as jnp
from jax import lax
from jax.experimental import pallas as pl
from jax.experimental.pallas import tpu as pltpu
from jax.sharding import PartitionSpec as P

D = 4096
HD = 128
BF = jnp.bfloat16
F32 = jnp.float32
LONGEST = 5 + 18 * 22
POSITIONS = 32
MIB = 1024 * 1024
STAT_ROWS = 16


def rotate(values, row_pos, col_pos):
    quarter = values.shape[-1] // 4
    frequency = 100.0 ** (-jnp.arange(quarter, dtype=jnp.float32) / quarter)
    angles = jnp.concatenate(
        [row_pos[:, None] * frequency[None, :], col_pos[:, None] * frequency[None, :]], axis=1
    )
    cosine = jnp.cos(angles)[:, None, :]
    sine_wave = jnp.sin(angles)[:, None, :]
    former = jnp.concatenate(
        [values[..., :quarter], values[..., 2 * quarter : 3 * quarter]], axis=-1
    )
    latter = jnp.concatenate(
        [values[..., quarter : 2 * quarter], values[..., 3 * quarter :]], axis=-1
    )
    new_former = former * cosine - latter * sine_wave
    new_latter = latter * cosine + former * sine_wave
    return jnp.concatenate(
        [
            new_former[..., :quarter],
            new_latter[..., :quarter],
            new_former[..., quarter:],
            new_latter[..., quarter:],
        ],
        axis=-1,
    )


def normalize(values, totals, squares, ln_gain, ln_shift):
    average = totals / D
    spread = squares / D - average * average
    scale_inv = lax.rsqrt(spread + 1e-06)
    return ((values - average[:, None]) * scale_inv[:, None] * ln_gain + ln_shift).astype(
        jnp.bfloat16
    )


def local_general(
    tokens, ln_gain, ln_shift, w_qkv, w_out, layer_scale, segments, present, coords, owner_slot
):
    own_rows = tokens.astype(jnp.float32)
    totals, squares = lax.psum(
        (jnp.sum(own_rows, axis=1), jnp.sum(own_rows * own_rows, axis=1)), "row"
    )
    normed = normalize(own_rows, totals, squares, ln_gain, ln_shift)
    gathered = lax.all_gather(normed, "col", axis=0, tiled=True)
    slot_count = owner_slot.shape[0]
    at_slot = (
        jnp.zeros((slot_count,), jnp.int32)
        .at[owner_slot]
        .set(jnp.arange(slot_count, dtype=jnp.int32))
    )
    placed = gathered[at_slot]
    group_rows = slot_count // lax.axis_size("row")
    mixed = lax.psum_scatter(
        jnp.dot(placed, w_qkv, preferred_element_type=jnp.float32).astype(jnp.bfloat16),
        "row",
        scatter_dimension=0,
        tiled=True,
    ).astype(jnp.float32)
    heads_here = w_qkv.shape[1] // (3 * HD)
    mixed = mixed.reshape(group_rows, heads_here, 3, HD)
    my_slots = lax.dynamic_slice_in_dim(at_slot, lax.axis_index("row") * group_rows, group_rows, 0)
    row_pos = coords[0][my_slots].astype(jnp.float32)
    col_pos = coords[1][my_slots].astype(jnp.float32)
    seg_rows = segments[my_slots]
    live_rows = present[my_slots]
    query_rows = rotate(mixed[:, :, 0], row_pos, col_pos).astype(jnp.bfloat16)
    key_rows = rotate(mixed[:, :, 1], row_pos, col_pos).astype(jnp.bfloat16)
    values = mixed[:, :, 2].astype(jnp.bfloat16)
    scores = jnp.einsum(
        "qhe,khe->hqk", query_rows, key_rows, preferred_element_type=jnp.float32
    ) * HD ** (-0.5)
    allowed = (seg_rows[:, None] == seg_rows[None, :]) & (live_rows[None, :] == 1)
    scores = jnp.where(allowed[None], scores, -1e30)
    highest = jnp.max(scores, axis=-1, keepdims=True)
    weights = jnp.exp(scores - highest)
    probability = (weights / jnp.sum(weights, axis=-1, keepdims=True)).astype(jnp.bfloat16)
    result = jnp.einsum("hqk,khe->qhe", probability, values, preferred_element_type=jnp.float32)
    attended = (result * live_rows[:, None, None].astype(jnp.float32)).astype(jnp.bfloat16)
    attended = attended.reshape(group_rows, heads_here * HD)
    all_slots = lax.all_gather(attended, "row", axis=0, tiled=True)
    projected = lax.psum_scatter(
        jnp.dot(all_slots[owner_slot], w_out, preferred_element_type=jnp.float32).astype(
            jnp.bfloat16
        ),
        "col",
        scatter_dimension=0,
        tiled=True,
    ).astype(jnp.float32)
    return (own_rows + layer_scale * projected).astype(jnp.bfloat16)


def whole(memory_space=pltpu.VMEM):
    return pl.BlockSpec(memory_space=memory_space)


def pack_kernel(sums, out):
    average = sums[0:1, :] / D
    spread = sums[1:2, :] / D - average * average
    rows = []
    for value in (average, lax.rsqrt(spread + 1e-06)):
        for _ in range(3):
            part = value.astype(BF).astype(F32)
            rows.append(part)
            value = value - part
    rows.append(jnp.zeros((STAT_ROWS - len(rows), out.shape[1]), F32))
    out[...] = jnp.concatenate(rows, axis=0).astype(BF)


def pack(sums, width):
    return pl.pallas_call(
        pack_kernel,
        out_shape=jax.ShapeDtypeStruct((STAT_ROWS, width), BF),
        in_specs=[whole()],
        out_specs=whole(),
        compiler_params=pltpu.CompilerParams(vmem_limit_bytes=16 * MIB),
        name="pack",
    )(jnp.pad(sums, ((0, 0), (0, width - sums.shape[1]))))


def norm_kernel(tokens, stats, gain, shift, out):
    block = tokens.shape[0]
    lanes = -(-block // 128) * 128
    columns = jnp.transpose(stats[:, :lanes].astype(F32))[:block]
    average = columns[:, 0:1] + columns[:, 1:2] + columns[:, 2:3]
    scale_inv = columns[:, 3:4] + columns[:, 4:5] + columns[:, 5:6]
    for left in range(0, tokens.shape[1], 256):
        piece = slice(left, left + 256)
        normed = (tokens[:, piece].astype(F32) - average) * scale_inv
        out[:, piece] = (normed * gain[:, piece] + shift[:, piece]).astype(BF)


def norm(tokens, stats, gain, shift):
    rows, width = tokens.shape
    return pl.pallas_call(
        norm_kernel,
        out_shape=jax.ShapeDtypeStruct(tokens.shape, BF),
        in_specs=[whole()] * 4,
        out_specs=whole(),
        compiler_params=pltpu.CompilerParams(vmem_limit_bytes=16 * MIB),
        cost_estimate=pl.CostEstimate(
            flops=4 * rows * width, bytes_accessed=4 * rows * width, transcendentals=0
        ),
        name="norm",
    )(tokens, stats, gain[None, :], shift[None, :])


def qkv_kernel(count, heads, w_own, w_peer, *refs):
    owns, peers, (keep, send) = refs[:count], refs[count : 2 * count], refs[2 * count :]
    width = keep.shape[1]
    first = 0
    for own, peer in zip(owns, peers):
        rows = own.shape[0]
        for k, target in ((1, send), (0, keep)):
            chosen = pl.ds(pl.multiple_of(heads[k] * width, HD), width)
            total = jnp.dot(own[...], w_own[:, chosen], preferred_element_type=F32)
            total += jnp.dot(
                peer[...], w_peer[:, k * width : (k + 1) * width], preferred_element_type=F32
            )
            target[first : first + rows, :] = total.astype(BF)
        first += rows


def qkv(owns, peers, heads, w_own, w_peer):
    rows = sum(own.shape[0] for own in owns)
    depth, columns = w_peer.shape
    out = jax.ShapeDtypeStruct((rows, columns // 2), BF)
    return pl.pallas_call(
        functools.partial(qkv_kernel, len(owns)),
        out_shape=(out, out),
        in_specs=[whole(pltpu.SMEM)] + [whole()] * (2 + 2 * len(owns)),
        out_specs=(whole(), whole()),
        compiler_params=pltpu.CompilerParams(vmem_limit_bytes=32 * MIB),
        cost_estimate=pl.CostEstimate(
            flops=4 * rows * depth * columns,
            bytes_accessed=4 * rows * depth + 4 * depth * columns + 2 * rows * columns,
            transcendentals=0,
        ),
        name="qkv",
    )(heads, w_own, w_peer, *owns, *peers)


def turn_kernel(group, block, starts, kept, received, table, *refs):
    out, turned, angles, load_sems, store_sems = refs[-5:]
    count = kept.shape[0] // block

    def place(k):
        return pl.ds(pl.multiple_of(starts[group + k], 16), block)

    def local(k):
        return pl.ds(k * block, block)

    def load(k):
        return pltpu.make_async_copy(table.at[place(k), :], angles.at[local(k), :], load_sems.at[k])

    def store(k):
        return pltpu.make_async_copy(turned.at[local(k), :], out.at[place(k), :], store_sems.at[k])

    for k in range(count):
        load(k).start()
    lane = lax.broadcasted_iota(jnp.int32, (block, HD), 1)
    first_half = (lane % 64) < 32
    for k in range(count):
        rows = slice(k * block, (k + 1) * block)

        def mixed(part):
            cols = slice(part * HD, (part + 1) * HD)
            terms = (ref[rows, cols].astype(F32) for ref in (kept, received))
            return sum(terms)

        turned[rows, 2 * HD :] = mixed(2).astype(BF)
        load(k).wait()
        for part in range(2):
            cols = slice(part * HD, (part + 1) * HD)
            both = mixed(part)
            swapped = jnp.where(first_half, pltpu.roll(both, HD - 32, 1), pltpu.roll(both, 32, 1))
            turned[rows, cols] = (both * angles[rows, :HD] + swapped * angles[rows, HD:]).astype(BF)
        store(k).start()
    for k in range(count):
        store(k).wait()


def turn(group, block, starts, kept, received, table, so_far):
    rows, columns = kept.shape
    operands = [starts, kept, received, table] + ([] if so_far is None else [so_far])
    return pl.pallas_call(
        functools.partial(turn_kernel, group, block),
        out_shape=jax.ShapeDtypeStruct((table.shape[0], columns), BF),
        in_specs=[whole(pltpu.SMEM)] + [whole()] * 2 + [whole(pl.ANY)] * (len(operands) - 3),
        out_specs=whole(pl.ANY),
        input_output_aliases={} if so_far is None else {4: 0},
        scratch_shapes=[
            pltpu.VMEM((rows, columns), BF),
            pltpu.VMEM((rows, 2 * HD), F32),
            pltpu.SemaphoreType.DMA((rows // block,)),
            pltpu.SemaphoreType.DMA((rows // block,)),
        ],
        compiler_params=pltpu.CompilerParams(vmem_limit_bytes=16 * MIB),
        cost_estimate=pl.CostEstimate(
            flops=8 * rows * HD, bytes_accessed=26 * rows * HD, transcendentals=0
        ),
        name="turn",
    )(*operands)


def attend_kernel(tile, windows, group, places, lows, sizes, seg_tiles, seg_row, rows, *refs):
    outs, (turned, result, sem) = refs[:-3], refs[-3:]
    load = pltpu.make_async_copy(rows, turned, sem)
    load.start()
    load.wait()
    scale = HD ** (-0.5) * 1.4426950408889634

    def step(j, carry):
        i = places[group + j]
        at = pl.ds(pl.multiple_of(i * tile, 16), tile)
        to = pl.ds(pl.multiple_of(j * tile, 16), tile)

        def look(window):
            near = pl.ds(pl.multiple_of(lows[i], 128), window)
            scores = (
                lax.dot_general(
                    turned[at, :HD],
                    turned[near, HD : 2 * HD],
                    (((1,), (1,)), ((), ())),
                    preferred_element_type=F32,
                )
                * scale
            )
            lanes = jnp.broadcast_to(seg_tiles[pl.ds(i, 1), :], (8, tile))
            marks = jnp.transpose(lanes)[:, 0:1]
            scores = jnp.where(marks == seg_row[0:1, near], scores, -1e30)
            highest = jnp.max(scores, axis=1, keepdims=True)
            weights = jnp.exp2(scores - highest)
            total = jnp.sum(weights, axis=1, keepdims=True)
            sums = jnp.dot(weights.astype(BF), turned[near, 2 * HD :], preferred_element_type=F32)
            live = jnp.where(marks >= 0, 1.0 / total, 0.0)
            result[to, :] = (sums * live).astype(BF)

        for kind, window in enumerate(windows):
            pl.when(sizes[i] == kind)(functools.partial(look, window))
        return carry

    lax.fori_loop(0, result.shape[0] // tile, step, 0)
    block = outs[0].shape[0]
    for n, out in enumerate(outs):
        out[...] = result[n * block : (n + 1) * block, :]


def attend(group, outs, places, lows, sizes, seg_tiles, seg_row, rows, block, tile, windows):
    total = rows.shape[0]
    return pl.pallas_call(
        functools.partial(attend_kernel, tile, windows, group),
        out_shape=[jax.ShapeDtypeStruct((block, HD), BF)] * outs,
        in_specs=[whole(pltpu.SMEM)] * 3 + [whole()] * 2 + [whole(pl.ANY)],
        out_specs=[whole()] * outs,
        scratch_shapes=[
            pltpu.VMEM((total, 3 * HD), BF),
            pltpu.VMEM((outs * block, HD), BF),
            pltpu.SemaphoreType.DMA,
        ],
        compiler_params=pltpu.CompilerParams(vmem_limit_bytes=32 * MIB),
        cost_estimate=pl.CostEstimate(
            flops=4 * outs * block * windows[-1] * HD,
            bytes_accessed=total * HD * 26,
            transcendentals=outs * block * windows[-1],
        ),
        name="attend",
    )(places, lows, sizes, seg_tiles, seg_row, rows)


def project_kernel(pieces, blocks, first, before, slots, *refs):
    weights, parts, rest = refs[:pieces], refs[pieces : pieces + 4], refs[pieces + 4 :]
    earlier, (out, all_weights, rows, weight_sems, sems) = rest[:-5], rest[-5:]
    depth = all_weights.shape[0] // blocks
    copies = []
    top = 0
    for m in range(pieces):
        size = weights[m].shape[0]
        copies.append(
            pltpu.make_async_copy(
                weights[m], all_weights.at[top : top + size, :], weight_sems.at[m]
            )
        )
        top += size
    for m in range(blocks):
        for j in range(4):
            start = pl.multiple_of(m * depth + slots[j] * HD, HD)
            left = (first + m) * HD
            copies.append(
                pltpu.make_async_copy(
                    parts[j].at[:, left : left + HD], rows.at[:, pl.ds(start, HD)], sems.at[4 * m + j]
                )
            )
    for copy in copies:
        copy.start()
    for copy in copies:
        copy.wait()
    for start in range(0, out.shape[1], 256):
        end = min(start + 256, out.shape[1])
        total = jnp.dot(rows[...], all_weights[:, start:end], preferred_element_type=F32)
        if earlier:
            total += earlier[0][:, before + start : before + end]
        out[:, start:end] = total.astype(out.dtype)


def project(slots, first, weights, parts, earlier, kind, left=0):
    pieces = len(weights)
    width = weights[0].shape[1]
    depth = sum(piece.shape[0] for piece in weights)
    blocks = depth // (4 * HD)
    count = parts[0].shape[0]
    more = [] if earlier is None else [earlier]
    return pl.pallas_call(
        functools.partial(project_kernel, pieces, blocks, first, left),
        out_shape=jax.ShapeDtypeStruct((count, width), kind),
        in_specs=[whole(pltpu.SMEM)]
        + [whole(pl.ANY)] * (pieces + 4)
        + [whole()] * len(more),
        out_specs=whole(),
        scratch_shapes=[
            pltpu.VMEM((depth, width), BF),
            pltpu.VMEM((count, depth), BF),
            pltpu.SemaphoreType.DMA((pieces,)),
            pltpu.SemaphoreType.DMA((4 * blocks,)),
        ],
        compiler_params=pltpu.CompilerParams(vmem_limit_bytes=32 * MIB),
        cost_estimate=pl.CostEstimate(
            flops=2 * count * depth * width,
            bytes_accessed=2 * (depth * (width + count) + 2 * count * width),
            transcendentals=0,
        ),
        name="project",
    )(slots, *weights, *parts, *more)


def local_heads(
    tokens, ln_gain, ln_shift, w_qkv, w_out, layer_scale, segments, present, coords, owner_slot
):
    rows = lax.axis_size("row")
    cols = lax.axis_size("col")
    count = segments.shape[0]
    block = tokens.shape[0]
    row = lax.axis_index("row")
    col = lax.axis_index("col")
    core, x_index = row % 2, row // 2
    head = 2 * core + x_index

    lines = cols // 2
    ring = list(range(0, lines, 2)) + list(range(lines - 1 - lines % 2, 0, -2))
    after = {z: ring[(i + 1) % lines] for i, z in enumerate(ring)}
    back = {b: a for a, b in after.items()}
    y_swap = [(c, c ^ 1) for c in range(cols)]
    z_next = [(2 * z + y, 2 * after[z] + y) for z in range(lines) for y in range(2)]
    core_swap = [(r, r ^ 1) for r in range(rows)]
    x_swap = [(r, r ^ 2) for r in range(rows)]

    def by_y(value):
        return lax.ppermute(value, "col", y_swap)

    def by_z(value):
        return lax.ppermute(value, "col", z_next)

    def by_core(value):
        return lax.ppermute(value, "row", core_swap)

    def by_x(value):
        return lax.ppermute(value, "row", x_swap)

    def hold(*values):
        return lax.optimization_barrier(values)

    def along(step, z, times):
        for _ in range(times):
            z = step[z]
        return z

    def per_col(value_of):
        return jnp.asarray([value_of(c // 2, c % 2) for c in range(cols)], jnp.int32)[col]

    def origins(z, y):
        at = [(0, 0), (1, 0), (0, 1)]
        at += [(k, u) for i in range(2, lines + 1) for k, u in ((i - 1, 1), (i, 0))][:-1]
        return [(2 * along(back, z, i) + (y ^ u)) * block for i, u in at]

    starts = per_col(origins)

    z_new, y_new = by_z(tokens), by_y(tokens)
    own_rows = tokens.astype(F32)
    sums = lax.psum(
        jnp.stack([jnp.sum(own_rows, axis=1), jnp.sum(own_rows * own_rows, axis=1)]), "row"
    )
    own_stats = pack(sums, tokens.shape[1])
    z_stats, y_stats = by_z(own_stats), by_y(own_stats)

    heads = jnp.stack([head, head ^ 1, head ^ 2, head ^ 3]).astype(jnp.int32)
    width = 3 * HD

    def head_columns(which):
        return lax.dynamic_slice_in_dim(w_qkv, which * width, width, 1)

    w_sent = jnp.concatenate([head_columns(head ^ 2), head_columns(head ^ 3)], axis=1)
    own_normed = norm(tokens, own_stats, ln_gain, ln_shift)
    z_new, y_new, z_stats, y_stats, w_sent, own_normed, segments, present, coords = hold(
        z_new, y_new, z_stats, y_stats, w_sent, own_normed, segments, present, coords
    )
    w_peer = by_core(w_sent)
    z_new = norm(z_new, z_stats, ln_gain, ln_shift)

    w_ring = [w_out]
    rows_turned = None

    def product(*blocks):
        return qkv(blocks, [by_core(own) for own in blocks], heads, w_qkv, w_peer)

    def turn_all(entries):
        nonlocal rows_turned
        for first, kept, received in entries:
            rows_turned = turn(first, block, starts, kept, received, table, rows_turned)

    quarter = HD // 4
    frequency = 100.0 ** (-jnp.arange(quarter, dtype=F32) / quarter)
    angles = jnp.arange(POSITIONS, dtype=F32)[:, None] * frequency[None, :]
    cosine, sine = jnp.cos(angles), jnp.sin(angles)
    none = jnp.zeros((POSITIONS, 2 * quarter), F32)
    cos_pair = jnp.concatenate([cosine, cosine], axis=1)
    sin_pair = jnp.concatenate([-sine, sine], axis=1)
    turns = jnp.concatenate(
        [
            jnp.concatenate([cos_pair, none, sin_pair, none], axis=1),
            jnp.concatenate([none, cos_pair, none, sin_pair], axis=1),
        ],
        axis=0,
    )
    spots = jnp.arange(POSITIONS, dtype=jnp.int32)
    chosen = jnp.concatenate(
        [coords[0][:, None] == spots[None, :], coords[1][:, None] == spots[None, :]], axis=1
    )
    table = jnp.dot(
        chosen.astype(F32),
        turns,
        precision=lax.Precision.HIGHEST,
        preferred_element_type=F32,
    )

    tile = block // 2
    most = -(-(127 + 2 * (LONGEST - 1) + tile) // 128) * 128
    windows = tuple(sorted({min(count, w) for w in (512, 640, 896, most)}))
    tiles = count // tile
    marks = jnp.where(present == 1, segments, -1).astype(F32)
    heads_of = segments.reshape(tiles, tile)
    real = jnp.sum(present)
    begin = jnp.sum((segments[None, :] < heads_of[:, :1]).astype(jnp.int32), axis=1)
    end = jnp.sum((segments[None, :] <= heads_of[:, -1:]).astype(jnp.int32), axis=1)
    begin = jnp.minimum(begin, real) // 128 * 128
    need = jnp.minimum(end, real) - begin
    sizes = sum((need > w).astype(jnp.int32) for w in windows[:-1])
    spans = sum(jnp.where(sizes == k, w, 0) for k, w in enumerate(windows))
    lows = jnp.minimum(begin, count - spans).astype(jnp.int32)
    seg_tiles, seg_row = marks.reshape(tiles, tile), marks[None, :]

    early = [norm(y_new, y_stats, ln_gain, ln_shift)]
    early.append(by_core(early[0]))
    y_new, ahead = by_y(z_new), by_z(z_new)
    kept, send = product(own_normed)
    received = by_x(send)
    late = product(z_new)
    extra = (table, seg_tiles, seg_row, lows, sizes)
    flat, tree = jax.tree.flatten((y_new, ahead, kept, received, early, late, extra))
    y_new, z_new, kept, received, early, late, extra = jax.tree.unflatten(tree, hold(*flat))
    table, seg_tiles, seg_row, lows, sizes = extra
    exchanged, pending = [(0, kept, received)], [(1, *late)]

    for i in range(2, lines):
        last = i == lines - 1
        y_hand, z_hand = y_new, z_new
        y_new = by_y(z_hand)
        ahead = by_z(w_ring[-1] if last else z_hand)
        entries = [(first, kept, by_x(send)) for first, kept, send in pending]
        if early:
            kept, send = qkv(early[:1], early[1:], heads, w_qkv, w_peer)
            entries.append((2, kept, by_x(send)))
            early = []
        kept, send = product(z_hand)
        pending = [(2 * i - 1, *product(y_hand))]
        if last:
            entries.append((2 * i, kept, by_x(send)))
        else:
            pending.append((2 * i, kept, send))
        turn_all(exchanged)
        arrays = [(kept, received) for _, kept, received in entries]
        later = [(kept, send) for _, kept, send in pending]
        flat, tree = jax.tree.flatten((ahead, y_new, arrays, rows_turned, later))
        held = jax.tree.unflatten(tree, hold(*flat))
        ahead, y_new, arrays, rows_turned, later = held
        exchanged = [(entry[0], *pair) for entry, pair in zip(entries, arrays)]
        pending = [(entry[0], *pair) for entry, pair in zip(pending, later)]
        if last:
            w_ring.append(ahead)
        else:
            z_new = ahead

    w_ring.append(by_z(w_ring[-1]))
    kept, send = product(y_new)
    pending.append((2 * lines - 1, kept, send))
    turn_all(exchanged)
    turn_all([(first, kept, by_x(send)) for first, kept, send in pending])
    ringed = [
        [(2 * z + y, 2 * along(after, z, i) + y) for z in range(lines) for y in range(2)]
        for i in range(lines)
    ]
    each = block // tile
    places = per_col(
        lambda z, y: [
            (2 * along(after, z, i) + u) * each + part
            for u in (1 - y, y)
            for i in range(lines)
            for part in range(each)
        ]
    )

    def attended(group):
        return attend(
            group * each, lines, places, lows, sizes, seg_tiles, seg_row, rows_turned, block, tile, windows
        )

    def ring_out(outs):
        return [outs[0]] + [lax.ppermute(outs[i], "col", ringed[i]) for i in range(1, lines)]

    def cross(group):
        return group, by_x(group), by_core(group)

    *other_outs, w_ring[-1] = hold(*attended(0), w_ring[-1])
    other_outs = ring_out(other_outs)
    own_outs = attended(lines)
    *both, w_last = hold(*other_outs, *own_outs, w_ring[-1])
    left = w_out.shape[1] * 4 // 8
    w_left = by_z(w_last[:, :left])
    others = cross(jnp.concatenate(both[:lines], axis=1))
    *both, w_left, w_last = hold(*others, *both[lines:], w_left, w_last)
    others, own_outs = both[:3], ring_out(both[3:])
    w_right = by_z(w_last[:, left:])
    others = [*others, by_core(others[1])]
    other = project(heads, 0, w_ring, others, None, F32)
    crossed = by_y(project(heads, lines - 1, [w_left], others, other, BF))
    owns = cross(jnp.concatenate(own_outs, axis=1))
    crossed, w_right = hold(crossed, w_right)
    crossed_right = by_y(project(heads, lines - 1, [w_right], others, other, BF, left))
    owns = [*owns, by_core(owns[1])]
    own = project(heads, 0, w_ring, owns, None, F32)
    own_left = project(heads, lines - 1, [w_left], owns, own, F32)
    own_right = project(heads, lines - 1, [w_right], owns, own, F32, left)
    projected = jnp.concatenate(
        [own_left + crossed.astype(F32), own_right + crossed_right.astype(F32)], axis=1
    )
    return (own_rows + layer_scale * projected).astype(BF)


def solution(mesh):
    in_specs = (
        P("col", "row"),
        P("row"),
        P("row"),
        P("row", "col"),
        P("col", "row"),
        P("row"),
        P(),
        P(),
        P(),
        P(),
    )
    out_specs = P("col", "row")
    rows, cols = mesh.shape["row"], mesh.shape["col"]

    def local(*args):
        heads_here = args[3].shape[1] // (3 * HD)
        if rows == 4 and heads_here == 4 and cols % 4 == 0 and cols > 4 and args[0].shape[0] % 32 == 0:
            return local_heads(*args)
        return local_general(*args)

    return jax.shard_map(local, mesh=mesh, in_specs=in_specs, out_specs=out_specs, check_vma=False)
```

```python
import functools

import jax
import jax.numpy as jnp
from jax import lax
from jax.experimental import pallas as pl
from jax.experimental.pallas import tpu as pltpu
from jax.sharding import PartitionSpec as P

D = 4096
HD = 128
BF = jnp.bfloat16
F32 = jnp.float32
LONGEST = 5 + 18 * 22
POSITIONS = 32
MIB = 1024 * 1024
STAT_ROWS = 16
LIGHT = 100


def rotate(values, row_pos, col_pos):
    quarter = values.shape[-1] // 4
    frequency = 100.0 ** (-jnp.arange(quarter, dtype=jnp.float32) / quarter)
    angles = jnp.concatenate(
        [row_pos[:, None] * frequency[None, :], col_pos[:, None] * frequency[None, :]], axis=1
    )
    cosine = jnp.cos(angles)[:, None, :]
    sine_wave = jnp.sin(angles)[:, None, :]
    former = jnp.concatenate(
        [values[..., :quarter], values[..., 2 * quarter : 3 * quarter]], axis=-1
    )
    latter = jnp.concatenate(
        [values[..., quarter : 2 * quarter], values[..., 3 * quarter :]], axis=-1
    )
    new_former = former * cosine - latter * sine_wave
    new_latter = latter * cosine + former * sine_wave
    return jnp.concatenate(
        [
            new_former[..., :quarter],
            new_latter[..., :quarter],
            new_former[..., quarter:],
            new_latter[..., quarter:],
        ],
        axis=-1,
    )


def normalize(values, totals, squares, ln_gain, ln_shift):
    average = totals / D
    spread = squares / D - average * average
    scale_inv = lax.rsqrt(spread + 1e-06)
    return ((values - average[:, None]) * scale_inv[:, None] * ln_gain + ln_shift).astype(
        jnp.bfloat16
    )


def local_general(
    tokens, ln_gain, ln_shift, w_qkv, w_out, layer_scale, segments, present, coords, owner_slot
):
    own_rows = tokens.astype(jnp.float32)
    totals, squares = lax.psum(
        (jnp.sum(own_rows, axis=1), jnp.sum(own_rows * own_rows, axis=1)), "row"
    )
    normed = normalize(own_rows, totals, squares, ln_gain, ln_shift)
    gathered = lax.all_gather(normed, "col", axis=0, tiled=True)
    slot_count = owner_slot.shape[0]
    at_slot = (
        jnp.zeros((slot_count,), jnp.int32)
        .at[owner_slot]
        .set(jnp.arange(slot_count, dtype=jnp.int32))
    )
    placed = gathered[at_slot]
    group_rows = slot_count // lax.axis_size("row")
    mixed = lax.psum_scatter(
        jnp.dot(placed, w_qkv, preferred_element_type=jnp.float32).astype(jnp.bfloat16),
        "row",
        scatter_dimension=0,
        tiled=True,
    ).astype(jnp.float32)
    heads_here = w_qkv.shape[1] // (3 * HD)
    mixed = mixed.reshape(group_rows, heads_here, 3, HD)
    my_slots = lax.dynamic_slice_in_dim(at_slot, lax.axis_index("row") * group_rows, group_rows, 0)
    row_pos = coords[0][my_slots].astype(jnp.float32)
    col_pos = coords[1][my_slots].astype(jnp.float32)
    seg_rows = segments[my_slots]
    live_rows = present[my_slots]
    query_rows = rotate(mixed[:, :, 0], row_pos, col_pos).astype(jnp.bfloat16)
    key_rows = rotate(mixed[:, :, 1], row_pos, col_pos).astype(jnp.bfloat16)
    values = mixed[:, :, 2].astype(jnp.bfloat16)
    scores = jnp.einsum(
        "qhe,khe->hqk", query_rows, key_rows, preferred_element_type=jnp.float32
    ) * HD ** (-0.5)
    allowed = (seg_rows[:, None] == seg_rows[None, :]) & (live_rows[None, :] == 1)
    scores = jnp.where(allowed[None], scores, -1e30)
    highest = jnp.max(scores, axis=-1, keepdims=True)
    weights = jnp.exp(scores - highest)
    probability = (weights / jnp.sum(weights, axis=-1, keepdims=True)).astype(jnp.bfloat16)
    result = jnp.einsum("hqk,khe->qhe", probability, values, preferred_element_type=jnp.float32)
    attended = (result * live_rows[:, None, None].astype(jnp.float32)).astype(jnp.bfloat16)
    attended = attended.reshape(group_rows, heads_here * HD)
    all_slots = lax.all_gather(attended, "row", axis=0, tiled=True)
    projected = lax.psum_scatter(
        jnp.dot(all_slots[owner_slot], w_out, preferred_element_type=jnp.float32).astype(
            jnp.bfloat16
        ),
        "col",
        scatter_dimension=0,
        tiled=True,
    ).astype(jnp.float32)
    return (own_rows + layer_scale * projected).astype(jnp.bfloat16)


def whole(memory_space=pltpu.VMEM):
    return pl.BlockSpec(memory_space=memory_space)


def pack_kernel(sums, out):
    average = sums[0:1, :] / D
    spread = sums[1:2, :] / D - average * average
    rows = []
    for value in (average, lax.rsqrt(spread + 1e-06)):
        for _ in range(3):
            part = value.astype(BF).astype(F32)
            rows.append(part)
            value = value - part
    rows.append(jnp.zeros((STAT_ROWS - len(rows), out.shape[1]), F32))
    out[...] = jnp.concatenate(rows, axis=0).astype(BF)


def pack(sums, width):
    return pl.pallas_call(
        pack_kernel,
        out_shape=jax.ShapeDtypeStruct((STAT_ROWS, width), BF),
        in_specs=[whole()],
        out_specs=whole(),
        compiler_params=pltpu.CompilerParams(vmem_limit_bytes=16 * MIB),
        name="pack",
    )(jnp.pad(sums, ((0, 0), (0, width - sums.shape[1]))))


def norm_kernel(tokens, stats, gain, shift, out):
    block = tokens.shape[0]
    lanes = -(-block // 128) * 128
    columns = jnp.transpose(stats[:, :lanes].astype(F32))[:block]
    average = columns[:, 0:1] + columns[:, 1:2] + columns[:, 2:3]
    scale_inv = columns[:, 3:4] + columns[:, 4:5] + columns[:, 5:6]
    for left in range(0, tokens.shape[1], 256):
        piece = slice(left, left + 256)
        normed = (tokens[:, piece].astype(F32) - average) * scale_inv
        out[:, piece] = (normed * gain[:, piece] + shift[:, piece]).astype(BF)


def norm(tokens, stats, gain, shift):
    rows, width = tokens.shape
    return pl.pallas_call(
        norm_kernel,
        out_shape=jax.ShapeDtypeStruct(tokens.shape, BF),
        in_specs=[whole()] * 4,
        out_specs=whole(),
        compiler_params=pltpu.CompilerParams(vmem_limit_bytes=16 * MIB),
        cost_estimate=pl.CostEstimate(
            flops=4 * rows * width, bytes_accessed=4 * rows * width, transcendentals=0
        ),
        name="norm",
    )(tokens, stats, gain[None, :], shift[None, :])


def qkv_kernel(count, heads, w_own, w_peer, *refs):
    owns, peers, (keep, send) = refs[:count], refs[count : 2 * count], refs[2 * count :]
    width = keep.shape[1]
    first = 0
    for own, peer in zip(owns, peers):
        rows = own.shape[0]
        for k, target in ((1, send), (0, keep)):
            chosen = pl.ds(pl.multiple_of(heads[k] * width, HD), width)
            total = jnp.dot(own[...], w_own[:, chosen], preferred_element_type=F32)
            total += jnp.dot(
                peer[...], w_peer[:, k * width : (k + 1) * width], preferred_element_type=F32
            )
            target[first : first + rows, :] = total.astype(BF)
        first += rows


def qkv(owns, peers, heads, w_own, w_peer):
    rows = sum(own.shape[0] for own in owns)
    depth, columns = w_peer.shape
    out = jax.ShapeDtypeStruct((rows, columns // 2), BF)
    return pl.pallas_call(
        functools.partial(qkv_kernel, len(owns)),
        out_shape=(out, out),
        in_specs=[whole(pltpu.SMEM)] + [whole()] * (2 + 2 * len(owns)),
        out_specs=(whole(), whole()),
        compiler_params=pltpu.CompilerParams(vmem_limit_bytes=32 * MIB),
        cost_estimate=pl.CostEstimate(
            flops=4 * rows * depth * columns // LIGHT,
            bytes_accessed=(4 * rows * depth + 4 * depth * columns + 2 * rows * columns) // LIGHT,
            transcendentals=0,
        ),
        name="qkv",
    )(heads, w_own, w_peer, *owns, *peers)


def turn_kernel(group, block, starts, kept, received, table, *refs):
    out, turned, angles, load_sems, store_sems = refs[-5:]
    count = kept.shape[0] // block

    def place(k):
        return pl.ds(pl.multiple_of(starts[group + k], 16), block)

    def local(k):
        return pl.ds(k * block, block)

    def load(k):
        return pltpu.make_async_copy(table.at[place(k), :], angles.at[local(k), :], load_sems.at[k])

    def store(k):
        return pltpu.make_async_copy(turned.at[local(k), :], out.at[place(k), :], store_sems.at[k])

    for k in range(count):
        load(k).start()
    lane = lax.broadcasted_iota(jnp.int32, (block, HD), 1)
    first_half = (lane % 64) < 32
    for k in range(count):
        rows = slice(k * block, (k + 1) * block)

        def mixed(part):
            cols = slice(part * HD, (part + 1) * HD)
            terms = (ref[rows, cols].astype(F32) for ref in (kept, received))
            return sum(terms)

        turned[rows, 2 * HD :] = mixed(2).astype(BF)
        load(k).wait()
        for part in range(2):
            cols = slice(part * HD, (part + 1) * HD)
            both = mixed(part)
            swapped = jnp.where(first_half, pltpu.roll(both, HD - 32, 1), pltpu.roll(both, 32, 1))
            turned[rows, cols] = (both * angles[rows, :HD] + swapped * angles[rows, HD:]).astype(BF)
        store(k).start()
    for k in range(count):
        store(k).wait()


def turn(group, block, starts, kept, received, table, so_far):
    rows, columns = kept.shape
    operands = [starts, kept, received, table] + ([] if so_far is None else [so_far])
    return pl.pallas_call(
        functools.partial(turn_kernel, group, block),
        out_shape=jax.ShapeDtypeStruct((table.shape[0], columns), BF),
        in_specs=[whole(pltpu.SMEM)] + [whole()] * 2 + [whole(pl.ANY)] * (len(operands) - 3),
        out_specs=whole(pl.ANY),
        input_output_aliases={} if so_far is None else {4: 0},
        scratch_shapes=[
            pltpu.VMEM((rows, columns), BF),
            pltpu.VMEM((rows, 2 * HD), F32),
            pltpu.SemaphoreType.DMA((rows // block,)),
            pltpu.SemaphoreType.DMA((rows // block,)),
        ],
        compiler_params=pltpu.CompilerParams(vmem_limit_bytes=16 * MIB),
        cost_estimate=pl.CostEstimate(
            flops=8 * rows * HD, bytes_accessed=26 * rows * HD, transcendentals=0
        ),
        name="turn",
    )(*operands)


def attend_kernel(tile, windows, group, places, lows, sizes, seg_tiles, seg_row, rows, *refs):
    outs, (turned, result, sem) = refs[:-3], refs[-3:]
    load = pltpu.make_async_copy(rows, turned, sem)
    load.start()
    load.wait()
    scale = HD ** (-0.5) * 1.4426950408889634

    def step(j, carry):
        i = places[group + j]
        at = pl.ds(pl.multiple_of(i * tile, 16), tile)
        to = pl.ds(pl.multiple_of(j * tile, 16), tile)

        def look(window):
            near = pl.ds(pl.multiple_of(lows[i], 128), window)
            scores = (
                lax.dot_general(
                    turned[at, :HD],
                    turned[near, HD : 2 * HD],
                    (((1,), (1,)), ((), ())),
                    preferred_element_type=F32,
                )
                * scale
            )
            lanes = jnp.broadcast_to(seg_tiles[pl.ds(i, 1), :], (8, tile))
            marks = jnp.transpose(lanes)[:, 0:1]
            scores = jnp.where(marks == seg_row[0:1, near], scores, -1e30)
            highest = jnp.max(scores, axis=1, keepdims=True)
            weights = jnp.exp2(scores - highest)
            total = jnp.sum(weights, axis=1, keepdims=True)
            sums = jnp.dot(weights.astype(BF), turned[near, 2 * HD :], preferred_element_type=F32)
            live = jnp.where(marks >= 0, 1.0 / total, 0.0)
            result[to, :] = (sums * live).astype(BF)

        for kind, window in enumerate(windows):
            pl.when(sizes[i] == kind)(functools.partial(look, window))
        return carry

    lax.fori_loop(0, result.shape[0] // tile, step, 0)
    block = outs[0].shape[0]
    for n, out in enumerate(outs):
        out[...] = result[n * block : (n + 1) * block, :]


def attend(group, outs, places, lows, sizes, seg_tiles, seg_row, rows, block, tile, windows):
    total = rows.shape[0]
    return pl.pallas_call(
        functools.partial(attend_kernel, tile, windows, group),
        out_shape=[jax.ShapeDtypeStruct((block, HD), BF)] * outs,
        in_specs=[whole(pltpu.SMEM)] * 3 + [whole()] * 2 + [whole(pl.ANY)],
        out_specs=[whole()] * outs,
        scratch_shapes=[
            pltpu.VMEM((total, 3 * HD), BF),
            pltpu.VMEM((outs * block, HD), BF),
            pltpu.SemaphoreType.DMA,
        ],
        compiler_params=pltpu.CompilerParams(vmem_limit_bytes=32 * MIB),
        cost_estimate=pl.CostEstimate(
            flops=4 * outs * block * windows[-1] * HD,
            bytes_accessed=total * HD * 26,
            transcendentals=outs * block * windows[-1],
        ),
        name="attend",
    )(places, lows, sizes, seg_tiles, seg_row, rows)


def project_kernel(pieces, blocks, first, before, slots, *refs):
    weights, parts, rest = refs[:pieces], refs[pieces : pieces + 4], refs[pieces + 4 :]
    earlier, (out, all_weights, rows, weight_sems, sems) = rest[:-5], rest[-5:]
    depth = all_weights.shape[0] // blocks
    copies = []
    top = 0
    for m in range(pieces):
        size = weights[m].shape[0]
        copies.append(
            pltpu.make_async_copy(
                weights[m], all_weights.at[top : top + size, :], weight_sems.at[m]
            )
        )
        top += size
    for m in range(blocks):
        for j in range(4):
            start = pl.multiple_of(m * depth + slots[j] * HD, HD)
            left = (first + m) * HD
            copies.append(
                pltpu.make_async_copy(
                    parts[j].at[:, left : left + HD], rows.at[:, pl.ds(start, HD)], sems.at[4 * m + j]
                )
            )
    for copy in copies:
        copy.start()
    for copy in copies:
        copy.wait()
    for start in range(0, out.shape[1], 256):
        end = min(start + 256, out.shape[1])
        total = jnp.dot(rows[...], all_weights[:, start:end], preferred_element_type=F32)
        if earlier:
            total += earlier[0][:, before + start : before + end]
        out[:, start:end] = total.astype(out.dtype)


def project(slots, first, weights, parts, earlier, kind, left=0):
    pieces = len(weights)
    width = weights[0].shape[1]
    depth = sum(piece.shape[0] for piece in weights)
    blocks = depth // (4 * HD)
    count = parts[0].shape[0]
    more = [] if earlier is None else [earlier]
    return pl.pallas_call(
        functools.partial(project_kernel, pieces, blocks, first, left),
        out_shape=jax.ShapeDtypeStruct((count, width), kind),
        in_specs=[whole(pltpu.SMEM)]
        + [whole(pl.ANY)] * (pieces + 4)
        + [whole()] * len(more),
        out_specs=whole(),
        scratch_shapes=[
            pltpu.VMEM((depth, width), BF),
            pltpu.VMEM((count, depth), BF),
            pltpu.SemaphoreType.DMA((pieces,)),
            pltpu.SemaphoreType.DMA((4 * blocks,)),
        ],
        compiler_params=pltpu.CompilerParams(vmem_limit_bytes=32 * MIB),
        cost_estimate=pl.CostEstimate(
            flops=2 * count * depth * width,
            bytes_accessed=2 * (depth * (width + count) + 2 * count * width),
            transcendentals=0,
        ),
        name="project",
    )(slots, *weights, *parts, *more)


def local_heads(
    tokens, ln_gain, ln_shift, w_qkv, w_out, layer_scale, segments, present, coords, owner_slot
):
    rows = lax.axis_size("row")
    cols = lax.axis_size("col")
    count = segments.shape[0]
    block = tokens.shape[0]
    row = lax.axis_index("row")
    col = lax.axis_index("col")
    core, x_index = row % 2, row // 2
    head = 2 * core + x_index

    lines = cols // 2
    ring = list(range(0, lines, 2)) + list(range(lines - 1 - lines % 2, 0, -2))
    after = {z: ring[(i + 1) % lines] for i, z in enumerate(ring)}
    back = {b: a for a, b in after.items()}
    y_swap = [(c, c ^ 1) for c in range(cols)]
    z_next = [(2 * z + y, 2 * after[z] + y) for z in range(lines) for y in range(2)]
    core_swap = [(r, r ^ 1) for r in range(rows)]
    x_swap = [(r, r ^ 2) for r in range(rows)]

    def by_y(value):
        return lax.ppermute(value, "col", y_swap)

    def by_z(value):
        return lax.ppermute(value, "col", z_next)

    def by_core(value):
        return lax.ppermute(value, "row", core_swap)

    def by_x(value):
        return lax.ppermute(value, "row", x_swap)

    def hold(*values):
        return lax.optimization_barrier(values)

    def along(step, z, times):
        for _ in range(times):
            z = step[z]
        return z

    def per_col(value_of):
        return jnp.asarray([value_of(c // 2, c % 2) for c in range(cols)], jnp.int32)[col]

    def origins(z, y):
        at = [(0, 0), (1, 0), (0, 1)]
        at += [(k, u) for i in range(2, lines + 1) for k, u in ((i - 1, 1), (i, 0))][:-1]
        return [(2 * along(back, z, i) + (y ^ u)) * block for i, u in at]

    starts = per_col(origins)

    z_new, y_new = by_z(tokens), by_y(tokens)
    own_rows = tokens.astype(F32)
    sums = lax.psum(
        jnp.stack([jnp.sum(own_rows, axis=1), jnp.sum(own_rows * own_rows, axis=1)]), "row"
    )
    own_stats = pack(sums, tokens.shape[1])
    z_stats, y_stats = by_z(own_stats), by_y(own_stats)

    heads = jnp.stack([head, head ^ 1, head ^ 2, head ^ 3]).astype(jnp.int32)
    width = 3 * HD

    def head_columns(which):
        return lax.dynamic_slice_in_dim(w_qkv, which * width, width, 1)

    w_sent = jnp.concatenate([head_columns(head ^ 2), head_columns(head ^ 3)], axis=1)
    own_normed = norm(tokens, own_stats, ln_gain, ln_shift)
    z_new, y_new, z_stats, y_stats, w_sent, own_normed, segments, present, coords = hold(
        z_new, y_new, z_stats, y_stats, w_sent, own_normed, segments, present, coords
    )
    w_peer = by_core(w_sent)
    z_new = norm(z_new, z_stats, ln_gain, ln_shift)

    w_ring = [w_out]
    rows_turned = None

    def product(*blocks):
        return qkv(blocks, [by_core(own) for own in blocks], heads, w_qkv, w_peer)

    def turn_all(entries):
        nonlocal rows_turned
        for first, kept, received in entries:
            rows_turned = turn(first, block, starts, kept, received, table, rows_turned)

    quarter = HD // 4
    frequency = 100.0 ** (-jnp.arange(quarter, dtype=F32) / quarter)
    angles = jnp.arange(POSITIONS, dtype=F32)[:, None] * frequency[None, :]
    cosine, sine = jnp.cos(angles), jnp.sin(angles)
    none = jnp.zeros((POSITIONS, 2 * quarter), F32)
    cos_pair = jnp.concatenate([cosine, cosine], axis=1)
    sin_pair = jnp.concatenate([-sine, sine], axis=1)
    turns = jnp.concatenate(
        [
            jnp.concatenate([cos_pair, none, sin_pair, none], axis=1),
            jnp.concatenate([none, cos_pair, none, sin_pair], axis=1),
        ],
        axis=0,
    )
    spots = jnp.arange(POSITIONS, dtype=jnp.int32)
    chosen = jnp.concatenate(
        [coords[0][:, None] == spots[None, :], coords[1][:, None] == spots[None, :]], axis=1
    )
    table = jnp.dot(
        chosen.astype(F32),
        turns,
        precision=lax.Precision.HIGHEST,
        preferred_element_type=F32,
    )

    tile = block // 2
    most = -(-(127 + 2 * (LONGEST - 1) + tile) // 128) * 128
    windows = tuple(sorted({min(count, w) for w in (512, 640, 896, most)}))
    tiles = count // tile
    marks = jnp.where(present == 1, segments, -1).astype(F32)
    heads_of = segments.reshape(tiles, tile)
    real = jnp.sum(present)
    begin = jnp.sum((segments[None, :] < heads_of[:, :1]).astype(jnp.int32), axis=1)
    end = jnp.sum((segments[None, :] <= heads_of[:, -1:]).astype(jnp.int32), axis=1)
    begin = jnp.minimum(begin, real) // 128 * 128
    need = jnp.minimum(end, real) - begin
    sizes = sum((need > w).astype(jnp.int32) for w in windows[:-1])
    spans = sum(jnp.where(sizes == k, w, 0) for k, w in enumerate(windows))
    lows = jnp.minimum(begin, count - spans).astype(jnp.int32)
    seg_tiles, seg_row = marks.reshape(tiles, tile), marks[None, :]

    early = [norm(y_new, y_stats, ln_gain, ln_shift)]
    early.append(by_core(early[0]))
    y_new, ahead = by_y(z_new), by_z(z_new)
    kept, send = product(own_normed)
    received = by_x(send)
    late = product(z_new)
    extra = (table, seg_tiles, seg_row, lows, sizes)
    flat, tree = jax.tree.flatten((y_new, ahead, kept, received, early, late, extra))
    y_new, z_new, kept, received, early, late, extra = jax.tree.unflatten(tree, hold(*flat))
    table, seg_tiles, seg_row, lows, sizes = extra
    exchanged, pending = [(0, kept, received)], [(1, *late)]

    for i in range(2, lines):
        last = i == lines - 1
        y_hand, z_hand = y_new, z_new
        y_new = by_y(z_hand)
        ahead = by_z(w_ring[-1] if last else z_hand)
        entries = [(first, kept, by_x(send)) for first, kept, send in pending]
        if early:
            kept, send = qkv(early[:1], early[1:], heads, w_qkv, w_peer)
            entries.append((2, kept, by_x(send)))
            early = []
        kept, send = product(z_hand)
        pending = [(2 * i - 1, *product(y_hand))]
        if last:
            entries.append((2 * i, kept, by_x(send)))
        else:
            pending.append((2 * i, kept, send))
        turn_all(exchanged)
        arrays = [(kept, received) for _, kept, received in entries]
        later = [(kept, send) for _, kept, send in pending]
        flat, tree = jax.tree.flatten((ahead, y_new, arrays, rows_turned, later))
        held = jax.tree.unflatten(tree, hold(*flat))
        ahead, y_new, arrays, rows_turned, later = held
        exchanged = [(entry[0], *pair) for entry, pair in zip(entries, arrays)]
        pending = [(entry[0], *pair) for entry, pair in zip(pending, later)]
        if last:
            w_ring.append(ahead)
        else:
            z_new = ahead

    w_ring.append(by_z(w_ring[-1]))
    kept, send = product(y_new)
    pending.append((2 * lines - 1, kept, send))
    turn_all(exchanged)
    turn_all([(first, kept, by_x(send)) for first, kept, send in pending])
    ringed = [
        [(2 * z + y, 2 * along(after, z, i) + y) for z in range(lines) for y in range(2)]
        for i in range(lines)
    ]
    each = block // tile
    places = per_col(
        lambda z, y: [
            (2 * along(after, z, i) + u) * each + part
            for u in (1 - y, y)
            for i in range(lines)
            for part in range(each)
        ]
    )

    def attended(group):
        return attend(
            group * each, lines, places, lows, sizes, seg_tiles, seg_row, rows_turned, block, tile, windows
        )

    def ring_out(outs):
        return [outs[0]] + [lax.ppermute(outs[i], "col", ringed[i]) for i in range(1, lines)]

    def cross(group):
        return group, by_x(group), by_core(group)

    *other_outs, w_ring[-1] = hold(*attended(0), w_ring[-1])
    other_outs = ring_out(other_outs)
    own_outs = attended(lines)
    *both, w_last = hold(*other_outs, *own_outs, w_ring[-1])
    left = w_out.shape[1] * 4 // 8
    w_left = by_z(w_last[:, :left])
    others = cross(jnp.concatenate(both[:lines], axis=1))
    *both, w_left, w_last = hold(*others, *both[lines:], w_left, w_last)
    others, own_outs = both[:3], ring_out(both[3:])
    w_right = by_z(w_last[:, left:])
    others = [*others, by_core(others[1])]
    other = project(heads, 0, w_ring, others, None, F32)
    crossed = by_y(project(heads, lines - 1, [w_left], others, other, BF))
    owns = cross(jnp.concatenate(own_outs, axis=1))
    crossed, w_right = hold(crossed, w_right)
    crossed_right = by_y(project(heads, lines - 1, [w_right], others, other, BF, left))
    owns = [*owns, by_core(owns[1])]
    own = project(heads, 0, w_ring, owns, None, F32)
    own_left = project(heads, lines - 1, [w_left], owns, own, F32)
    own_right = project(heads, lines - 1, [w_right], owns, own, F32, left)
    projected = jnp.concatenate(
        [own_left + crossed.astype(F32), own_right + crossed_right.astype(F32)], axis=1
    )
    return (own_rows + layer_scale * projected).astype(BF)


def solution(mesh):
    in_specs = (
        P("col", "row"),
        P("row"),
        P("row"),
        P("row", "col"),
        P("col", "row"),
        P("row"),
        P(),
        P(),
        P(),
        P(),
    )
    out_specs = P("col", "row")
    rows, cols = mesh.shape["row"], mesh.shape["col"]

    def local(*args):
        heads_here = args[3].shape[1] // (3 * HD)
        if rows == 4 and heads_here == 4 and cols % 4 == 0 and cols > 4 and args[0].shape[0] % 32 == 0:
            return local_heads(*args)
        return local_general(*args)

    return jax.shard_map(local, mesh=mesh, in_specs=in_specs, out_specs=out_specs, check_vma=False)
```

```python
import functools

import jax
import jax.numpy as jnp
from jax import lax
from jax.experimental import pallas as pl
from jax.experimental.pallas import tpu as pltpu
from jax.sharding import PartitionSpec as P

D = 4096
HD = 128
BF = jnp.bfloat16
F32 = jnp.float32
LONGEST = 5 + 18 * 22
POSITIONS = 32
MIB = 1024 * 1024
STAT_ROWS = 16
URGENT = 20 * 10**9
LIGHT = 100


def rotate(values, row_pos, col_pos):
    quarter = values.shape[-1] // 4
    frequency = 100.0 ** (-jnp.arange(quarter, dtype=jnp.float32) / quarter)
    angles = jnp.concatenate(
        [row_pos[:, None] * frequency[None, :], col_pos[:, None] * frequency[None, :]], axis=1
    )
    cosine = jnp.cos(angles)[:, None, :]
    sine_wave = jnp.sin(angles)[:, None, :]
    former = jnp.concatenate(
        [values[..., :quarter], values[..., 2 * quarter : 3 * quarter]], axis=-1
    )
    latter = jnp.concatenate(
        [values[..., quarter : 2 * quarter], values[..., 3 * quarter :]], axis=-1
    )
    new_former = former * cosine - latter * sine_wave
    new_latter = latter * cosine + former * sine_wave
    return jnp.concatenate(
        [
            new_former[..., :quarter],
            new_latter[..., :quarter],
            new_former[..., quarter:],
            new_latter[..., quarter:],
        ],
        axis=-1,
    )


def normalize(values, totals, squares, ln_gain, ln_shift):
    average = totals / D
    spread = squares / D - average * average
    scale_inv = lax.rsqrt(spread + 1e-06)
    return ((values - average[:, None]) * scale_inv[:, None] * ln_gain + ln_shift).astype(
        jnp.bfloat16
    )


def local_general(
    tokens, ln_gain, ln_shift, w_qkv, w_out, layer_scale, segments, present, coords, owner_slot
):
    own_rows = tokens.astype(jnp.float32)
    totals, squares = lax.psum(
        (jnp.sum(own_rows, axis=1), jnp.sum(own_rows * own_rows, axis=1)), "row"
    )
    normed = normalize(own_rows, totals, squares, ln_gain, ln_shift)
    gathered = lax.all_gather(normed, "col", axis=0, tiled=True)
    slot_count = owner_slot.shape[0]
    at_slot = (
        jnp.zeros((slot_count,), jnp.int32)
        .at[owner_slot]
        .set(jnp.arange(slot_count, dtype=jnp.int32))
    )
    placed = gathered[at_slot]
    group_rows = slot_count // lax.axis_size("row")
    mixed = lax.psum_scatter(
        jnp.dot(placed, w_qkv, preferred_element_type=jnp.float32).astype(jnp.bfloat16),
        "row",
        scatter_dimension=0,
        tiled=True,
    ).astype(jnp.float32)
    heads_here = w_qkv.shape[1] // (3 * HD)
    mixed = mixed.reshape(group_rows, heads_here, 3, HD)
    my_slots = lax.dynamic_slice_in_dim(at_slot, lax.axis_index("row") * group_rows, group_rows, 0)
    row_pos = coords[0][my_slots].astype(jnp.float32)
    col_pos = coords[1][my_slots].astype(jnp.float32)
    seg_rows = segments[my_slots]
    live_rows = present[my_slots]
    query_rows = rotate(mixed[:, :, 0], row_pos, col_pos).astype(jnp.bfloat16)
    key_rows = rotate(mixed[:, :, 1], row_pos, col_pos).astype(jnp.bfloat16)
    values = mixed[:, :, 2].astype(jnp.bfloat16)
    scores = jnp.einsum(
        "qhe,khe->hqk", query_rows, key_rows, preferred_element_type=jnp.float32
    ) * HD ** (-0.5)
    allowed = (seg_rows[:, None] == seg_rows[None, :]) & (live_rows[None, :] == 1)
    scores = jnp.where(allowed[None], scores, -1e30)
    highest = jnp.max(scores, axis=-1, keepdims=True)
    weights = jnp.exp(scores - highest)
    probability = (weights / jnp.sum(weights, axis=-1, keepdims=True)).astype(jnp.bfloat16)
    result = jnp.einsum("hqk,khe->qhe", probability, values, preferred_element_type=jnp.float32)
    attended = (result * live_rows[:, None, None].astype(jnp.float32)).astype(jnp.bfloat16)
    attended = attended.reshape(group_rows, heads_here * HD)
    all_slots = lax.all_gather(attended, "row", axis=0, tiled=True)
    projected = lax.psum_scatter(
        jnp.dot(all_slots[owner_slot], w_out, preferred_element_type=jnp.float32).astype(
            jnp.bfloat16
        ),
        "col",
        scatter_dimension=0,
        tiled=True,
    ).astype(jnp.float32)
    return (own_rows + layer_scale * projected).astype(jnp.bfloat16)


def whole(memory_space=pltpu.VMEM):
    return pl.BlockSpec(memory_space=memory_space)


def pack_kernel(sums, out):
    average = sums[0:1, :] / D
    spread = sums[1:2, :] / D - average * average
    rows = []
    for value in (average, lax.rsqrt(spread + 1e-06)):
        for _ in range(3):
            part = value.astype(BF).astype(F32)
            rows.append(part)
            value = value - part
    rows.append(jnp.zeros((STAT_ROWS - len(rows), out.shape[1]), F32))
    out[...] = jnp.concatenate(rows, axis=0).astype(BF)


def pack(sums, width):
    return pl.pallas_call(
        pack_kernel,
        out_shape=jax.ShapeDtypeStruct((STAT_ROWS, width), BF),
        in_specs=[whole()],
        out_specs=whole(),
        compiler_params=pltpu.CompilerParams(vmem_limit_bytes=16 * MIB),
        name="pack",
    )(jnp.pad(sums, ((0, 0), (0, width - sums.shape[1]))))


def norm_kernel(tokens, stats, gain, shift, out):
    block = tokens.shape[0]
    lanes = -(-block // 128) * 128
    columns = jnp.transpose(stats[:, :lanes].astype(F32))[:block]
    average = columns[:, 0:1] + columns[:, 1:2] + columns[:, 2:3]
    scale_inv = columns[:, 3:4] + columns[:, 4:5] + columns[:, 5:6]
    for left in range(0, tokens.shape[1], 256):
        piece = slice(left, left + 256)
        normed = (tokens[:, piece].astype(F32) - average) * scale_inv
        out[:, piece] = (normed * gain[:, piece] + shift[:, piece]).astype(BF)


def norm(tokens, stats, gain, shift):
    rows, width = tokens.shape
    return pl.pallas_call(
        norm_kernel,
        out_shape=jax.ShapeDtypeStruct(tokens.shape, BF),
        in_specs=[whole()] * 4,
        out_specs=whole(),
        compiler_params=pltpu.CompilerParams(vmem_limit_bytes=16 * MIB),
        cost_estimate=pl.CostEstimate(
            flops=4 * rows * width, bytes_accessed=4 * rows * width, transcendentals=0
        ),
        name="norm",
    )(tokens, stats, gain[None, :], shift[None, :])


def qkv_kernel(count, heads, w_own, w_peer, *refs):
    owns, peers, (keep, send) = refs[:count], refs[count : 2 * count], refs[2 * count :]
    width = keep.shape[1]
    first = 0
    for own, peer in zip(owns, peers):
        rows = own.shape[0]
        for k, target in ((1, send), (0, keep)):
            chosen = pl.ds(pl.multiple_of(heads[k] * width, HD), width)
            total = jnp.dot(own[...], w_own[:, chosen], preferred_element_type=F32)
            total += jnp.dot(
                peer[...], w_peer[:, k * width : (k + 1) * width], preferred_element_type=F32
            )
            target[first : first + rows, :] = total.astype(BF)
        first += rows


def qkv(owns, peers, heads, w_own, w_peer):
    rows = sum(own.shape[0] for own in owns)
    depth, columns = w_peer.shape
    out = jax.ShapeDtypeStruct((rows, columns // 2), BF)
    return pl.pallas_call(
        functools.partial(qkv_kernel, len(owns)),
        out_shape=(out, out),
        in_specs=[whole(pltpu.SMEM)] + [whole()] * (2 + 2 * len(owns)),
        out_specs=(whole(), whole()),
        compiler_params=pltpu.CompilerParams(vmem_limit_bytes=32 * MIB),
        cost_estimate=pl.CostEstimate(
            flops=4 * rows * depth * columns // LIGHT,
            bytes_accessed=(4 * rows * depth + 4 * depth * columns + 2 * rows * columns) // LIGHT,
            transcendentals=0,
        ),
        name="qkv",
    )(heads, w_own, w_peer, *owns, *peers)


def turn_kernel(group, block, starts, kept, received, table, *refs):
    out, turned, angles, load_sems, store_sems = refs[-5:]
    count = kept.shape[0] // block

    def place(k):
        return pl.ds(pl.multiple_of(starts[group + k], 16), block)

    def local(k):
        return pl.ds(k * block, block)

    def load(k):
        return pltpu.make_async_copy(table.at[place(k), :], angles.at[local(k), :], load_sems.at[k])

    def store(k):
        return pltpu.make_async_copy(turned.at[local(k), :], out.at[place(k), :], store_sems.at[k])

    for k in range(count):
        load(k).start()
    lane = lax.broadcasted_iota(jnp.int32, (block, HD), 1)
    first_half = (lane % 64) < 32
    for k in range(count):
        rows = slice(k * block, (k + 1) * block)

        def mixed(part):
            cols = slice(part * HD, (part + 1) * HD)
            terms = (ref[rows, cols].astype(F32) for ref in (kept, received))
            return sum(terms)

        turned[rows, 2 * HD :] = mixed(2).astype(BF)
        load(k).wait()
        for part in range(2):
            cols = slice(part * HD, (part + 1) * HD)
            both = mixed(part)
            swapped = jnp.where(first_half, pltpu.roll(both, HD - 32, 1), pltpu.roll(both, 32, 1))
            turned[rows, cols] = (both * angles[rows, :HD] + swapped * angles[rows, HD:]).astype(BF)
        store(k).start()
    for k in range(count):
        store(k).wait()


def turn(group, block, starts, kept, received, table, so_far):
    rows, columns = kept.shape
    operands = [starts, kept, received, table] + ([] if so_far is None else [so_far])
    return pl.pallas_call(
        functools.partial(turn_kernel, group, block),
        out_shape=jax.ShapeDtypeStruct((table.shape[0], columns), BF),
        in_specs=[whole(pltpu.SMEM)] + [whole()] * 2 + [whole(pl.ANY)] * (len(operands) - 3),
        out_specs=whole(pl.ANY),
        input_output_aliases={} if so_far is None else {4: 0},
        scratch_shapes=[
            pltpu.VMEM((rows, columns), BF),
            pltpu.VMEM((rows, 2 * HD), F32),
            pltpu.SemaphoreType.DMA((rows // block,)),
            pltpu.SemaphoreType.DMA((rows // block,)),
        ],
        compiler_params=pltpu.CompilerParams(vmem_limit_bytes=16 * MIB),
        cost_estimate=pl.CostEstimate(
            flops=8 * rows * HD, bytes_accessed=26 * rows * HD, transcendentals=0
        ),
        name="turn",
    )(*operands)


def attend_kernel(tile, windows, group, places, lows, sizes, seg_tiles, seg_row, rows, *refs):
    outs, (turned, result, sem) = refs[:-3], refs[-3:]
    load = pltpu.make_async_copy(rows, turned, sem)
    load.start()
    load.wait()
    scale = HD ** (-0.5) * 1.4426950408889634

    def step(j, carry):
        i = places[group + j]
        at = pl.ds(pl.multiple_of(i * tile, 16), tile)
        to = pl.ds(pl.multiple_of(j * tile, 16), tile)

        def look(window):
            near = pl.ds(pl.multiple_of(lows[i], 128), window)
            scores = (
                lax.dot_general(
                    turned[at, :HD],
                    turned[near, HD : 2 * HD],
                    (((1,), (1,)), ((), ())),
                    preferred_element_type=F32,
                )
                * scale
            )
            lanes = jnp.broadcast_to(seg_tiles[pl.ds(i, 1), :], (8, tile))
            marks = jnp.transpose(lanes)[:, 0:1]
            scores = jnp.where(marks == seg_row[0:1, near], scores, -1e30)
            highest = jnp.max(scores, axis=1, keepdims=True)
            weights = jnp.exp2(scores - highest)
            total = jnp.sum(weights, axis=1, keepdims=True)
            sums = jnp.dot(weights.astype(BF), turned[near, 2 * HD :], preferred_element_type=F32)
            live = jnp.where(marks >= 0, 1.0 / total, 0.0)
            result[to, :] = (sums * live).astype(BF)

        for kind, window in enumerate(windows):
            pl.when(sizes[i] == kind)(functools.partial(look, window))
        return carry

    lax.fori_loop(0, result.shape[0] // tile, step, 0)
    block = outs[0].shape[0]
    for n, out in enumerate(outs):
        out[...] = result[n * block : (n + 1) * block, :]


def attend(group, outs, places, lows, sizes, seg_tiles, seg_row, rows, block, tile, windows):
    total = rows.shape[0]
    return pl.pallas_call(
        functools.partial(attend_kernel, tile, windows, group),
        out_shape=[jax.ShapeDtypeStruct((block, HD), BF)] * outs,
        in_specs=[whole(pltpu.SMEM)] * 3 + [whole()] * 2 + [whole(pl.ANY)],
        out_specs=[whole()] * outs,
        scratch_shapes=[
            pltpu.VMEM((total, 3 * HD), BF),
            pltpu.VMEM((outs * block, HD), BF),
            pltpu.SemaphoreType.DMA,
        ],
        compiler_params=pltpu.CompilerParams(vmem_limit_bytes=32 * MIB),
        cost_estimate=pl.CostEstimate(
            flops=4 * outs * block * windows[-1] * HD,
            bytes_accessed=total * HD * 26,
            transcendentals=outs * block * windows[-1],
        ),
        name="attend",
    )(places, lows, sizes, seg_tiles, seg_row, rows)


def project_kernel(pieces, blocks, first, before, slots, *refs):
    weights, parts, rest = refs[:pieces], refs[pieces : pieces + 4], refs[pieces + 4 :]
    earlier, (out, all_weights, rows, weight_sems, sems) = rest[:-5], rest[-5:]
    depth = all_weights.shape[0] // blocks
    copies = []
    top = 0
    for m in range(pieces):
        size = weights[m].shape[0]
        copies.append(
            pltpu.make_async_copy(
                weights[m], all_weights.at[top : top + size, :], weight_sems.at[m]
            )
        )
        top += size
    for m in range(blocks):
        for j in range(4):
            start = pl.multiple_of(m * depth + slots[j] * HD, HD)
            left = (first + m) * HD
            copies.append(
                pltpu.make_async_copy(
                    parts[j].at[:, left : left + HD], rows.at[:, pl.ds(start, HD)], sems.at[4 * m + j]
                )
            )
    for copy in copies:
        copy.start()
    for copy in copies:
        copy.wait()
    for start in range(0, out.shape[1], 256):
        end = min(start + 256, out.shape[1])
        total = jnp.dot(rows[...], all_weights[:, start:end], preferred_element_type=F32)
        if earlier:
            total += earlier[0][:, before + start : before + end]
        out[:, start:end] = total.astype(out.dtype)


def project(slots, first, weights, parts, earlier, kind, left=0, urgent=0):
    pieces = len(weights)
    width = weights[0].shape[1]
    depth = sum(piece.shape[0] for piece in weights)
    blocks = depth // (4 * HD)
    count = parts[0].shape[0]
    more = [] if earlier is None else [earlier]
    return pl.pallas_call(
        functools.partial(project_kernel, pieces, blocks, first, left),
        out_shape=jax.ShapeDtypeStruct((count, width), kind),
        in_specs=[whole(pltpu.SMEM)]
        + [whole(pl.ANY)] * (pieces + 4)
        + [whole()] * len(more),
        out_specs=whole(),
        scratch_shapes=[
            pltpu.VMEM((depth, width), BF),
            pltpu.VMEM((count, depth), BF),
            pltpu.SemaphoreType.DMA((pieces,)),
            pltpu.SemaphoreType.DMA((4 * blocks,)),
        ],
        compiler_params=pltpu.CompilerParams(vmem_limit_bytes=32 * MIB),
        cost_estimate=pl.CostEstimate(
            flops=2 * count * depth * width + urgent,
            bytes_accessed=2 * (depth * (width + count) + 2 * count * width),
            transcendentals=0,
        ),
        name="project",
    )(slots, *weights, *parts, *more)


def local_heads(
    tokens, ln_gain, ln_shift, w_qkv, w_out, layer_scale, segments, present, coords, owner_slot
):
    rows = lax.axis_size("row")
    cols = lax.axis_size("col")
    count = segments.shape[0]
    block = tokens.shape[0]
    row = lax.axis_index("row")
    col = lax.axis_index("col")
    core, x_index = row % 2, row // 2
    head = 2 * core + x_index

    lines = cols // 2
    ring = list(range(0, lines, 2)) + list(range(lines - 1 - lines % 2, 0, -2))
    after = {z: ring[(i + 1) % lines] for i, z in enumerate(ring)}
    back = {b: a for a, b in after.items()}
    y_swap = [(c, c ^ 1) for c in range(cols)]
    z_next = [(2 * z + y, 2 * after[z] + y) for z in range(lines) for y in range(2)]
    core_swap = [(r, r ^ 1) for r in range(rows)]
    x_swap = [(r, r ^ 2) for r in range(rows)]

    def by_y(value):
        return lax.ppermute(value, "col", y_swap)

    def by_z(value):
        return lax.ppermute(value, "col", z_next)

    def by_core(value):
        return lax.ppermute(value, "row", core_swap)

    def by_x(value):
        return lax.ppermute(value, "row", x_swap)

    def hold(*values):
        return lax.optimization_barrier(values)

    def along(step, z, times):
        for _ in range(times):
            z = step[z]
        return z

    def per_col(value_of):
        return jnp.asarray([value_of(c // 2, c % 2) for c in range(cols)], jnp.int32)[col]

    def origins(z, y):
        at = [(0, 0), (1, 0), (0, 1)]
        at += [(k, u) for i in range(2, lines + 1) for k, u in ((i - 1, 1), (i, 0))][:-1]
        return [(2 * along(back, z, i) + (y ^ u)) * block for i, u in at]

    starts = per_col(origins)

    z_new, y_new = by_z(tokens), by_y(tokens)
    own_rows = tokens.astype(F32)
    sums = lax.psum(
        jnp.stack([jnp.sum(own_rows, axis=1), jnp.sum(own_rows * own_rows, axis=1)]), "row"
    )
    own_stats = pack(sums, tokens.shape[1])
    z_stats, y_stats = by_z(own_stats), by_y(own_stats)

    heads = jnp.stack([head, head ^ 1, head ^ 2, head ^ 3]).astype(jnp.int32)
    width = 3 * HD

    def head_columns(which):
        return lax.dynamic_slice_in_dim(w_qkv, which * width, width, 1)

    w_sent = jnp.concatenate([head_columns(head ^ 2), head_columns(head ^ 3)], axis=1)
    own_normed = norm(tokens, own_stats, ln_gain, ln_shift)
    z_new, y_new, z_stats, y_stats, w_sent, own_normed, segments, present, coords = hold(
        z_new, y_new, z_stats, y_stats, w_sent, own_normed, segments, present, coords
    )
    w_peer = by_core(w_sent)
    z_new = norm(z_new, z_stats, ln_gain, ln_shift)

    w_ring = [w_out]
    rows_turned = None

    def product(*blocks):
        return qkv(blocks, [by_core(own) for own in blocks], heads, w_qkv, w_peer)

    def turn_all(entries):
        nonlocal rows_turned
        for first, kept, received in entries:
            rows_turned = turn(first, block, starts, kept, received, table, rows_turned)

    quarter = HD // 4
    frequency = 100.0 ** (-jnp.arange(quarter, dtype=F32) / quarter)
    angles = jnp.arange(POSITIONS, dtype=F32)[:, None] * frequency[None, :]
    cosine, sine = jnp.cos(angles), jnp.sin(angles)
    none = jnp.zeros((POSITIONS, 2 * quarter), F32)
    cos_pair = jnp.concatenate([cosine, cosine], axis=1)
    sin_pair = jnp.concatenate([-sine, sine], axis=1)
    turns = jnp.concatenate(
        [
            jnp.concatenate([cos_pair, none, sin_pair, none], axis=1),
            jnp.concatenate([none, cos_pair, none, sin_pair], axis=1),
        ],
        axis=0,
    )
    spots = jnp.arange(POSITIONS, dtype=jnp.int32)
    chosen = jnp.concatenate(
        [coords[0][:, None] == spots[None, :], coords[1][:, None] == spots[None, :]], axis=1
    )
    table = jnp.dot(
        chosen.astype(F32),
        turns,
        precision=lax.Precision.HIGHEST,
        preferred_element_type=F32,
    )

    tile = block // 2
    most = -(-(127 + 2 * (LONGEST - 1) + tile) // 128) * 128
    windows = tuple(sorted({min(count, w) for w in (512, 640, 896, most)}))
    tiles = count // tile
    marks = jnp.where(present == 1, segments, -1).astype(F32)
    heads_of = segments.reshape(tiles, tile)
    real = jnp.sum(present)
    begin = jnp.sum((segments[None, :] < heads_of[:, :1]).astype(jnp.int32), axis=1)
    end = jnp.sum((segments[None, :] <= heads_of[:, -1:]).astype(jnp.int32), axis=1)
    begin = jnp.minimum(begin, real) // 128 * 128
    need = jnp.minimum(end, real) - begin
    sizes = sum((need > w).astype(jnp.int32) for w in windows[:-1])
    spans = sum(jnp.where(sizes == k, w, 0) for k, w in enumerate(windows))
    lows = jnp.minimum(begin, count - spans).astype(jnp.int32)
    seg_tiles, seg_row = marks.reshape(tiles, tile), marks[None, :]

    early = [norm(y_new, y_stats, ln_gain, ln_shift)]
    early.append(by_core(early[0]))
    y_new, ahead = by_y(z_new), by_z(z_new)
    kept, send = product(own_normed)
    received = by_x(send)
    late = product(z_new)
    extra = (table, seg_tiles, seg_row, lows, sizes)
    flat, tree = jax.tree.flatten((y_new, ahead, kept, received, early, late, extra))
    y_new, z_new, kept, received, early, late, extra = jax.tree.unflatten(tree, hold(*flat))
    table, seg_tiles, seg_row, lows, sizes = extra
    exchanged, pending = [(0, kept, received)], [(1, *late)]

    for i in range(2, lines):
        last = i == lines - 1
        y_hand, z_hand = y_new, z_new
        y_new = by_y(z_hand)
        ahead = by_z(w_ring[-1] if last else z_hand)
        entries = [(first, kept, by_x(send)) for first, kept, send in pending]
        if early:
            kept, send = qkv(early[:1], early[1:], heads, w_qkv, w_peer)
            entries.append((2, kept, by_x(send)))
            early = []
        kept, send = product(z_hand)
        pending = [(2 * i - 1, *product(y_hand))]
        if last:
            entries.append((2 * i, kept, by_x(send)))
        else:
            pending.append((2 * i, kept, send))
        turn_all(exchanged)
        arrays = [(kept, received) for _, kept, received in entries]
        later = [(kept, send) for _, kept, send in pending]
        flat, tree = jax.tree.flatten((ahead, y_new, arrays, rows_turned, later))
        held = jax.tree.unflatten(tree, hold(*flat))
        ahead, y_new, arrays, rows_turned, later = held
        exchanged = [(entry[0], *pair) for entry, pair in zip(entries, arrays)]
        pending = [(entry[0], *pair) for entry, pair in zip(pending, later)]
        if last:
            w_ring.append(ahead)
        else:
            z_new = ahead

    w_ring.append(by_z(w_ring[-1]))
    kept, send = product(y_new)
    pending.append((2 * lines - 1, kept, send))
    turn_all(exchanged)
    turn_all([(first, kept, by_x(send)) for first, kept, send in pending])
    ringed = [
        [(2 * z + y, 2 * along(after, z, i) + y) for z in range(lines) for y in range(2)]
        for i in range(lines)
    ]
    each = block // tile
    places = per_col(
        lambda z, y: [
            (2 * along(after, z, i) + u) * each + part
            for u in (1 - y, y)
            for i in range(lines)
            for part in range(each)
        ]
    )

    def attended(group):
        return attend(
            group * each, lines, places, lows, sizes, seg_tiles, seg_row, rows_turned, block, tile, windows
        )

    def ring_out(outs):
        return [outs[0]] + [lax.ppermute(outs[i], "col", ringed[i]) for i in range(1, lines)]

    def cross(group):
        return group, by_x(group), by_core(group)

    *other_outs, w_ring[-1] = hold(*attended(0), w_ring[-1])
    other_outs = ring_out(other_outs)
    own_outs = attended(lines)
    *both, w_last = hold(*other_outs, *own_outs, w_ring[-1])
    left = w_out.shape[1] * 4 // 8
    w_left = by_z(w_last[:, :left])
    others = cross(jnp.concatenate(both[:lines], axis=1))
    *both, w_left, w_last = hold(*others, *both[lines:], w_left, w_last)
    others, own_outs = both[:3], ring_out(both[3:])
    others = [*others, by_core(others[1])]
    other = project(heads, 0, w_ring, others, None, F32)
    other_left = project(heads, lines - 1, [w_left], others, other, BF)
    *own_outs, other_left, w_last = hold(*own_outs, other_left, w_last)
    w_right = by_z(w_last[:, left:])
    crossed = by_y(other_left)
    owns = cross(jnp.concatenate(own_outs, axis=1))
    crossed, w_right = hold(crossed, w_right)
    crossed_right = by_y(
        project(heads, lines - 1, [w_right], others, other, BF, left, URGENT)
    )
    owns = [*owns, by_core(owns[1])]
    own = project(heads, 0, w_ring, owns, None, F32)
    own_left = project(heads, lines - 1, [w_left], owns, own, F32)
    own_right = project(heads, lines - 1, [w_right], owns, own, F32, left)
    projected = jnp.concatenate(
        [own_left + crossed.astype(F32), own_right + crossed_right.astype(F32)], axis=1
    )
    return (own_rows + layer_scale * projected).astype(BF)


def solution(mesh):
    in_specs = (
        P("col", "row"),
        P("row"),
        P("row"),
        P("row", "col"),
        P("col", "row"),
        P("row"),
        P(),
        P(),
        P(),
        P(),
    )
    out_specs = P("col", "row")
    rows, cols = mesh.shape["row"], mesh.shape["col"]

    def local(*args):
        heads_here = args[3].shape[1] // (3 * HD)
        if rows == 4 and heads_here == 4 and cols % 4 == 0 and cols > 4 and args[0].shape[0] % 32 == 0:
            return local_heads(*args)
        return local_general(*args)

    return jax.shard_map(local, mesh=mesh, in_specs=in_specs, out_specs=out_specs, check_vma=False)
```

```python
import functools

import jax
import jax.numpy as jnp
from jax import lax
from jax.experimental import pallas as pl
from jax.experimental.pallas import tpu as pltpu
from jax.sharding import PartitionSpec as P

D = 4096
HD = 128
BF = jnp.bfloat16
F32 = jnp.float32
LONGEST = 5 + 18 * 22
POSITIONS = 32
MIB = 1024 * 1024
STAT_ROWS = 16
URGENT = 20 * 10**9
LIGHT = 100


def rotate(values, row_pos, col_pos):
    quarter = values.shape[-1] // 4
    frequency = 100.0 ** (-jnp.arange(quarter, dtype=jnp.float32) / quarter)
    angles = jnp.concatenate(
        [row_pos[:, None] * frequency[None, :], col_pos[:, None] * frequency[None, :]], axis=1
    )
    cosine = jnp.cos(angles)[:, None, :]
    sine_wave = jnp.sin(angles)[:, None, :]
    former = jnp.concatenate(
        [values[..., :quarter], values[..., 2 * quarter : 3 * quarter]], axis=-1
    )
    latter = jnp.concatenate(
        [values[..., quarter : 2 * quarter], values[..., 3 * quarter :]], axis=-1
    )
    new_former = former * cosine - latter * sine_wave
    new_latter = latter * cosine + former * sine_wave
    return jnp.concatenate(
        [
            new_former[..., :quarter],
            new_latter[..., :quarter],
            new_former[..., quarter:],
            new_latter[..., quarter:],
        ],
        axis=-1,
    )


def normalize(values, totals, squares, ln_gain, ln_shift):
    average = totals / D
    spread = squares / D - average * average
    scale_inv = lax.rsqrt(spread + 1e-06)
    return ((values - average[:, None]) * scale_inv[:, None] * ln_gain + ln_shift).astype(
        jnp.bfloat16
    )


def local_general(
    tokens, ln_gain, ln_shift, w_qkv, w_out, layer_scale, segments, present, coords, owner_slot
):
    own_rows = tokens.astype(jnp.float32)
    totals, squares = lax.psum(
        (jnp.sum(own_rows, axis=1), jnp.sum(own_rows * own_rows, axis=1)), "row"
    )
    normed = normalize(own_rows, totals, squares, ln_gain, ln_shift)
    gathered = lax.all_gather(normed, "col", axis=0, tiled=True)
    slot_count = owner_slot.shape[0]
    at_slot = (
        jnp.zeros((slot_count,), jnp.int32)
        .at[owner_slot]
        .set(jnp.arange(slot_count, dtype=jnp.int32))
    )
    placed = gathered[at_slot]
    group_rows = slot_count // lax.axis_size("row")
    mixed = lax.psum_scatter(
        jnp.dot(placed, w_qkv, preferred_element_type=jnp.float32).astype(jnp.bfloat16),
        "row",
        scatter_dimension=0,
        tiled=True,
    ).astype(jnp.float32)
    heads_here = w_qkv.shape[1] // (3 * HD)
    mixed = mixed.reshape(group_rows, heads_here, 3, HD)
    my_slots = lax.dynamic_slice_in_dim(at_slot, lax.axis_index("row") * group_rows, group_rows, 0)
    row_pos = coords[0][my_slots].astype(jnp.float32)
    col_pos = coords[1][my_slots].astype(jnp.float32)
    seg_rows = segments[my_slots]
    live_rows = present[my_slots]
    query_rows = rotate(mixed[:, :, 0], row_pos, col_pos).astype(jnp.bfloat16)
    key_rows = rotate(mixed[:, :, 1], row_pos, col_pos).astype(jnp.bfloat16)
    values = mixed[:, :, 2].astype(jnp.bfloat16)
    scores = jnp.einsum(
        "qhe,khe->hqk", query_rows, key_rows, preferred_element_type=jnp.float32
    ) * HD ** (-0.5)
    allowed = (seg_rows[:, None] == seg_rows[None, :]) & (live_rows[None, :] == 1)
    scores = jnp.where(allowed[None], scores, -1e30)
    highest = jnp.max(scores, axis=-1, keepdims=True)
    weights = jnp.exp(scores - highest)
    probability = (weights / jnp.sum(weights, axis=-1, keepdims=True)).astype(jnp.bfloat16)
    result = jnp.einsum("hqk,khe->qhe", probability, values, preferred_element_type=jnp.float32)
    attended = (result * live_rows[:, None, None].astype(jnp.float32)).astype(jnp.bfloat16)
    attended = attended.reshape(group_rows, heads_here * HD)
    all_slots = lax.all_gather(attended, "row", axis=0, tiled=True)
    projected = lax.psum_scatter(
        jnp.dot(all_slots[owner_slot], w_out, preferred_element_type=jnp.float32).astype(
            jnp.bfloat16
        ),
        "col",
        scatter_dimension=0,
        tiled=True,
    ).astype(jnp.float32)
    return (own_rows + layer_scale * projected).astype(jnp.bfloat16)


def whole(memory_space=pltpu.VMEM):
    return pl.BlockSpec(memory_space=memory_space)


def pack_kernel(sums, out):
    average = sums[0:1, :] / D
    spread = sums[1:2, :] / D - average * average
    rows = []
    for value in (average, lax.rsqrt(spread + 1e-06)):
        for _ in range(3):
            part = value.astype(BF).astype(F32)
            rows.append(part)
            value = value - part
    rows.append(jnp.zeros((STAT_ROWS - len(rows), out.shape[1]), F32))
    out[...] = jnp.concatenate(rows, axis=0).astype(BF)


def pack(sums, width):
    return pl.pallas_call(
        pack_kernel,
        out_shape=jax.ShapeDtypeStruct((STAT_ROWS, width), BF),
        in_specs=[whole()],
        out_specs=whole(),
        compiler_params=pltpu.CompilerParams(vmem_limit_bytes=16 * MIB),
        name="pack",
    )(jnp.pad(sums, ((0, 0), (0, width - sums.shape[1]))))


def norm_kernel(tokens, stats, gain, shift, out):
    block = tokens.shape[0]
    lanes = -(-block // 128) * 128
    columns = jnp.transpose(stats[:, :lanes].astype(F32))[:block]
    average = columns[:, 0:1] + columns[:, 1:2] + columns[:, 2:3]
    scale_inv = columns[:, 3:4] + columns[:, 4:5] + columns[:, 5:6]
    for left in range(0, tokens.shape[1], 256):
        piece = slice(left, left + 256)
        normed = (tokens[:, piece].astype(F32) - average) * scale_inv
        out[:, piece] = (normed * gain[:, piece] + shift[:, piece]).astype(BF)


def norm(tokens, stats, gain, shift):
    rows, width = tokens.shape
    return pl.pallas_call(
        norm_kernel,
        out_shape=jax.ShapeDtypeStruct(tokens.shape, BF),
        in_specs=[whole()] * 4,
        out_specs=whole(),
        compiler_params=pltpu.CompilerParams(vmem_limit_bytes=16 * MIB),
        cost_estimate=pl.CostEstimate(
            flops=rows, bytes_accessed=rows, transcendentals=0
        ),
        name="norm",
    )(tokens, stats, gain[None, :], shift[None, :])


def qkv_kernel(count, heads, w_own, w_peer, *refs):
    owns, peers, (keep, send) = refs[:count], refs[count : 2 * count], refs[2 * count :]
    width = keep.shape[1]
    first = 0
    for own, peer in zip(owns, peers):
        rows = own.shape[0]
        for k, target in ((1, send), (0, keep)):
            chosen = pl.ds(pl.multiple_of(heads[k] * width, HD), width)
            total = jnp.dot(own[...], w_own[:, chosen], preferred_element_type=F32)
            total += jnp.dot(
                peer[...], w_peer[:, k * width : (k + 1) * width], preferred_element_type=F32
            )
            target[first : first + rows, :] = total.astype(BF)
        first += rows


def qkv(owns, peers, heads, w_own, w_peer):
    rows = sum(own.shape[0] for own in owns)
    depth, columns = w_peer.shape
    out = jax.ShapeDtypeStruct((rows, columns // 2), BF)
    return pl.pallas_call(
        functools.partial(qkv_kernel, len(owns)),
        out_shape=(out, out),
        in_specs=[whole(pltpu.SMEM)] + [whole()] * (2 + 2 * len(owns)),
        out_specs=(whole(), whole()),
        compiler_params=pltpu.CompilerParams(vmem_limit_bytes=32 * MIB),
        cost_estimate=pl.CostEstimate(
            flops=4 * rows * depth * columns // LIGHT,
            bytes_accessed=(4 * rows * depth + 4 * depth * columns + 2 * rows * columns) // LIGHT,
            transcendentals=0,
        ),
        name="qkv",
    )(heads, w_own, w_peer, *owns, *peers)


def turn_kernel(group, block, starts, kept, received, table, *refs):
    out, turned, angles, load_sems, store_sems = refs[-5:]
    count = kept.shape[0] // block

    def place(k):
        return pl.ds(pl.multiple_of(starts[group + k], 16), block)

    def local(k):
        return pl.ds(k * block, block)

    def load(k):
        return pltpu.make_async_copy(table.at[place(k), :], angles.at[local(k), :], load_sems.at[k])

    def store(k):
        return pltpu.make_async_copy(turned.at[local(k), :], out.at[place(k), :], store_sems.at[k])

    for k in range(count):
        load(k).start()
    lane = lax.broadcasted_iota(jnp.int32, (block, HD), 1)
    first_half = (lane % 64) < 32
    for k in range(count):
        rows = slice(k * block, (k + 1) * block)

        def mixed(part):
            cols = slice(part * HD, (part + 1) * HD)
            terms = (ref[rows, cols].astype(F32) for ref in (kept, received))
            return sum(terms)

        turned[rows, 2 * HD :] = mixed(2).astype(BF)
        load(k).wait()
        for part in range(2):
            cols = slice(part * HD, (part + 1) * HD)
            both = mixed(part)
            swapped = jnp.where(first_half, pltpu.roll(both, HD - 32, 1), pltpu.roll(both, 32, 1))
            turned[rows, cols] = (both * angles[rows, :HD] + swapped * angles[rows, HD:]).astype(BF)
        store(k).start()
    for k in range(count):
        store(k).wait()


def turn(group, block, starts, kept, received, table, so_far):
    rows, columns = kept.shape
    operands = [starts, kept, received, table] + ([] if so_far is None else [so_far])
    return pl.pallas_call(
        functools.partial(turn_kernel, group, block),
        out_shape=jax.ShapeDtypeStruct((table.shape[0], columns), BF),
        in_specs=[whole(pltpu.SMEM)] + [whole()] * 2 + [whole(pl.ANY)] * (len(operands) - 3),
        out_specs=whole(pl.ANY),
        input_output_aliases={} if so_far is None else {4: 0},
        scratch_shapes=[
            pltpu.VMEM((rows, columns), BF),
            pltpu.VMEM((rows, 2 * HD), F32),
            pltpu.SemaphoreType.DMA((rows // block,)),
            pltpu.SemaphoreType.DMA((rows // block,)),
        ],
        compiler_params=pltpu.CompilerParams(vmem_limit_bytes=16 * MIB),
        cost_estimate=pl.CostEstimate(
            flops=rows, bytes_accessed=rows, transcendentals=0
        ),
        name="turn",
    )(*operands)


def attend_kernel(tile, windows, group, places, lows, sizes, seg_tiles, seg_row, rows, *refs):
    outs, (turned, result, sem) = refs[:-3], refs[-3:]
    load = pltpu.make_async_copy(rows, turned, sem)
    load.start()
    load.wait()
    scale = HD ** (-0.5) * 1.4426950408889634

    def step(j, carry):
        i = places[group + j]
        at = pl.ds(pl.multiple_of(i * tile, 16), tile)
        to = pl.ds(pl.multiple_of(j * tile, 16), tile)

        def look(window):
            near = pl.ds(pl.multiple_of(lows[i], 128), window)
            scores = (
                lax.dot_general(
                    turned[at, :HD],
                    turned[near, HD : 2 * HD],
                    (((1,), (1,)), ((), ())),
                    preferred_element_type=F32,
                )
                * scale
            )
            lanes = jnp.broadcast_to(seg_tiles[pl.ds(i, 1), :], (8, tile))
            marks = jnp.transpose(lanes)[:, 0:1]
            scores = jnp.where(marks == seg_row[0:1, near], scores, -1e30)
            highest = jnp.max(scores, axis=1, keepdims=True)
            weights = jnp.exp2(scores - highest)
            total = jnp.sum(weights, axis=1, keepdims=True)
            sums = jnp.dot(weights.astype(BF), turned[near, 2 * HD :], preferred_element_type=F32)
            live = jnp.where(marks >= 0, 1.0 / total, 0.0)
            result[to, :] = (sums * live).astype(BF)

        for kind, window in enumerate(windows):
            pl.when(sizes[i] == kind)(functools.partial(look, window))
        return carry

    lax.fori_loop(0, result.shape[0] // tile, step, 0)
    block = outs[0].shape[0]
    for n, out in enumerate(outs):
        out[...] = result[n * block : (n + 1) * block, :]


def attend(group, outs, places, lows, sizes, seg_tiles, seg_row, rows, block, tile, windows):
    total = rows.shape[0]
    return pl.pallas_call(
        functools.partial(attend_kernel, tile, windows, group),
        out_shape=[jax.ShapeDtypeStruct((block, HD), BF)] * outs,
        in_specs=[whole(pltpu.SMEM)] * 3 + [whole()] * 2 + [whole(pl.ANY)],
        out_specs=[whole()] * outs,
        scratch_shapes=[
            pltpu.VMEM((total, 3 * HD), BF),
            pltpu.VMEM((outs * block, HD), BF),
            pltpu.SemaphoreType.DMA,
        ],
        compiler_params=pltpu.CompilerParams(vmem_limit_bytes=32 * MIB),
        cost_estimate=pl.CostEstimate(
            flops=4 * outs * block * windows[-1] * HD,
            bytes_accessed=total * HD * 26,
            transcendentals=outs * block * windows[-1],
        ),
        name="attend",
    )(places, lows, sizes, seg_tiles, seg_row, rows)


def project_kernel(pieces, blocks, first, before, slots, *refs):
    weights, parts, rest = refs[:pieces], refs[pieces : pieces + 4], refs[pieces + 4 :]
    earlier, (out, all_weights, rows, weight_sems, sems) = rest[:-5], rest[-5:]
    depth = all_weights.shape[0] // blocks
    copies = []
    top = 0
    for m in range(pieces):
        size = weights[m].shape[0]
        copies.append(
            pltpu.make_async_copy(
                weights[m], all_weights.at[top : top + size, :], weight_sems.at[m]
            )
        )
        top += size
    for m in range(blocks):
        for j in range(4):
            start = pl.multiple_of(m * depth + slots[j] * HD, HD)
            left = (first + m) * HD
            copies.append(
                pltpu.make_async_copy(
                    parts[j].at[:, left : left + HD], rows.at[:, pl.ds(start, HD)], sems.at[4 * m + j]
                )
            )
    for copy in copies:
        copy.start()
    for copy in copies:
        copy.wait()
    for start in range(0, out.shape[1], 256):
        end = min(start + 256, out.shape[1])
        total = jnp.dot(rows[...], all_weights[:, start:end], preferred_element_type=F32)
        if earlier:
            total += earlier[0][:, before + start : before + end]
        out[:, start:end] = total.astype(out.dtype)


def project(slots, first, weights, parts, earlier, kind, left=0, urgent=0):
    pieces = len(weights)
    width = weights[0].shape[1]
    depth = sum(piece.shape[0] for piece in weights)
    blocks = depth // (4 * HD)
    count = parts[0].shape[0]
    more = [] if earlier is None else [earlier]
    return pl.pallas_call(
        functools.partial(project_kernel, pieces, blocks, first, left),
        out_shape=jax.ShapeDtypeStruct((count, width), kind),
        in_specs=[whole(pltpu.SMEM)]
        + [whole(pl.ANY)] * (pieces + 4)
        + [whole()] * len(more),
        out_specs=whole(),
        scratch_shapes=[
            pltpu.VMEM((depth, width), BF),
            pltpu.VMEM((count, depth), BF),
            pltpu.SemaphoreType.DMA((pieces,)),
            pltpu.SemaphoreType.DMA((4 * blocks,)),
        ],
        compiler_params=pltpu.CompilerParams(vmem_limit_bytes=32 * MIB),
        cost_estimate=pl.CostEstimate(
            flops=2 * count * depth * width + urgent,
            bytes_accessed=2 * (depth * (width + count) + 2 * count * width),
            transcendentals=0,
        ),
        name="project",
    )(slots, *weights, *parts, *more)


def local_heads(
    tokens, ln_gain, ln_shift, w_qkv, w_out, layer_scale, segments, present, coords, owner_slot
):
    rows = lax.axis_size("row")
    cols = lax.axis_size("col")
    count = segments.shape[0]
    block = tokens.shape[0]
    row = lax.axis_index("row")
    col = lax.axis_index("col")
    core, x_index = row % 2, row // 2
    head = 2 * core + x_index

    lines = cols // 2
    ring = list(range(0, lines, 2)) + list(range(lines - 1 - lines % 2, 0, -2))
    after = {z: ring[(i + 1) % lines] for i, z in enumerate(ring)}
    back = {b: a for a, b in after.items()}
    y_swap = [(c, c ^ 1) for c in range(cols)]
    z_next = [(2 * z + y, 2 * after[z] + y) for z in range(lines) for y in range(2)]
    core_swap = [(r, r ^ 1) for r in range(rows)]
    x_swap = [(r, r ^ 2) for r in range(rows)]

    def by_y(value):
        return lax.ppermute(value, "col", y_swap)

    def by_z(value):
        return lax.ppermute(value, "col", z_next)

    def by_core(value):
        return lax.ppermute(value, "row", core_swap)

    def by_x(value):
        return lax.ppermute(value, "row", x_swap)

    def hold(*values):
        return lax.optimization_barrier(values)

    def along(step, z, times):
        for _ in range(times):
            z = step[z]
        return z

    def per_col(value_of):
        return jnp.asarray([value_of(c // 2, c % 2) for c in range(cols)], jnp.int32)[col]

    def origins(z, y):
        at = [(0, 0), (1, 0), (0, 1)]
        at += [(k, u) for i in range(2, lines + 1) for k, u in ((i - 1, 1), (i, 0))][:-1]
        return [(2 * along(back, z, i) + (y ^ u)) * block for i, u in at]

    starts = per_col(origins)

    z_new, y_new = by_z(tokens), by_y(tokens)
    own_rows = tokens.astype(F32)
    sums = lax.psum(
        jnp.stack([jnp.sum(own_rows, axis=1), jnp.sum(own_rows * own_rows, axis=1)]), "row"
    )
    own_stats = pack(sums, tokens.shape[1])
    z_stats, y_stats = by_z(own_stats), by_y(own_stats)

    heads = jnp.stack([head, head ^ 1, head ^ 2, head ^ 3]).astype(jnp.int32)
    width = 3 * HD

    def head_columns(which):
        return lax.dynamic_slice_in_dim(w_qkv, which * width, width, 1)

    w_sent = jnp.concatenate([head_columns(head ^ 2), head_columns(head ^ 3)], axis=1)
    own_normed = norm(tokens, own_stats, ln_gain, ln_shift)
    z_new, y_new, z_stats, y_stats, w_sent, own_normed, segments, present, coords = hold(
        z_new, y_new, z_stats, y_stats, w_sent, own_normed, segments, present, coords
    )
    w_peer = by_core(w_sent)
    z_new = norm(z_new, z_stats, ln_gain, ln_shift)

    w_ring = [w_out]
    rows_turned = None

    def product(*blocks):
        return qkv(blocks, [by_core(own) for own in blocks], heads, w_qkv, w_peer)

    def turn_all(entries):
        nonlocal rows_turned
        for first, kept, received in entries:
            rows_turned = turn(first, block, starts, kept, received, table, rows_turned)

    quarter = HD // 4
    frequency = 100.0 ** (-jnp.arange(quarter, dtype=F32) / quarter)
    angles = jnp.arange(POSITIONS, dtype=F32)[:, None] * frequency[None, :]
    cosine, sine = jnp.cos(angles), jnp.sin(angles)
    none = jnp.zeros((POSITIONS, 2 * quarter), F32)
    cos_pair = jnp.concatenate([cosine, cosine], axis=1)
    sin_pair = jnp.concatenate([-sine, sine], axis=1)
    turns = jnp.concatenate(
        [
            jnp.concatenate([cos_pair, none, sin_pair, none], axis=1),
            jnp.concatenate([none, cos_pair, none, sin_pair], axis=1),
        ],
        axis=0,
    )
    spots = jnp.arange(POSITIONS, dtype=jnp.int32)
    chosen = jnp.concatenate(
        [coords[0][:, None] == spots[None, :], coords[1][:, None] == spots[None, :]], axis=1
    )
    table = jnp.dot(
        chosen.astype(F32),
        turns,
        precision=lax.Precision.HIGHEST,
        preferred_element_type=F32,
    )

    tile = block // 2
    most = -(-(127 + 2 * (LONGEST - 1) + tile) // 128) * 128
    windows = tuple(sorted({min(count, w) for w in (512, 640, 896, most)}))
    tiles = count // tile
    marks = jnp.where(present == 1, segments, -1).astype(F32)
    heads_of = segments.reshape(tiles, tile)
    real = jnp.sum(present)
    begin = jnp.sum((segments[None, :] < heads_of[:, :1]).astype(jnp.int32), axis=1)
    end = jnp.sum((segments[None, :] <= heads_of[:, -1:]).astype(jnp.int32), axis=1)
    begin = jnp.minimum(begin, real) // 128 * 128
    need = jnp.minimum(end, real) - begin
    sizes = sum((need > w).astype(jnp.int32) for w in windows[:-1])
    spans = sum(jnp.where(sizes == k, w, 0) for k, w in enumerate(windows))
    lows = jnp.minimum(begin, count - spans).astype(jnp.int32)
    seg_tiles, seg_row = marks.reshape(tiles, tile), marks[None, :]

    early = [norm(y_new, y_stats, ln_gain, ln_shift)]
    early.append(by_core(early[0]))
    y_new, ahead = by_y(z_new), by_z(z_new)
    kept, send = product(own_normed)
    received = by_x(send)
    late = product(z_new)
    extra = (table, seg_tiles, seg_row, lows, sizes)
    flat, tree = jax.tree.flatten((y_new, ahead, kept, received, early, late, extra))
    y_new, z_new, kept, received, early, late, extra = jax.tree.unflatten(tree, hold(*flat))
    table, seg_tiles, seg_row, lows, sizes = extra
    exchanged, pending = [(0, kept, received)], [(1, *late)]

    for i in range(2, lines):
        last = i == lines - 1
        y_hand, z_hand = y_new, z_new
        y_new = by_y(z_hand)
        ahead = by_z(w_ring[-1] if last else z_hand)
        entries = [(first, kept, by_x(send)) for first, kept, send in pending]
        if early:
            kept, send = qkv(early[:1], early[1:], heads, w_qkv, w_peer)
            entries.append((2, kept, by_x(send)))
            early = []
        kept, send = product(z_hand)
        pending = [(2 * i - 1, *product(y_hand))]
        if last:
            entries.append((2 * i, kept, by_x(send)))
        else:
            pending.append((2 * i, kept, send))
        turn_all(exchanged)
        arrays = [(kept, received) for _, kept, received in entries]
        later = [(kept, send) for _, kept, send in pending]
        flat, tree = jax.tree.flatten((ahead, y_new, arrays, rows_turned, later))
        held = jax.tree.unflatten(tree, hold(*flat))
        ahead, y_new, arrays, rows_turned, later = held
        exchanged = [(entry[0], *pair) for entry, pair in zip(entries, arrays)]
        pending = [(entry[0], *pair) for entry, pair in zip(pending, later)]
        if last:
            w_ring.append(ahead)
        else:
            z_new = ahead

    w_ring.append(by_z(w_ring[-1]))
    kept, send = product(y_new)
    pending.append((2 * lines - 1, kept, send))
    turn_all(exchanged)
    turn_all([(first, kept, by_x(send)) for first, kept, send in pending])
    ringed = [
        [(2 * z + y, 2 * along(after, z, i) + y) for z in range(lines) for y in range(2)]
        for i in range(lines)
    ]
    each = block // tile
    places = per_col(
        lambda z, y: [
            (2 * along(after, z, i) + u) * each + part
            for u in (1 - y, y)
            for i in range(lines)
            for part in range(each)
        ]
    )

    def attended(group):
        return attend(
            group * each, lines, places, lows, sizes, seg_tiles, seg_row, rows_turned, block, tile, windows
        )

    def ring_out(outs):
        return [outs[0]] + [lax.ppermute(outs[i], "col", ringed[i]) for i in range(1, lines)]

    def cross(group):
        return group, by_x(group), by_core(group)

    *other_outs, w_ring[-1] = hold(*attended(0), w_ring[-1])
    other_outs = ring_out(other_outs)
    own_outs = attended(lines)
    *both, w_last = hold(*other_outs, *own_outs, w_ring[-1])
    left = w_out.shape[1] * 4 // 8
    w_left = by_z(w_last[:, :left])
    others = cross(jnp.concatenate(both[:lines], axis=1))
    *both, w_left, w_last = hold(*others, *both[lines:], w_left, w_last)
    others, own_outs = both[:3], ring_out(both[3:])
    others = [*others, by_core(others[1])]
    other = project(heads, 0, w_ring, others, None, F32)
    other_left = project(heads, lines - 1, [w_left], others, other, BF)
    *own_outs, other_left, w_last = hold(*own_outs, other_left, w_last)
    w_right = by_z(w_last[:, left:])
    crossed = by_y(other_left)
    owns = cross(jnp.concatenate(own_outs, axis=1))
    crossed, w_right = hold(crossed, w_right)
    crossed_right = by_y(
        project(heads, lines - 1, [w_right], others, other, BF, left, URGENT)
    )
    owns = [*owns, by_core(owns[1])]
    own = project(heads, 0, w_ring, owns, None, F32)
    own_left = project(heads, lines - 1, [w_left], owns, own, F32)
    own_right = project(heads, lines - 1, [w_right], owns, own, F32, left)
    projected = jnp.concatenate(
        [own_left + crossed.astype(F32), own_right + crossed_right.astype(F32)], axis=1
    )
    return (own_rows + layer_scale * projected).astype(BF)


def solution(mesh):
    in_specs = (
        P("col", "row"),
        P("row"),
        P("row"),
        P("row", "col"),
        P("col", "row"),
        P("row"),
        P(),
        P(),
        P(),
        P(),
    )
    out_specs = P("col", "row")
    rows, cols = mesh.shape["row"], mesh.shape["col"]

    def local(*args):
        heads_here = args[3].shape[1] // (3 * HD)
        if rows == 4 and heads_here == 4 and cols % 4 == 0 and cols > 4 and args[0].shape[0] % 32 == 0:
            return local_heads(*args)
        return local_general(*args)

    return jax.shard_map(local, mesh=mesh, in_specs=in_specs, out_specs=out_specs, check_vma=False)
```
